32 devices in a mesh: lat: 4 (over z), lon: 8 (over y, x, core).
Axes of the slice: x: 2, y: 2, z: 4, core: 2. Of those that a mesh axis runs over, the one named last changes fastest.
Arguments:
- wind_u: float32 [8, 256, 12000], P(None, 'lat', 'lon'), may hold values from -6 to 6
- wind_v: float32 [8, 256, 12000], P(None, 'lat', 'lon'), may hold values from -6 to 6
- tracer: float32 [8, 256, 12000], P(None, 'lat', 'lon'), may hold values from -6 to 6
- cutoff: int32 [256], P('lat'), may hold values from 1 to 1024, as said below
- row_scale: float32 [256], P('lat'), may hold values from 1 to 10
Outputs:
- tracer_next: float32 [8, 256, 12000], P(None, 'lat', 'lon')
- divergence: float32 [8, 256, 12000], P(None, 'lat', 'lon')
- vorticity: float32 [8, 256, 12000], P(None, 'lat', 'lon')
The draws below stay inside these ranges and needn't reach their ends.
Inputs may be any that keep to these rules, and one draw needn't show every extreme that they name: cutoff of row r is min(1024, 1024 * (r + 1) // 256 + j) with a whole j from 0 to 63 drawn per row, and at least 1; the last row's is 1024.
All inputs are finite; a program needn't handle non-finite values.
Results may differ from the reference program's by a relative error of at most 0.00014.
Values sent between devices are 32-bit elements; how exact they have to be, the bound alone decides.
No kernel may reach another device: no remote copies, remote signals or barrier semaphores. Data moves between devices by JAX's collectives and lax.ppermute only.
A program may use at most 128 MiB of HBM per device.

```python
import math
import jax
import jax.numpy as jnp

NLON = 12000
LEV = 8
KMAX = 1024
NSLAB = 256


def draw_cutoff(key, part):
    rows = jnp.arange(NSLAB, dtype=jnp.int32)
    base = KMAX * (rows + 1) // NSLAB
    jitter = jax.random.randint(jax.random.fold_in(key, 7), (NSLAB,), 0, 64)
    return jnp.clip(base + jitter, 1, KMAX).astype(jnp.int32)


def block_scale(own_key, shape, pieces, least, top_value):
    def one(axis_at, blocks):
        heights = jax.random.uniform(jax.random.fold_in(jax.random.fold_in(own_key, 6), axis_at), (blocks,), jnp.float32, least / len(pieces), top_value / len(pieces))
        return jnp.repeat(jnp.exp(heights), shape[axis_at] // blocks).reshape((-1,) + (1,) * (len(shape) - axis_at - 1))

    gain = one(*pieces[0])
    for cut in pieces[1:]:
        gain = gain * one(*cut)
    return gain


def scatter_about(stream_key, extent, spread, bound, shards=(), held_as=jnp.bfloat16):
    level = block_scale(stream_key, extent, shards, -0.22, 0.18) if shards else 1.0
    drawn = jax.random.normal(stream_key, extent, jnp.float32) * spread * level
    return jnp.minimum(jnp.maximum(drawn, -bound), bound).astype(held_as)


def setup_inputs(seed: int = 0) -> dict:
    streams_of = jax.random.split(jax.random.key(seed), 6)
    return {
        "wind_u": scatter_about(streams_of[0], (LEV, NSLAB, NLON), 1.0, 6.0, ((1, 4), (2, 8)), jnp.float32),
        "wind_v": scatter_about(streams_of[1], (LEV, NSLAB, NLON), 1.0, 6.0, ((1, 4), (2, 8)), jnp.float32),
        "tracer": scatter_about(streams_of[2], (LEV, NSLAB, NLON), 1.0, 6.0, ((1, 4), (2, 8)), jnp.float32),
        "cutoff": draw_cutoff(jax.random.fold_in(streams_of[5], 71), 0),
        "row_scale": jnp.clip(jnp.exp(math.log(10.0) - 2.3025851 * jax.random.uniform(streams_of[4], (NSLAB,), jnp.float32) ** block_scale(streams_of[4], (NSLAB,), ((0, 4),), -0.2, 0.2)), 1.0, 10.0),
    }


courant = 0.5


def filter_field(field, keep):
    spectrum = jnp.fft.rfft(field, axis=-1)[..., :KMAX] * keep[None]
    return jnp.fft.irfft(spectrum, n=NLON, axis=-1).astype(jnp.float32)


def east_west(field):
    return jnp.roll(field, -1, axis=2) - jnp.roll(field, 1, axis=2)


def north_south(field):
    padded = jnp.pad(field, ((0, 0), (1, 1), (0, 0)))
    return padded[:, 2:] - padded[:, :-2]


def reference(wind_u, wind_v, tracer, cutoff, row_scale):
    numbers = jnp.arange(KMAX, dtype=jnp.int32)
    keep = (numbers[None, :] < cutoff[:, None]).astype(jnp.float32)
    filt_u = filter_field(wind_u, keep)
    filt_v = filter_field(wind_v, keep)
    filt_q = filter_field(tracer, keep)
    metric = row_scale[None, :, None]
    divergence = metric * (east_west(filt_u) + north_south(filt_v / metric))
    vorticity = metric * (east_west(filt_v) - north_south(filt_u / metric))
    tracer_next = tracer - courant * (filt_u * metric * east_west(filt_q) + filt_v * north_south(filt_q))
    return tracer_next, divergence, vorticity
```

```python
import functools
import math

import jax
import jax.numpy as jnp
import ml_dtypes
import numpy as np
from jax import lax
from jax.experimental import pallas as pl
from jax.experimental.pallas import tpu as pltpu
from jax.sharding import PartitionSpec as P

NLON = 12000
KMAX = 1024
MOMENTS = 32
EXTRA = 32
LANES = 128
CHUNKS = 1
courant = 0.5
BF = jnp.bfloat16
F32 = jnp.float32
VMEM_LIMIT = 56 * 1024 * 1024


def prolate(points, band, count):
    i = np.arange(points)
    diag = ((points - 1 - 2 * i) / 2.0) ** 2 * np.cos(2 * np.pi * band)
    off = i[1:] * (points - i[1:]) / 2.0
    mid = points // 2
    half = (count + 1) // 2
    out = np.zeros((points, 2 * half))
    dd, ee = diag[mid:], off[mid:].copy()
    scaled = ee.copy()
    scaled[0] *= math.sqrt(2.0)
    even = np.linalg.eigh(np.diag(dd) + np.diag(scaled, 1) + np.diag(scaled, -1))[1]
    even = even[:, ::-1][:, :half]
    wing = even[1:] / math.sqrt(2.0)
    out[mid, 0::2] = even[0]
    out[mid + 1 :, 0::2] = wing
    out[:mid, 0::2] = wing[::-1]
    odd = np.linalg.eigh(np.diag(dd[1:]) + np.diag(ee[1:], 1) + np.diag(ee[1:], -1))[1]
    wing = odd[:, ::-1][:, :half] / math.sqrt(2.0)
    out[mid + 1 :, 1::2] = wing
    out[:mid, 1::2] = -wing[::-1]
    return out


def interpolation(low, high, nodes, snap):
    fine = prolate(2 * (high - low) + 1, (KMAX - 0.5) / NLON / 2, nodes + 2)
    wave = fine[:, nodes]
    at = np.nonzero(wave[:-1] * wave[1:] < 0)[0]
    roots = (at + wave[at] / (wave[at] - wave[at + 1]))[: nodes // 2] / 2 + low
    left = snap(roots)
    for i in range(1, len(left)):
        left[i] = max(left[i], left[i - 1] + 1)
    places = np.concatenate([left, (low + high) - left[::-1]])
    kept = nodes - 4
    index = np.round((places - low) * 2).astype(int)
    return places, fine[::2, :kept] @ np.linalg.pinv(fine[index, :kept])


def near_kernel(distance):
    return 1.0 / (NLON * np.sin(np.pi * distance / NLON))


def two_parts(table):
    high = table.astype(np.float32).astype(ml_dtypes.bfloat16)
    low = (table - high.astype(np.float64)).astype(np.float32).astype(ml_dtypes.bfloat16)
    return high, low


@functools.lru_cache(maxsize=4)
def make_tables(width, segments):
    nodes = -(-2 * KMAX * width // NLON // 32) * 32 + EXTRA
    source, gather = interpolation(0, width - 1, nodes, np.round)
    target, spread = interpolation(-1, width, nodes, lambda r: np.floor(r) + 0.5)
    local = near_kernel(target[:, None] - source[None])
    offsets = [d for d in range(-(segments - 1), segments) if d]
    far = {d: near_kernel(target[:, None] + width * d - source[None]) for d in offsets}
    every = np.concatenate([far[d] for d in offsets])
    half, pairs = nodes // 2, MOMENTS // 2
    mirrored = every[:, ::-1][:, :half]
    even = np.linalg.svd(every[:, :half] + mirrored, full_matrices=False)[2][:pairs]
    odd = np.linalg.svd(every[:, :half] - mirrored, full_matrices=False)[2][:pairs]
    moments = np.concatenate(
        [
            np.concatenate([even, even[:, ::-1]], 1),
            np.concatenate([odd, -odd[:, ::-1]], 1),
        ]
    ) / math.sqrt(2.0)
    moments *= np.sign(moments[:, :1])

    high, low = two_parts(gather.T)
    gather_table = np.concatenate([high, low], 0)
    high, low = two_parts(np.concatenate([local, moments], 0))
    local_table = np.concatenate([high, low, high], 1)
    blocks = []
    for d in range(segments):
        zero = np.zeros((nodes, MOMENTS))
        row = [zero if e == d else far[d - e] @ moments.T for e in range(segments)]
        high, low = two_parts(np.concatenate(row, 1))
        blocks.append(np.concatenate([high, low, high], 1))
    far_table = np.stack(blocks)
    lanes = -(-(width + 2) // LANES) * LANES
    wide = np.zeros((nodes, lanes))
    wide[:, : width + 1] = spread.T[:, 1:]
    wide[:, lanes - 1] = spread.T[:, 0]
    high, low = two_parts(wide)
    spread_table = np.concatenate([high, low, high], 0)
    places = np.stack([2 * source - width, 2 * target - width]).astype(np.float32)
    return gather_table, local_table, far_table, spread_table, places[:, :, None]


def phases(cut, places, device, segments, width):
    full = 4.0 * NLON
    odd = 2.0 * cut - 1.0
    inner = odd * places
    inner = inner - full * jnp.floor(inner * (1.0 / full) + 0.5)
    base = odd * (2.0 * device + 1.0)
    cycle = 4.0 * segments
    base = (base - cycle * jnp.floor(base * (1.0 / cycle))) * float(width)
    total = inner + base
    total = total - full * jnp.floor(total * (1.0 / full) + 0.5)
    angle = total * (2.0 * math.pi / full)
    return jnp.cos(angle), jnp.sin(angle)


def parts(values):
    high = values.astype(BF)
    return high, (values - high.astype(F32)).astype(BF)


def stacked(values):
    high, low = parts(values)
    return jnp.concatenate([high, high, low], axis=0)


def product(a, b, dims):
    return lax.dot_general(a, b, (dims, ((), ())), preferred_element_type=F32)


def fill_phases(cut_ref, places_ref, device, segments, width, table_ref):
    for side in range(2):
        cosine, sine = phases(cut_ref[...], places_ref[side], device, segments, width)
        table_ref[2 * side] = cosine
        table_ref[2 * side + 1] = sine


def analyse_lines(lines, gather_ref, local_ref, table_ref, near_ref, moment_ref):
    nodes = gather_ref.shape[0] // 2
    tiles = lines.shape[0] // LANES
    high, low = parts(lines)
    both = product(gather_ref[...], high, ((1,), (1,)))
    rest = product(gather_ref[:nodes], low, ((1,), (1,)))
    held = both[:nodes] + both[nodes:] + rest
    for tile in range(tiles):
        mine = held[:, tile * LANES : (tile + 1) * LANES]
        turned = jnp.concatenate([mine * table_ref[0], mine * table_ref[1]], axis=1)
        out = product(local_ref[...], stacked(turned), ((1,), (0,)))
        near_ref[tile] = (
            table_ref[3] * out[:nodes, :LANES] - table_ref[2] * out[:nodes, LANES:]
        )
        moment_ref[tile, 0] = out[nodes:, :LANES]
        moment_ref[tile, 1] = out[nodes:, LANES:]


def analyse_kernel(
    segments, first, groups, device_ref, cut_ref, places_ref, gather_ref, local_ref,
    u_ref, v_ref, q_ref, near_ref, moment_ref, lines_ref, table_ref, sems,
):
    step = pl.program_id(0)
    width = u_ref.shape[2]
    levels = lines_ref.shape[1]

    def transfer(at, start):
        field, group = at // groups, at % groups
        slot = at % 2
        for number, ref in enumerate((u_ref, v_ref, q_ref)):

            @pl.when(field == number)
            def _():
                copy = pltpu.make_async_copy(
                    ref.at[pl.ds(first + group * levels, levels)], lines_ref.at[slot], sems.at[slot]
                )
                if start:
                    copy.start()
                else:
                    copy.wait()

    @pl.when(step == 0)
    def _():
        transfer(step, True)
        fill_phases(cut_ref, places_ref, device_ref[0].astype(F32), segments, width, table_ref)

    @pl.when(step + 1 < pl.num_programs(0))
    def _():
        transfer(step + 1, True)

    transfer(step, False)
    lines = lines_ref[step % 2]
    lines = lines.reshape(levels * lines.shape[1], width)
    analyse_lines(lines, gather_ref, local_ref, table_ref, near_ref, moment_ref)


def edge_kernel(
    segments, device_ref, cut_ref, places_ref, gather_ref, local_ref, up_ref, down_ref,
    near_in, moment_in, near_ref, moment_ref, table_ref,
):
    width = up_ref.shape[1]
    fill_phases(cut_ref, places_ref, device_ref[0].astype(F32), segments, width, table_ref)
    count = up_ref.shape[0]
    pad = jnp.zeros((LANES - 2 * count, width), F32)
    lines = jnp.concatenate([up_ref[...], down_ref[...], pad], axis=0)
    analyse_lines(lines, gather_ref, local_ref, table_ref, near_ref, moment_ref)


def finish_kernel(
    segments, first, levels_total, device_ref, cut_ref, edge_cut_ref, places_ref, far_ref, spread_ref,
    scale_ref, edge_scale_ref,
    near_u, near_v, near_q, near_e, far_u, far_v, far_q, far_e, tracer_ref,
    next_ref, div_ref, vort_ref, table_ref, edge_ref,
):
    step = pl.program_id(0)
    pair, rows, width = tracer_ref.shape
    moments = far_u.shape[3]
    nodes = near_u.shape[1]
    lanes = spread_ref.shape[1]
    device = device_ref[0].astype(F32)

    def whole(near_parts, far_parts, table):
        count = len(near_parts)
        sides = []
        for side in range(2):
            for part in far_parts:
                sides.append(part[:, 0, side].reshape(segments * moments, LANES))
        got = product(far_ref[0], stacked(jnp.concatenate(sides, axis=1)), ((1,), (0,)))
        values = []
        for i, near in enumerate(near_parts):
            cosine = got[:, i * LANES : (i + 1) * LANES]
            sine = got[:, (count + i) * LANES : (count + i + 1) * LANES]
            values.append(near[0] + table[1] * cosine - table[0] * sine)
        held = stacked(jnp.concatenate(values, axis=1))
        return product(held, spread_ref[...], ((0,), (0,)))

    @pl.when(step == 0)
    def _():
        cosine, sine = phases(edge_cut_ref[...], places_ref[1], device, segments, width)
        table_ref[0] = cosine
        table_ref[1] = sine
        edges = whole([near_e], [far_e], table_ref)
        edge_ref[...] = edges[: edge_ref.shape[0]] * edge_scale_ref[...]
        cosine, sine = phases(cut_ref[...], places_ref[1], device, segments, width)
        table_ref[0] = cosine
        table_ref[1] = sine

    filtered = whole([near_u, near_v, near_q], [far_u, far_v, far_q], table_ref)
    scale = scale_ref[...]
    inverse = 1.0 / scale
    row_number = lax.broadcasted_iota(jnp.int32, (rows, 1), 0)
    for part in range(pair):
        level = first + step * pair + part

        def field(number):
            at = number * pair * rows + part * rows
            return filtered[at : at + rows]

        def east_west(values):
            return pltpu.roll(values, lanes - 1, 1) - pltpu.roll(values, 1, 1)

        def north_south(values, number):
            above = edge_ref[pl.ds(number * levels_total + level, 1), :]
            below = edge_ref[pl.ds((3 + number) * levels_total + level, 1), :]
            later = jnp.where(row_number == rows - 1, below, pltpu.roll(values, rows - 1, 0))
            earlier = jnp.where(row_number == 0, above, pltpu.roll(values, 1, 0))
            return later - earlier

        u, v, q = field(0), field(1), field(2)
        div = scale * (east_west(u) + north_south(v * inverse, 1))
        vort = scale * (east_west(v) - north_south(u * inverse, 0))
        change = courant * (u * scale * east_west(q) + v * north_south(q, 2))
        div_ref[part] = div[:, :width]
        vort_ref[part] = vort[:, :width]
        next_ref[part] = tracer_ref[part] - change[:, :width]


def whole_spec():
    return pl.BlockSpec(memory_space=pltpu.VMEM)


def on_device(segments, lats, tables, wind_u, wind_v, tracer, cutoff, row_scale):
    levels, rows, width = wind_u.shape
    gather_table, local_table, far_table, spread_table, places = tables
    nodes = gather_table.shape[0] // 2
    lanes = spread_table.shape[1]
    nl = levels // CHUNKS
    pair = LANES // rows
    group = 2 * pair
    groups = nl // group
    tiles = 3 * nl // pair
    device = lax.axis_index("lon").astype(jnp.int32)[None]

    def edge(row):
        pack = jnp.stack([cutoff[row].astype(F32), row_scale[row]])
        pack = jnp.pad(pack, (0, width - 2))[None]
        return jnp.concatenate([wind_u[:, row], wind_v[:, row], tracer[:, row], pack], axis=0)

    up = lax.ppermute(edge(rows - 1), "lat", [(i, i + 1) for i in range(lats - 1)])
    down = lax.ppermute(edge(0), "lat", [(i + 1, i) for i in range(lats - 1)])
    count = 3 * levels
    edge_cut = jnp.concatenate(
        [
            jnp.broadcast_to(up[count, 0], (count,)),
            jnp.broadcast_to(down[count, 0], (count,)),
            jnp.ones((LANES - 2 * count,), F32),
        ]
    )[None]
    weighted = jnp.arange(count) < 2 * levels

    def edge_weight(got):
        held = got[count, 1]
        held = jnp.where(held > 0.0, held, 1.0)
        return jnp.where(weighted, 1.0 / held, 1.0)

    edge_scale = jnp.concatenate([edge_weight(up), edge_weight(down)])[:, None]
    cut = jnp.tile(cutoff.astype(F32), pair)[None]
    scale = row_scale[:, None]

    smem = pl.BlockSpec(memory_space=pltpu.SMEM)
    anywhere = pl.BlockSpec(memory_space=pl.ANY)
    params = pltpu.CompilerParams(
        dimension_semantics=("arbitrary",), vmem_limit_bytes=VMEM_LIMIT
    )
    table_scratch = pltpu.VMEM((4, nodes, LANES), F32)

    def analyse(chunk, extra):
        shapes = (
            jax.ShapeDtypeStruct((tiles + extra, nodes, LANES), F32),
            jax.ShapeDtypeStruct((tiles + extra, 2, MOMENTS, LANES), F32),
        )
        return pl.pallas_call(
            functools.partial(analyse_kernel, segments, chunk * nl, groups),
            out_shape=shapes,
            grid=(3 * groups,),
            in_specs=[smem] + [whole_spec()] * 4 + [anywhere] * 3,
            out_specs=(
                pl.BlockSpec((2, nodes, LANES), lambda s: (s, 0, 0)),
                pl.BlockSpec((2, 2, MOMENTS, LANES), lambda s: (s, 0, 0, 0)),
            ),
            scratch_shapes=[
                pltpu.VMEM((2, group, rows, width), F32),
                table_scratch,
                pltpu.SemaphoreType.DMA((2,)),
            ],
            compiler_params=params,
            name="analyse",
        )(device, cut, places, gather_table, local_table, wind_u, wind_v, tracer)

    def analyse_edges(near, moment):
        last = tiles
        return pl.pallas_call(
            functools.partial(edge_kernel, segments),
            out_shape=(
                jax.ShapeDtypeStruct(near.shape, F32),
                jax.ShapeDtypeStruct(moment.shape, F32),
            ),
            grid=(1,),
            in_specs=[smem] + [whole_spec()] * 6 + [anywhere] * 2,
            out_specs=(
                pl.BlockSpec((1, nodes, LANES), lambda s: (last, 0, 0)),
                pl.BlockSpec((1, 2, MOMENTS, LANES), lambda s: (last, 0, 0, 0)),
            ),
            scratch_shapes=[table_scratch],
            input_output_aliases={7: 0, 8: 1},
            compiler_params=params,
            name="edges",
        )(device, edge_cut, places, gather_table, local_table, up[:count], down[:count], near, moment)

    def finish(chunk, near, far, edge_near, edge_far):
        per_field = nl // pair

        def near_spec(at, moving):
            return pl.BlockSpec((1, nodes, LANES), lambda s, d: (at + s * moving, 0, 0))

        def far_spec(at, moving):
            return pl.BlockSpec(
                (segments, 1, 2, MOMENTS, LANES), lambda s, d: (0, at + s * moving, 0, 0, 0)
            )

        start = chunk * nl // pair
        block = pl.BlockSpec((pair, rows, width), lambda s, d: (start + s, 0, 0))
        out_block = pl.BlockSpec((pair, rows, width), lambda s, d: (s, 0, 0))
        return pl.pallas_call(
            functools.partial(finish_kernel, segments, chunk * nl, levels),
            out_shape=(jax.ShapeDtypeStruct((nl, rows, width), F32),) * 3,
            grid_spec=pltpu.PrefetchScalarGridSpec(
                num_scalar_prefetch=1,
                grid=(per_field,),
                in_specs=[whole_spec()] * 3
                + [pl.BlockSpec((1,) + far_table.shape[1:], lambda s, d: (d[0], 0, 0))]
                + [whole_spec()] * 3
                + [near_spec(0, 1), near_spec(per_field, 1), near_spec(2 * per_field, 1)]
                + [near_spec(tiles, 0)]
                + [far_spec(0, 1), far_spec(per_field, 1), far_spec(2 * per_field, 1)]
                + [far_spec(tiles, 0), block],
                out_specs=(out_block,) * 3,
                scratch_shapes=[
                    pltpu.VMEM((2, nodes, LANES), F32),
                    pltpu.VMEM((2 * count, lanes), F32),
                ],
            ),
            compiler_params=params,
            name="finish",
        )(
            device, cut, edge_cut, places, far_table, spread_table, scale, edge_scale,
            near, near, near, edge_near, far, far, far, edge_far, tracer,
        )

    near, moment = analyse(0, 1)
    near, moment = analyse_edges(near, moment)
    far = lax.all_gather(moment, "lon")
    return finish(0, near, far, near, far)


def solution(mesh):
    segments, lats = mesh.shape["lon"], mesh.shape["lat"]
    tables = tuple(make_tables(NLON // segments, segments))
    line = P(None, "lat", "lon")
    return jax.shard_map(
        functools.partial(on_device, segments, lats, tables),
        mesh=mesh,
        in_specs=(line, line, line, P("lat"), P("lat")),
        out_specs=(line, line, line),
        check_vma=False,
    )
```

```python
import functools
import math

import jax
import jax.numpy as jnp
import ml_dtypes
import numpy as np
from jax import lax
from jax.experimental import pallas as pl
from jax.experimental.pallas import tpu as pltpu
from jax.sharding import PartitionSpec as P

NLON = 12000
KMAX = 1024
NEAR = 16
FAR = 8
EXTRA = 32
LANES = 128
CHUNKS = 1
courant = 0.5
BF = jnp.bfloat16
F32 = jnp.float32
VMEM_LIMIT = 56 * 1024 * 1024


def prolate(points, band, count):
    i = np.arange(points)
    diag = ((points - 1 - 2 * i) / 2.0) ** 2 * np.cos(2 * np.pi * band)
    off = i[1:] * (points - i[1:]) / 2.0
    mid = points // 2
    half = (count + 1) // 2
    out = np.zeros((points, 2 * half))
    dd, ee = diag[mid:], off[mid:].copy()
    scaled = ee.copy()
    scaled[0] *= math.sqrt(2.0)
    even = np.linalg.eigh(np.diag(dd) + np.diag(scaled, 1) + np.diag(scaled, -1))[1]
    even = even[:, ::-1][:, :half]
    wing = even[1:] / math.sqrt(2.0)
    out[mid, 0::2] = even[0]
    out[mid + 1 :, 0::2] = wing
    out[:mid, 0::2] = wing[::-1]
    odd = np.linalg.eigh(np.diag(dd[1:]) + np.diag(ee[1:], 1) + np.diag(ee[1:], -1))[1]
    wing = odd[:, ::-1][:, :half] / math.sqrt(2.0)
    out[mid + 1 :, 1::2] = wing
    out[:mid, 1::2] = -wing[::-1]
    return out


def interpolation(low, high, nodes, snap):
    fine = prolate(2 * (high - low) + 1, (KMAX - 0.5) / NLON / 2, nodes + 2)
    wave = fine[:, nodes]
    at = np.nonzero(wave[:-1] * wave[1:] < 0)[0]
    roots = (at + wave[at] / (wave[at] - wave[at + 1]))[: nodes // 2] / 2 + low
    left = snap(roots)
    for i in range(1, len(left)):
        left[i] = max(left[i], left[i - 1] + 1)
    places = np.concatenate([left, (low + high) - left[::-1]])
    kept = nodes - 4
    index = np.round((places - low) * 2).astype(int)
    return places, fine[::2, :kept] @ np.linalg.pinv(fine[index, :kept])


def near_kernel(distance):
    return 1.0 / (NLON * np.sin(np.pi * distance / NLON))


def two_parts(table):
    high = table.astype(np.float32).astype(ml_dtypes.bfloat16)
    low = (table - high.astype(np.float64)).astype(np.float32).astype(ml_dtypes.bfloat16)
    return high, low


@functools.lru_cache(maxsize=4)
def make_tables(width, segments):
    main = -(-2 * KMAX * width // NLON // LANES) * LANES
    nodes = main + EXTRA
    source, gather = interpolation(0, width - 1, nodes, np.round)
    target, spread = interpolation(-1, width, nodes, lambda r: np.floor(r) + 0.5)
    local = near_kernel(target[:, None] - source[None])
    offsets = [d for d in range(-(segments - 1), segments) if d]
    far = {d: near_kernel(target[:, None] + width * d - source[None]) for d in offsets}

    def leading(kernel, count):
        found = np.linalg.svd(kernel, full_matrices=False)[2][:count]
        peak = np.take_along_axis(found, np.abs(found).argmax(1)[:, None], 1)
        return found * np.sign(peak)

    right, left = leading(far[1], NEAR), leading(far[-1], NEAR)
    every = np.concatenate([far[d] for d in range(2, segments - 1)])
    half = nodes // 2
    mirrored = every[:, ::-1][:, :half]
    even = leading(every[:, :half] + mirrored, FAR // 2)
    odd = leading(every[:, :half] - mirrored, FAR // 2)
    rest = np.concatenate(
        [np.concatenate([even, even[:, ::-1]], 1), np.concatenate([odd, -odd[:, ::-1]], 1)]
    ) / math.sqrt(2.0)

    high, low = two_parts(gather.T)
    gather_table = np.concatenate([high, low], 0)
    high, low = two_parts(np.concatenate([local, right, left, rest], 0))
    local_table = np.concatenate([high, low, high], 1)
    blocks = []
    for d in range(segments):
        row = [far[d - (d - 1) % segments] @ right.T, far[d - (d + 1) % segments] @ left.T]
        row += [far[d - (d - s) % segments] @ rest.T for s in range(2, segments - 1)]
        high, low = two_parts(np.concatenate(row, 1))
        blocks.append(np.concatenate([high, low, high], 1))
    far_table = np.stack(blocks)
    lanes = -(-(width + 2) // LANES) * LANES
    wide = np.zeros((nodes, lanes))
    wide[:, : width + 1] = spread.T[:, 1:]
    wide[:, lanes - 1] = spread.T[:, 0]
    high, low = two_parts(wide)
    none = np.zeros((LANES - 3 * EXTRA, lanes), high.dtype)
    spread_table = np.concatenate(
        [high[:main], low[:main], high[:main], high[main:], low[main:], high[main:], none], 0
    )
    places = np.stack([2 * source - width, 2 * target - width]).astype(np.float32)
    return gather_table, local_table, far_table, spread_table, places[:, :, None]


def phases(cut, places, device, segments, width):
    full = 4.0 * NLON
    odd = 2.0 * cut - 1.0
    inner = odd * places
    inner = inner - full * jnp.floor(inner * (1.0 / full) + 0.5)
    base = odd * (2.0 * device + 1.0)
    cycle = 4.0 * segments
    base = (base - cycle * jnp.floor(base * (1.0 / cycle))) * float(width)
    total = inner + base
    total = total - full * jnp.floor(total * (1.0 / full) + 0.5)
    quarter = jnp.floor(total * (4.0 / full) + 0.5)
    x = (total - (full / 4.0) * quarter) * (2.0 * math.pi / full)
    y = x * x
    sine = x + x * y * (
        -1.0 / 6 + y * (1.0 / 120 + y * (-1.0 / 5040 + y * (1.0 / 362880)))
    )
    cosine = 1.0 + y * (
        -0.5 + y * (1.0 / 24 + y * (-1.0 / 720 + y * (1.0 / 40320 + y * (-1.0 / 3628800))))
    )
    odd_quarter = jnp.abs(quarter) == 1.0
    turned_c = jnp.where(odd_quarter, -quarter * sine, cosine)
    turned_s = jnp.where(odd_quarter, quarter * cosine, sine)
    flip = jnp.where(jnp.abs(quarter) == 2.0, -1.0, 1.0)
    return turned_c * flip, turned_s * flip


def parts(values):
    high = values.astype(BF)
    return high, (values - high.astype(F32)).astype(BF)


def stacked(values):
    high, low = parts(values)
    return jnp.concatenate([high, high, low], axis=0)


def product(a, b, dims):
    return lax.dot_general(a, b, (dims, ((), ())), preferred_element_type=F32)


def lane_cut(cut_ref):
    cut = cut_ref[...].astype(F32)
    return jnp.concatenate([cut] * (LANES // cut.shape[1]), axis=1)


def packed(values):
    main = values.shape[1] - LANES
    high, low = parts(values)
    last, last_low = high[:, main:].astype(F32), low[:, main:].astype(F32)
    last = last + pltpu.roll(last, EXTRA, 1) + pltpu.roll(last_low, 2 * EXTRA, 1)
    return jnp.concatenate([high[:, :main], low[:, :main], last.astype(BF)], axis=1)


def spread_lines(pack, spread_ref):
    main = (pack.shape[1] - LANES) // 2
    held = jnp.concatenate([pack[:, :main], pack], axis=1)
    return product(held, spread_ref[...], ((1,), (0,)))


def analyse_kernel(
    segments, first, groups, device_ref, cut_ref, places_ref, gather_ref, local_ref,
    u_ref, v_ref, q_ref, near_ref, right_ref, left_ref, far_ref, lines_ref, table_ref, sems,
):
    step = pl.program_id(0)
    width = u_ref.shape[2]
    levels = lines_ref.shape[1]
    nodes = gather_ref.shape[0] // 2

    def transfer(at, start):
        field, group = at // groups, at % groups
        slot = at % 2
        for number, ref in enumerate((u_ref, v_ref, q_ref)):

            @pl.when(field == number)
            def _():
                copy = pltpu.make_async_copy(
                    ref.at[pl.ds(first + group * levels, levels)], lines_ref.at[slot], sems.at[slot]
                )
                if start:
                    copy.start()
                else:
                    copy.wait()

    @pl.when(step == 0)
    def _():
        transfer(step, True)
        device = device_ref[0].astype(F32)
        for side in range(2):
            cosine, sine = phases(lane_cut(cut_ref), places_ref[side], device, segments, width)
            table_ref[2 * side] = cosine
            table_ref[2 * side + 1] = sine

    @pl.when(step + 1 < pl.num_programs(0))
    def _():
        transfer(step + 1, True)

    transfer(step, False)
    lines = lines_ref[step % 2]
    lines = lines.reshape(levels * lines.shape[1], width)
    high, low = parts(lines)
    both = product(gather_ref[...], high, ((1,), (1,)))
    rest = product(gather_ref[:nodes], low, ((1,), (1,)))
    held = both[:nodes] + both[nodes:] + rest
    for tile in range(lines.shape[0] // LANES):
        mine = held[:, tile * LANES : (tile + 1) * LANES]
        turned = jnp.concatenate([mine * table_ref[0], mine * table_ref[1]], axis=1)
        out = product(local_ref[...], stacked(turned), ((1,), (0,)))
        near_ref[tile] = (
            table_ref[3] * out[:nodes, :LANES] - table_ref[2] * out[:nodes, LANES:]
        )
        at = nodes
        for ref in (right_ref, left_ref, far_ref):
            count = ref.shape[2]
            ref[tile, 0] = out[at : at + count, :LANES]
            ref[tile, 1] = out[at : at + count, LANES:]
            at += count


def combine_kernel(segments, width, per_field, device_ref, cut_ref, scale_ref, places_ref, table_in, near_ref, *refs):
    moment_refs, (pack_ref, top_ref, bottom_ref, table_ref) = refs[:-4], refs[-4:]
    step = pl.program_id(0)
    tiles, nodes, _ = near_ref.shape
    rows = cut_ref.shape[1]

    @pl.when(step == 0)
    def _():
        device = device_ref[0].astype(F32)
        cosine, sine = phases(lane_cut(cut_ref), places_ref[1], device, segments, width)
        table_ref[0] = cosine
        table_ref[1] = sine

    sides = []
    for tile in range(tiles):
        for side in range(2):
            sides.append(jnp.concatenate([ref[tile, side] for ref in moment_refs], axis=0))
    got = product(table_in[0], stacked(jnp.concatenate(sides, axis=1)), ((1,), (0,)))
    inverse = 1.0 / scale_ref[...]
    none = jnp.zeros((LANES - EXTRA, LANES), F32)
    for tile in range(tiles):
        at = 2 * tile * LANES
        cosine, sine = got[:, at : at + LANES], got[:, at + LANES : at + 2 * LANES]
        values = near_ref[tile] + table_ref[1] * cosine - table_ref[0] * sine
        values = jnp.transpose(jnp.concatenate([values, none], axis=0))
        pack_ref[tile] = packed(values)
        number = step * tiles + tile
        wind = number < 2 * per_field
        top_weight = jnp.where(wind, inverse[:, :1], 1.0)
        bottom_weight = jnp.where(wind, inverse[:, rows - 1 :], 1.0)
        pair = LANES // rows
        for part in range(pair):
            line = number * pair + part
            top_ref[pl.ds(line, 1), :] = values[part * rows : part * rows + 1] * top_weight
            last = part * rows + rows - 1
            bottom_ref[pl.ds(line, 1), :] = values[last : last + 1] * bottom_weight


def finish_kernel(
    scale_ref, spread_ref, above_ref, below_ref, pack_u, pack_v, pack_q, tracer_ref, *refs
):
    next_ref, div_ref, vort_ref, edge_ref, column_ref = refs[-5:]
    step = pl.program_id(0)
    pair, rows, width = tracer_ref.shape
    lanes = spread_ref.shape[1]
    count = above_ref.shape[0]
    levels = count // 3

    @pl.when(step == 0)
    def _():
        edges = jnp.concatenate([above_ref[...], below_ref[...]], axis=0)
        edge_ref[...] = spread_lines(packed(edges), spread_ref)
        here = lax.broadcasted_iota(jnp.int32, (rows, rows), 0)
        there = lax.broadcasted_iota(jnp.int32, (rows, rows), 1)
        column = jnp.where(here == there, jnp.broadcast_to(scale_ref[...], (rows, rows)), 0.0)
        column = jnp.sum(column, axis=1, keepdims=True)
        column_ref[0] = jnp.broadcast_to(column, (rows, LANES))
        column_ref[1] = 1.0 / column_ref[0]

    pack = jnp.concatenate([pack_u[0], pack_v[0], pack_q[0]], axis=0)
    filtered = spread_lines(pack, spread_ref)
    scale = column_ref[0][:, :1]
    inverse = column_ref[1][:, :1]
    row_number = lax.broadcasted_iota(jnp.int32, (rows, 1), 0)
    for part in range(pair):
        level = step * pair + part

        def field(number):
            at = number * pair * rows + part * rows
            return filtered[at : at + rows]

        def east_west(values):
            return pltpu.roll(values, lanes - 1, 1) - pltpu.roll(values, 1, 1)

        def north_south(values, number):
            above = edge_ref[pl.ds(number * levels + level, 1), :]
            below = edge_ref[pl.ds(count + number * levels + level, 1), :]
            later = jnp.where(row_number == rows - 1, below, pltpu.roll(values, rows - 1, 0))
            earlier = jnp.where(row_number == 0, above, pltpu.roll(values, 1, 0))
            return later - earlier

        u, v, q = field(0), field(1), field(2)
        div = scale * (east_west(u) + north_south(v * inverse, 1))
        vort = scale * (east_west(v) - north_south(u * inverse, 0))
        change = courant * (u * scale * east_west(q) + v * north_south(q, 2))
        div_ref[part] = div[:, :width]
        vort_ref[part] = vort[:, :width]
        next_ref[part] = tracer_ref[part] - change[:, :width]


def whole_spec():
    return pl.BlockSpec(memory_space=pltpu.VMEM)


def on_device(segments, lats, tables, wind_u, wind_v, tracer, cutoff, row_scale):
    levels, rows, width = wind_u.shape
    gather_table, local_table, far_table, spread_table, places = tables
    nodes = gather_table.shape[0] // 2
    lanes = spread_table.shape[1]
    wide = nodes - EXTRA + LANES
    nl = levels // CHUNKS
    pair = LANES // rows
    group = 2 * pair
    groups = nl // group
    tiles = 3 * nl // pair
    per_field = nl // pair
    count = 3 * nl
    device = lax.axis_index("lon").astype(jnp.int32)[None]
    cut = cutoff.reshape(1, rows)
    scale = row_scale.reshape(1, rows)

    smem = pl.BlockSpec(memory_space=pltpu.SMEM)
    anywhere = pl.BlockSpec(memory_space=pl.ANY)
    params = pltpu.CompilerParams(
        dimension_semantics=("arbitrary",), vmem_limit_bytes=VMEM_LIMIT
    )

    def analyse(chunk):
        moments = (NEAR, NEAR, FAR)
        return pl.pallas_call(
            functools.partial(analyse_kernel, segments, chunk * nl, groups),
            out_shape=(jax.ShapeDtypeStruct((tiles, nodes, LANES), F32),)
            + tuple(jax.ShapeDtypeStruct((tiles, 2, n, LANES), F32) for n in moments),
            grid=(3 * groups,),
            in_specs=[smem] + [whole_spec()] * 4 + [anywhere] * 3,
            out_specs=(pl.BlockSpec((2, nodes, LANES), lambda s: (s, 0, 0)),)
            + tuple(pl.BlockSpec((2, 2, n, LANES), lambda s: (s, 0, 0, 0)) for n in moments),
            scratch_shapes=[
                pltpu.VMEM((2, group, rows, width), F32),
                pltpu.VMEM((4, nodes, LANES), F32),
                pltpu.SemaphoreType.DMA((2,)),
            ],
            compiler_params=params,
            name="analyse",
        )(device, cut, places, gather_table, local_table, wind_u, wind_v, tracer)

    def exchange(right, left, far):
        def shifted(array, by):
            return lax.ppermute(
                array, "lon", [(i, (i + by) % segments) for i in range(segments)]
            )

        got = [shifted(right, 1), shifted(left, -1)]
        return got + [shifted(far, s) for s in range(2, segments - 1)]

    def combine(near, moments):
        step_tiles = 2
        moment_specs = [
            pl.BlockSpec((step_tiles,) + m.shape[1:], lambda s, d: (s, 0, 0, 0)) for m in moments
        ]
        edge = jax.ShapeDtypeStruct((count, wide), F32)
        return pl.pallas_call(
            functools.partial(combine_kernel, segments, width, per_field),
            out_shape=(
                jax.ShapeDtypeStruct((tiles, LANES, 2 * wide - LANES), BF), edge, edge,
            ),
            grid_spec=pltpu.PrefetchScalarGridSpec(
                num_scalar_prefetch=1,
                grid=(tiles // step_tiles,),
                in_specs=[whole_spec()] * 3
                + [pl.BlockSpec((1,) + far_table.shape[1:], lambda s, d: (d[0], 0, 0))]
                + [pl.BlockSpec((step_tiles, nodes, LANES), lambda s, d: (s, 0, 0))]
                + moment_specs,
                out_specs=(
                    pl.BlockSpec((step_tiles, LANES, 2 * wide - LANES), lambda s, d: (s, 0, 0)),
                    pl.BlockSpec((count, wide), lambda s, d: (0, 0)),
                    pl.BlockSpec((count, wide), lambda s, d: (0, 0)),
                ),
                scratch_shapes=[pltpu.VMEM((2, nodes, LANES), F32)],
            ),
            compiler_params=params,
            name="combine",
        )(device, cut, scale, places, far_table, near, *moments)

    def finish(chunk, pack, above, below, before):
        def pack_spec(field):
            return pl.BlockSpec(
                (1, LANES, 2 * wide - LANES), lambda s: (field * per_field + s, 0, 0)
            )

        start = chunk * nl // pair
        block = pl.BlockSpec((pair, rows, width), lambda s: (start + s, 0, 0))
        return pl.pallas_call(
            finish_kernel,
            out_shape=(jax.ShapeDtypeStruct((levels, rows, width), F32),) * 3,
            grid=(per_field,),
            in_specs=[whole_spec()] * 4
            + [pack_spec(0), pack_spec(1), pack_spec(2), block]
            + [anywhere] * len(before),
            out_specs=(block,) * 3,
            scratch_shapes=[
                pltpu.VMEM((2 * count, lanes), F32),
                pltpu.VMEM((2, rows, LANES), F32),
            ],
            input_output_aliases={8 + i: i for i in range(len(before))},
            compiler_params=params,
            name="finish",
        )(scale, spread_table, above, below, pack, pack, pack, tracer, *before)

    analysed = [analyse(chunk) for chunk in range(CHUNKS)]
    moments = [exchange(*got[1:]) for got in analysed]
    edges, packs = [], []
    for got, moment in zip(analysed, moments):
        pack, top, bottom = combine(got[0], moment)
        above = lax.ppermute(bottom, "lat", [(i, i + 1) for i in range(lats - 1)])
        below = lax.ppermute(top, "lat", [(i + 1, i) for i in range(lats - 1)])
        packs.append(pack)
        edges.append((above, below))
    out = ()
    for chunk in range(CHUNKS):
        out = finish(chunk, packs[chunk], *edges[chunk], out)
    return out


def solution(mesh):
    segments, lats = mesh.shape["lon"], mesh.shape["lat"]
    tables = tuple(make_tables(NLON // segments, segments))
    line = P(None, "lat", "lon")
    return jax.shard_map(
        functools.partial(on_device, segments, lats, tables),
        mesh=mesh,
        in_specs=(line, line, line, P("lat"), P("lat")),
        out_specs=(line, line, line),
        check_vma=False,
    )
```

```python
import functools
import math

import jax
import jax.numpy as jnp
import ml_dtypes
import numpy as np
from jax import lax
from jax.experimental import pallas as pl
from jax.experimental.pallas import tpu as pltpu
from jax.sharding import PartitionSpec as P

NLON = 12000
KMAX = 1024
NEAR = 12
FAR = 4
EXTRA = 32
LANES = 128
CHUNKS = 1
courant = 0.5
BF = jnp.bfloat16
F32 = jnp.float32
VMEM_LIMIT = 56 * 1024 * 1024


def prolate(points, band, count):
    i = np.arange(points)
    diag = ((points - 1 - 2 * i) / 2.0) ** 2 * np.cos(2 * np.pi * band)
    off = i[1:] * (points - i[1:]) / 2.0
    mid = points // 2
    half = (count + 1) // 2
    out = np.zeros((points, 2 * half))
    dd, ee = diag[mid:], off[mid:].copy()
    scaled = ee.copy()
    scaled[0] *= math.sqrt(2.0)
    even = np.linalg.eigh(np.diag(dd) + np.diag(scaled, 1) + np.diag(scaled, -1))[1]
    even = even[:, ::-1][:, :half]
    wing = even[1:] / math.sqrt(2.0)
    out[mid, 0::2] = even[0]
    out[mid + 1 :, 0::2] = wing
    out[:mid, 0::2] = wing[::-1]
    odd = np.linalg.eigh(np.diag(dd[1:]) + np.diag(ee[1:], 1) + np.diag(ee[1:], -1))[1]
    wing = odd[:, ::-1][:, :half] / math.sqrt(2.0)
    out[mid + 1 :, 1::2] = wing
    out[:mid, 1::2] = -wing[::-1]
    return out


def interpolation(low, high, nodes, snap):
    fine = prolate(2 * (high - low) + 1, (KMAX - 0.5) / NLON / 2, nodes + 2)
    wave = fine[:, nodes]
    at = np.nonzero(wave[:-1] * wave[1:] < 0)[0]
    roots = (at + wave[at] / (wave[at] - wave[at + 1]))[: nodes // 2] / 2 + low
    left = snap(roots)
    for i in range(1, len(left)):
        left[i] = max(left[i], left[i - 1] + 1)
    places = np.concatenate([left, (low + high) - left[::-1]])
    kept = nodes - 4
    index = np.round((places - low) * 2).astype(int)
    return places, fine[::2, :kept] @ np.linalg.pinv(fine[index, :kept])


def near_kernel(distance):
    return 1.0 / (NLON * np.sin(np.pi * distance / NLON))


def two_parts(table):
    high = table.astype(np.float32).astype(ml_dtypes.bfloat16)
    low = (table - high.astype(np.float64)).astype(np.float32).astype(ml_dtypes.bfloat16)
    return high, low


@functools.lru_cache(maxsize=4)
def make_tables(width, segments):
    main = -(-2 * KMAX * width // NLON // LANES) * LANES
    nodes = main + EXTRA
    source, gather = interpolation(0, width - 1, nodes, np.round)
    target, spread = interpolation(-1, width, nodes, lambda r: np.floor(r) + 0.5)
    local = near_kernel(target[:, None] - source[None])
    offsets = [d for d in range(-(segments - 1), segments) if d]
    far = {d: near_kernel(target[:, None] + width * d - source[None]) for d in offsets}

    def leading(kernel, count):
        found = np.linalg.svd(kernel, full_matrices=False)[2][:count]
        peak = np.take_along_axis(found, np.abs(found).argmax(1)[:, None], 1)
        return found * np.sign(peak)

    ahead = range(1, segments)
    basis = {s: leading(far[s], FAR) for s in ahead}
    for s in (1, segments - 1):
        both = leading(far[s], FAR + NEAR)
        basis[s], basis[-s] = both[:FAR], both[FAR:]

    high, low = two_parts(gather.T)
    gather_table = np.concatenate([high, low], 0)
    more = [basis[-1], basis[1 - segments]] + [basis[s] for s in ahead]
    rows = np.concatenate([local] + more, 0)
    rows = np.pad(rows, ((0, -len(rows) % 8), (0, 0)))
    high, low = two_parts(rows)
    local_table = np.concatenate([high, low, high], 1)
    blocks = []
    for d in range(segments):
        pieces = [far[d - (d - s) % segments] @ basis[-s].T for s in (1, segments - 1)]
        for e in range(segments):
            if e == d:
                pieces.append(np.zeros((nodes, FAR)))
            else:
                pieces.append(far[d - e] @ basis[(d - e) % segments].T)
        top = [p for piece in pieces for p in (piece, 0 * piece)]
        low_part = [p for piece in pieces for p in (0 * piece, piece)]
        both = np.concatenate([np.concatenate(top, 1), np.concatenate(low_part, 1)], 0)
        high, low = two_parts(both)
        blocks.append(np.concatenate([high, low, high], 1))
    far_table = np.stack(blocks)
    lanes = -(-(width + 2) // LANES) * LANES
    wide = np.zeros((nodes, lanes))
    wide[:, : width + 1] = spread.T[:, 1:]
    wide[:, lanes - 1] = spread.T[:, 0]
    high, low = two_parts(wide)
    none = np.zeros((LANES - 3 * EXTRA, lanes), high.dtype)
    spread_table = np.concatenate(
        [high[:main], low[:main], high[:main], high[main:], low[main:], high[main:], none], 0
    )
    places = np.stack([2 * source - width, 2 * target - width]).astype(np.float32)
    return gather_table, local_table, far_table, spread_table, places[:, :, None]


def phases(cut, places, device, segments, width):
    full = 4.0 * NLON
    odd = 2.0 * cut - 1.0
    inner = odd * places
    inner = inner - full * jnp.floor(inner * (1.0 / full) + 0.5)
    base = odd * (2.0 * device + 1.0)
    cycle = 4.0 * segments
    base = (base - cycle * jnp.floor(base * (1.0 / cycle))) * float(width)
    total = inner + base
    total = total - full * jnp.floor(total * (1.0 / full) + 0.5)
    quarter = jnp.floor(total * (4.0 / full) + 0.5)
    x = (total - (full / 4.0) * quarter) * (2.0 * math.pi / full)
    y = x * x
    sine = x + x * y * (
        -1.0 / 6 + y * (1.0 / 120 + y * (-1.0 / 5040 + y * (1.0 / 362880)))
    )
    cosine = 1.0 + y * (
        -0.5 + y * (1.0 / 24 + y * (-1.0 / 720 + y * (1.0 / 40320 + y * (-1.0 / 3628800))))
    )
    odd_quarter = jnp.abs(quarter) == 1.0
    turned_c = jnp.where(odd_quarter, -quarter * sine, cosine)
    turned_s = jnp.where(odd_quarter, quarter * cosine, sine)
    flip = jnp.where(jnp.abs(quarter) == 2.0, -1.0, 1.0)
    return turned_c * flip, turned_s * flip


def parts(values):
    high = values.astype(BF)
    return high, (values - high.astype(F32)).astype(BF)


def stacked(values):
    high, low = parts(values)
    return jnp.concatenate([high, high, low], axis=0)


def product(a, b, dims):
    return lax.dot_general(a, b, (dims, ((), ())), preferred_element_type=F32)


def lane_cut(cut_ref):
    cut = cut_ref[...].astype(F32)
    return jnp.concatenate([cut] * (LANES // cut.shape[1]), axis=1)


def packed(values):
    main = values.shape[1] - LANES
    high, low = parts(values)
    last, last_low = high[:, main:].astype(F32), low[:, main:].astype(F32)
    last = last + pltpu.roll(last, EXTRA, 1) + pltpu.roll(last_low, 2 * EXTRA, 1)
    return jnp.concatenate([high[:, :main], low[:, :main], last.astype(BF)], axis=1)


def spread_lines(pack, spread_ref):
    main = (pack.shape[1] - LANES) // 2
    held = jnp.concatenate([pack[:, :main], pack], axis=1)
    return product(held, spread_ref[...], ((1,), (0,)))


def analyse_kernel(
    segments, first, groups, device_ref, cut_ref, places_ref, gather_ref, local_ref,
    u_ref, v_ref, q_ref, near_ref, ahead_ref, behind_ref, every_ref, turn_ref,
    lines_ref, high_ref, low_ref, held_ref, table_ref, sems,
):
    width = u_ref.shape[2]
    steps, levels, rows, _ = lines_ref.shape
    lines = levels * rows
    nodes = gather_ref.shape[0] // 2
    me = device_ref[0]

    copies = []
    for step in range(steps):
        ref = (u_ref, v_ref, q_ref)[step // groups]
        levels_at = pl.ds(first + (step % groups) * levels, levels)
        copies.append(pltpu.make_async_copy(ref.at[levels_at], lines_ref.at[step], sems.at[step]))
        copies[-1].start()
    for side in range(2):
        cosine, sine = phases(
            lane_cut(cut_ref), places_ref[side], me.astype(F32), segments, width
        )
        if side == 0:
            table_ref[0], table_ref[1] = cosine, sine
        else:
            turn_ref[0], turn_ref[1] = cosine, sine
    every_ref[me] = jnp.zeros(every_ref.shape[1:], F32)

    def cast(step):
        values = lines_ref[step].reshape(lines, width)
        high, low = parts(values)
        high_ref[step % 2] = high
        low_ref[step % 2] = low

    def gather(step):
        both = product(gather_ref[...], high_ref[step % 2], ((1,), (1,)))
        rest = product(gather_ref[:nodes], low_ref[step % 2], ((1,), (1,)))
        held_ref[step % 2] = both[:nodes] + both[nodes:] + rest

    def local(step):
        for part in range(lines // LANES):
            tile = step * (lines // LANES) + part
            mine = held_ref[step % 2, :, part * LANES : (part + 1) * LANES]
            turned = jnp.concatenate([mine * table_ref[0], mine * table_ref[1]], axis=1)
            out = product(local_ref[...], stacked(turned), ((1,), (0,)))
            near_ref[tile] = (
                turn_ref[1] * out[:nodes, :LANES] - turn_ref[0] * out[:nodes, LANES:]
            )
            at = nodes
            for ref in (ahead_ref, behind_ref):
                ref[tile, :NEAR] = out[at : at + NEAR, :LANES]
                ref[tile, NEAR:] = out[at : at + NEAR, LANES:]
                at += NEAR
            for s in range(1, segments):
                to = lax.rem(me + s, segments)
                every_ref[to, tile, :FAR] = out[at : at + FAR, :LANES]
                every_ref[to, tile, FAR:] = out[at : at + FAR, LANES:]
                at += FAR

    copies[0].wait()
    cast(0)
    for step in range(steps):
        if step + 1 < steps:
            copies[step + 1].wait()
        gather(step)
        if step + 1 < steps:
            cast(step + 1)
        if step > 0:
            local(step - 1)
    local(steps - 1)


def combine_kernel(
    per_field, rows, device_ref, scale_ref, turn_ref, table_in, near_ref, behind_ref, ahead_ref,
    every_ref, pack_ref, top_ref, bottom_ref,
):
    step = pl.program_id(0)
    tiles, nodes, _ = near_ref.shape
    segments = every_ref.shape[0]
    columns = []
    for tile in range(tiles):
        pieces = [behind_ref[tile], ahead_ref[tile]]
        pieces += [every_ref[e, tile] for e in range(segments)]
        columns.append(jnp.concatenate(pieces, axis=0))
    got = product(table_in[0], stacked(jnp.concatenate(columns, axis=1)), ((1,), (0,)))
    inverse = 1.0 / scale_ref[...]
    none = jnp.zeros((LANES - EXTRA, LANES), F32)
    for tile in range(tiles):
        at = tile * LANES
        cosine, sine = got[:nodes, at : at + LANES], got[nodes:, at : at + LANES]
        values = near_ref[tile] + turn_ref[1] * cosine - turn_ref[0] * sine
        values = jnp.transpose(jnp.concatenate([values, none], axis=0))
        pack_ref[tile] = packed(values)
        number = step * tiles + tile
        wind = number < 2 * per_field
        top_weight = jnp.where(wind, inverse[:, :1], 1.0)
        bottom_weight = jnp.where(wind, inverse[:, rows - 1 :], 1.0)
        pair = LANES // rows
        for part in range(pair):
            line = number * pair + part
            top_ref[pl.ds(line, 1), :] = values[part * rows : part * rows + 1] * top_weight
            last = part * rows + rows - 1
            bottom_ref[pl.ds(line, 1), :] = values[last : last + 1] * bottom_weight


def finish_kernel(
    first, scale_ref, spread_ref, above_ref, below_ref, pack_ref, tracer_ref, *refs
):
    outs = refs[-9:-6]
    filtered_ref, edge_ref, column_ref, held_ref, load_sems, sems = refs[-6:]
    _, rows, width = tracer_ref.shape
    lanes = spread_ref.shape[1]
    count = above_ref.shape[0]
    levels = count // 3
    pair = LANES // rows
    steps = levels // pair
    tracer_slot = 6 * pair

    def load(step):
        return pltpu.make_async_copy(
            tracer_ref.at[pl.ds(first + step * pair, pair)],
            held_ref.at[pl.ds(tracer_slot + step % 2 * pair, pair)],
            load_sems.at[step % 2],
        )

    def store(step, number):
        return pltpu.make_async_copy(
            held_ref.at[pl.ds((3 * (step % 2) + number) * pair, pair)],
            outs[number].at[pl.ds(first + step * pair, pair)],
            sems.at[step % 2, number],
        )

    load(0).start()
    edges = jnp.concatenate([above_ref[...], below_ref[...]], axis=0)
    edge_ref[...] = spread_lines(packed(edges), spread_ref)
    here = lax.broadcasted_iota(jnp.int32, (rows, rows), 0)
    there = lax.broadcasted_iota(jnp.int32, (rows, rows), 1)
    column = jnp.where(here == there, jnp.broadcast_to(scale_ref[...], (rows, rows)), 0.0)
    column = jnp.sum(column, axis=1, keepdims=True)
    column_ref[0] = jnp.broadcast_to(column, (rows, LANES))
    column_ref[1] = 1.0 / column_ref[0]
    row_number = lax.broadcasted_iota(jnp.int32, (rows, 1), 0)

    def fill(step):
        pack = jnp.concatenate([pack_ref[f * steps + step] for f in range(3)], axis=0)
        filtered_ref[step % 2] = spread_lines(pack, spread_ref)

    def east_west(values):
        return pltpu.roll(values, lanes - 1, 1) - pltpu.roll(values, 1, 1)

    def stencil(step):
        scale = column_ref[0][:, :1]
        inverse = column_ref[1][:, :1]
        for part in range(pair):
            level = step * pair + part

            def field(number):
                at = number * pair * rows + part * rows
                return filtered_ref[step % 2, at : at + rows]

            def north_south(values, number):
                at = number * levels + level
                above = edge_ref[at : at + 1]
                below = edge_ref[count + at : count + at + 1]
                later = jnp.where(row_number == rows - 1, below, pltpu.roll(values, rows - 1, 0))
                earlier = jnp.where(row_number == 0, above, pltpu.roll(values, 1, 0))
                return later - earlier

            u, v, q = field(0), field(1), field(2)
            div = scale * (east_west(u) + north_south(v * inverse, 1))
            vort = scale * (east_west(v) - north_south(u * inverse, 0))
            change = courant * (u * scale * east_west(q) + v * north_south(q, 2))
            base = 3 * (step % 2) * pair + part
            held_ref[base] = held_ref[tracer_slot + step % 2 * pair + part] - change[:, :width]
            held_ref[base + pair] = div[:, :width]
            held_ref[base + 2 * pair] = vort[:, :width]

    fill(0)
    for step in range(steps):
        if step + 1 < steps:
            load(step + 1).start()
        load(step).wait()
        if step >= 2:
            for number in range(3):
                store(step - 2, number).wait()
        stencil(step)
        if step + 1 < steps:
            fill(step + 1)
        for number in range(3):
            store(step, number).start()
    for step in range(max(steps - 2, 0), steps):
        for number in range(3):
            store(step, number).wait()


def whole_spec():
    return pl.BlockSpec(memory_space=pltpu.VMEM)


def on_device(segments, lats, tables, wind_u, wind_v, tracer, cutoff, row_scale):
    levels, rows, width = wind_u.shape
    gather_table, local_table, far_table, spread_table, places = tables
    nodes = gather_table.shape[0] // 2
    lanes = spread_table.shape[1]
    wide = nodes - EXTRA + LANES
    nl = levels // CHUNKS
    pair = LANES // rows
    group = 2 * pair
    groups = nl // group
    tiles = 3 * nl // pair
    per_field = nl // pair
    count = 3 * nl
    device = lax.axis_index("lon").astype(jnp.int32)[None]
    cut = cutoff.reshape(1, rows)
    scale = row_scale.reshape(1, rows)

    smem = pl.BlockSpec(memory_space=pltpu.SMEM)
    anywhere = pl.BlockSpec(memory_space=pl.ANY)
    params = pltpu.CompilerParams(
        dimension_semantics=("arbitrary",), vmem_limit_bytes=VMEM_LIMIT
    )
    flat = pltpu.CompilerParams(vmem_limit_bytes=VMEM_LIMIT)

    def analyse(chunk):
        steps = 3 * groups
        extra = jax.ShapeDtypeStruct((tiles, 2 * NEAR, LANES), F32)
        return pl.pallas_call(
            functools.partial(analyse_kernel, segments, chunk * nl, groups),
            out_shape=(
                jax.ShapeDtypeStruct((tiles, nodes, LANES), F32),
                extra,
                extra,
                jax.ShapeDtypeStruct((segments, tiles, 2 * FAR, LANES), F32),
                jax.ShapeDtypeStruct((2, nodes, LANES), F32),
            ),
            in_specs=[smem] + [whole_spec()] * 4 + [anywhere] * 3,
            out_specs=(whole_spec(),) * 5,
            scratch_shapes=[
                pltpu.VMEM((steps, group, rows, width), F32),
                pltpu.VMEM((2, group * rows, width), BF),
                pltpu.VMEM((2, group * rows, width), BF),
                pltpu.VMEM((2, nodes, group * rows), F32),
                pltpu.VMEM((2, nodes, LANES), F32),
                pltpu.SemaphoreType.DMA((steps,)),
            ],
            compiler_params=flat,
            name="analyse",
        )(device, cut, places, gather_table, local_table, wind_u, wind_v, tracer)

    def exchange(ahead, behind, every):
        def shifted(array, by):
            return lax.ppermute(
                array, "lon", [(i, (i + by) % segments) for i in range(segments)]
            )

        got = lax.all_to_all(every, "lon", 0, 0)
        return shifted(ahead, 1), shifted(behind, -1), got

    def combine(near, turn, moments):
        step_tiles = 4
        edge = jax.ShapeDtypeStruct((count, wide), F32)
        extra_spec = pl.BlockSpec((step_tiles, 2 * NEAR, LANES), lambda s, d: (s, 0, 0))
        return pl.pallas_call(
            functools.partial(combine_kernel, per_field, rows),
            out_shape=(
                jax.ShapeDtypeStruct((tiles, LANES, 2 * wide - LANES), BF), edge, edge,
            ),
            grid_spec=pltpu.PrefetchScalarGridSpec(
                num_scalar_prefetch=1,
                grid=(tiles // step_tiles,),
                in_specs=[whole_spec()] * 2
                + [pl.BlockSpec((1,) + far_table.shape[1:], lambda s, d: (d[0], 0, 0))]
                + [pl.BlockSpec((step_tiles, nodes, LANES), lambda s, d: (s, 0, 0))]
                + [extra_spec, extra_spec]
                + [
                    pl.BlockSpec(
                        (segments, step_tiles, 2 * FAR, LANES), lambda s, d: (0, s, 0, 0)
                    )
                ],
                out_specs=(
                    pl.BlockSpec((step_tiles, LANES, 2 * wide - LANES), lambda s, d: (s, 0, 0)),
                    pl.BlockSpec((count, wide), lambda s, d: (0, 0)),
                    pl.BlockSpec((count, wide), lambda s, d: (0, 0)),
                ),
            ),
            compiler_params=params,
            name="combine",
        )(device, scale, turn, far_table, near, *moments)

    def finish(chunk, pack, above, below, before):
        return pl.pallas_call(
            functools.partial(finish_kernel, chunk * nl),
            out_shape=(jax.ShapeDtypeStruct((levels, rows, width), F32),) * 3,
            in_specs=[whole_spec()] * 5 + [anywhere] * (1 + len(before)),
            out_specs=(anywhere,) * 3,
            scratch_shapes=[
                pltpu.VMEM((2, 3 * LANES, lanes), F32),
                pltpu.VMEM((2 * count, lanes), F32),
                pltpu.VMEM((2, rows, LANES), F32),
                pltpu.VMEM((8 * pair, rows, width), F32),
                pltpu.SemaphoreType.DMA((2,)),
                pltpu.SemaphoreType.DMA((2, 3)),
            ],
            input_output_aliases={6 + i: i for i in range(len(before))},
            compiler_params=flat,
            name="finish",
        )(scale, spread_table, above, below, pack, tracer, *before)

    analysed = [analyse(chunk) for chunk in range(CHUNKS)]
    moments = [exchange(*got[1:4]) for got in analysed]
    edges, packs = [], []
    for got, moment in zip(analysed, moments):
        pack, top, bottom = combine(got[0], got[4], moment)
        above = lax.ppermute(bottom, "lat", [(i, i + 1) for i in range(lats - 1)])
        below = lax.ppermute(top, "lat", [(i + 1, i) for i in range(lats - 1)])
        packs.append(pack)
        edges.append((above, below))
    out = ()
    for chunk in range(CHUNKS):
        out = finish(chunk, packs[chunk], *edges[chunk], out)
    return out


def solution(mesh):
    segments, lats = mesh.shape["lon"], mesh.shape["lat"]
    tables = tuple(make_tables(NLON // segments, segments))
    line = P(None, "lat", "lon")
    return jax.shard_map(
        functools.partial(on_device, segments, lats, tables),
        mesh=mesh,
        in_specs=(line, line, line, P("lat"), P("lat")),
        out_specs=(line, line, line),
        check_vma=False,
    )
```

```python
import functools
import math

import jax
import jax.numpy as jnp
import ml_dtypes
import numpy as np
from jax import lax
from jax.experimental import pallas as pl
from jax.experimental.pallas import tpu as pltpu
from jax.sharding import PartitionSpec as P

NLON = 12000
KMAX = 1024
NEAR = 12
FAR = 4
EXTRA = 32
LANES = 128
SPAN = 512
CHUNKS = 2
courant = 0.5
BF = jnp.bfloat16
F32 = jnp.float32
VMEM_LIMIT = 56 * 1024 * 1024


def prolate(points, band, count):
    i = np.arange(points)
    diag = ((points - 1 - 2 * i) / 2.0) ** 2 * np.cos(2 * np.pi * band)
    off = i[1:] * (points - i[1:]) / 2.0
    mid = points // 2
    half = (count + 1) // 2
    out = np.zeros((points, 2 * half))
    dd, ee = diag[mid:], off[mid:].copy()
    scaled = ee.copy()
    scaled[0] *= math.sqrt(2.0)
    even = np.linalg.eigh(np.diag(dd) + np.diag(scaled, 1) + np.diag(scaled, -1))[1]
    even = even[:, ::-1][:, :half]
    wing = even[1:] / math.sqrt(2.0)
    out[mid, 0::2] = even[0]
    out[mid + 1 :, 0::2] = wing
    out[:mid, 0::2] = wing[::-1]
    odd = np.linalg.eigh(np.diag(dd[1:]) + np.diag(ee[1:], 1) + np.diag(ee[1:], -1))[1]
    wing = odd[:, ::-1][:, :half] / math.sqrt(2.0)
    out[mid + 1 :, 1::2] = wing
    out[:mid, 1::2] = -wing[::-1]
    return out


def interpolation(low, high, nodes, snap):
    fine = prolate(2 * (high - low) + 1, (KMAX - 0.5) / NLON / 2, nodes + 2)
    wave = fine[:, nodes]
    at = np.nonzero(wave[:-1] * wave[1:] < 0)[0]
    roots = (at + wave[at] / (wave[at] - wave[at + 1]))[: nodes // 2] / 2 + low
    left = snap(roots)
    for i in range(1, len(left)):
        left[i] = max(left[i], left[i - 1] + 1)
    places = np.concatenate([left, (low + high) - left[::-1]])
    kept = nodes - 4
    index = np.round((places - low) * 2).astype(int)
    return places, fine[::2, :kept] @ np.linalg.pinv(fine[index, :kept])


def near_kernel(distance):
    return 1.0 / (NLON * np.sin(np.pi * distance / NLON))


def two_parts(table):
    high = table.astype(np.float32).astype(ml_dtypes.bfloat16)
    low = (table - high.astype(np.float64)).astype(np.float32).astype(ml_dtypes.bfloat16)
    return high, low


@functools.lru_cache(maxsize=4)
def make_tables(width, segments):
    main = -(-2 * KMAX * width // NLON // LANES) * LANES
    nodes = main + EXTRA
    source, gather = interpolation(0, width - 1, nodes, np.round)
    target, spread = interpolation(-1, width, nodes, lambda r: np.floor(r) + 0.5)
    local = near_kernel(target[:, None] - source[None])
    offsets = [d for d in range(-(segments - 1), segments) if d]
    far = {d: near_kernel(target[:, None] + width * d - source[None]) for d in offsets}

    def leading(kernel, count):
        found = np.linalg.svd(kernel, full_matrices=False)[2][:count]
        peak = np.take_along_axis(found, np.abs(found).argmax(1)[:, None], 1)
        return found * np.sign(peak)

    ahead = range(1, segments)
    basis = {s: leading(far[s], FAR) for s in ahead}
    for s in (1, segments - 1):
        both = leading(far[s], FAR + NEAR)
        basis[s], basis[-s] = both[:FAR], both[FAR:]

    high, low = two_parts(gather.T)
    gather_table = np.concatenate([high, low], 0)
    more = [basis[-1], basis[1 - segments]] + [basis[s] for s in ahead]
    rows = np.concatenate([local] + more, 0)
    rows = np.pad(rows, ((0, -len(rows) % 8), (0, 0)))
    high, low = two_parts(rows)
    local_table = np.concatenate([high, low, high], 1)
    blocks = []
    for d in range(segments):
        pieces = [far[d - (d - s) % segments] @ basis[-s].T for s in (1, segments - 1)]
        for e in range(segments):
            if e == d:
                pieces.append(np.zeros((nodes, FAR)))
            else:
                pieces.append(far[d - e] @ basis[(d - e) % segments].T)
        top = [p for piece in pieces for p in (piece, 0 * piece)]
        low_part = [p for piece in pieces for p in (0 * piece, piece)]
        both = np.concatenate([np.concatenate(top, 1), np.concatenate(low_part, 1)], 0)
        high, low = two_parts(both)
        blocks.append(np.concatenate([high, low, high], 1))
    far_table = np.stack(blocks)
    lanes = -(-(width + 2) // LANES) * LANES
    wide = np.zeros((nodes, lanes))
    wide[:, : width + 1] = spread.T[:, 1:]
    wide[:, lanes - 1] = spread.T[:, 0]
    high, low = two_parts(wide)
    none = np.zeros((LANES - 3 * EXTRA, lanes), high.dtype)
    spread_table = np.concatenate(
        [high[:main], low[:main], high[:main], high[main:], low[main:], high[main:], none], 0
    )
    places = np.stack([2 * source - width, 2 * target - width]).astype(np.float32)
    return gather_table, local_table, far_table, spread_table, places[:, :, None]


def phases(cut, places, device, segments, width):
    full = 4.0 * NLON
    odd = 2.0 * cut - 1.0
    inner = odd * places
    inner = inner - full * jnp.floor(inner * (1.0 / full) + 0.5)
    base = odd * (2.0 * device + 1.0)
    cycle = 4.0 * segments
    base = (base - cycle * jnp.floor(base * (1.0 / cycle))) * float(width)
    total = inner + base
    total = total - full * jnp.floor(total * (1.0 / full) + 0.5)
    quarter = jnp.floor(total * (4.0 / full) + 0.5)
    x = (total - (full / 4.0) * quarter) * (2.0 * math.pi / full)
    y = x * x
    sine = x + x * y * (
        -1.0 / 6 + y * (1.0 / 120 + y * (-1.0 / 5040 + y * (1.0 / 362880)))
    )
    cosine = 1.0 + y * (
        -0.5 + y * (1.0 / 24 + y * (-1.0 / 720 + y * (1.0 / 40320 + y * (-1.0 / 3628800))))
    )
    odd_quarter = jnp.abs(quarter) == 1.0
    turned_c = jnp.where(odd_quarter, -quarter * sine, cosine)
    turned_s = jnp.where(odd_quarter, quarter * cosine, sine)
    flip = jnp.where(jnp.abs(quarter) == 2.0, -1.0, 1.0)
    return turned_c * flip, turned_s * flip


def parts(values):
    high = values.astype(BF)
    return high, (values - high.astype(F32)).astype(BF)


def stacked(values):
    high, low = parts(values)
    return jnp.concatenate([high, high, low], axis=0)


def product(a, b, dims):
    return lax.dot_general(a, b, (dims, ((), ())), preferred_element_type=F32)


def lane_cut(cut_ref):
    cut = cut_ref[...].astype(F32)
    return jnp.concatenate([cut] * (LANES // cut.shape[1]), axis=1)


def packed(values):
    main = values.shape[1] - LANES
    high, low = parts(values)
    last, last_low = high[:, main:].astype(F32), low[:, main:].astype(F32)
    last = last + pltpu.roll(last, EXTRA, 1) + pltpu.roll(last_low, 2 * EXTRA, 1)
    return jnp.concatenate([high[:, :main], low[:, :main], last.astype(BF)], axis=1)


def spread_lines(pack, spread_ref, columns):
    main = (pack.shape[1] - LANES) // 2
    held = jnp.concatenate([pack[:, :main], pack], axis=1)
    return product(held, spread_ref[:, columns], ((1,), (0,)))


def analyse_kernel(
    segments, first, groups, device_ref, cut_ref, places_ref, gather_ref, local_ref,
    u_ref, v_ref, q_ref, near_ref, ahead_ref, behind_ref, every_ref, turn_ref,
    lines_ref, high_ref, low_ref, held_ref, table_ref, sems,
):
    width = u_ref.shape[2]
    steps, levels, rows, _ = lines_ref.shape
    lines = levels * rows
    nodes = gather_ref.shape[0] // 2
    me = device_ref[0]

    copies = []
    for step in range(steps):
        ref = (u_ref, v_ref, q_ref)[step // groups]
        levels_at = pl.ds(first + (step % groups) * levels, levels)
        copies.append(pltpu.make_async_copy(ref.at[levels_at], lines_ref.at[step], sems.at[step]))
        copies[-1].start()
    for side in range(2):
        cosine, sine = phases(
            lane_cut(cut_ref), places_ref[side], me.astype(F32), segments, width
        )
        if side == 0:
            table_ref[0], table_ref[1] = cosine, sine
        else:
            turn_ref[0], turn_ref[1] = cosine, sine
    every_ref[me] = jnp.zeros(every_ref.shape[1:], F32)

    spans = [slice(at, min(at + SPAN, width)) for at in range(0, width, SPAN)]

    def cast(step, span):
        values = lines_ref[step, :, :, span].reshape(lines, span.stop - span.start)
        high, low = parts(values)
        high_ref[step % 2, :, span] = high
        low_ref[step % 2, :, span] = low

    def gather(step, span):
        both = product(gather_ref[:, span], high_ref[step % 2, :, span], ((1,), (1,)))
        rest = product(gather_ref[:nodes, span], low_ref[step % 2, :, span], ((1,), (1,)))
        more = both[:nodes] + both[nodes:] + rest
        if span.start > 0:
            more = more + held_ref[step % 2]
        held_ref[step % 2] = more

    def local(step, part):
        tile = step * (lines // LANES) + part
        mine = held_ref[step % 2, :, part * LANES : (part + 1) * LANES]
        turned = jnp.concatenate([mine * table_ref[0], mine * table_ref[1]], axis=1)
        out = product(local_ref[...], stacked(turned), ((1,), (0,)))
        near_ref[tile] = turn_ref[1] * out[:nodes, :LANES] - turn_ref[0] * out[:nodes, LANES:]
        at = nodes
        for ref in (ahead_ref, behind_ref):
            ref[tile, :NEAR] = out[at : at + NEAR, :LANES]
            ref[tile, NEAR:] = out[at : at + NEAR, LANES:]
            at += NEAR
        for s in range(1, segments):
            to = lax.rem(me + s, segments)
            every_ref[to, tile, :FAR] = out[at : at + FAR, :LANES]
            every_ref[to, tile, FAR:] = out[at : at + FAR, LANES:]
            at += FAR

    copies[0].wait()
    for span in spans:
        cast(0, span)
    for step in range(steps + 1):
        if step + 1 < steps:
            copies[step + 1].wait()
        for number in range(max(len(spans), lines // LANES)):
            if step < steps and number < len(spans):
                gather(step, spans[number])
            if step + 1 < steps and number < len(spans):
                cast(step + 1, spans[number])
            if step > 0 and number < lines // LANES:
                local(step - 1, number)


def combine_kernel(
    per_field, rows, device_ref, scale_ref, turn_ref, table_in, near_ref, behind_ref, ahead_ref,
    every_ref, pack_ref, top_ref, bottom_ref,
):
    step = pl.program_id(0)
    tiles, nodes, _ = near_ref.shape
    segments = every_ref.shape[0]
    columns = []
    for tile in range(tiles):
        pieces = [behind_ref[tile], ahead_ref[tile]]
        pieces += [every_ref[e, tile] for e in range(segments)]
        columns.append(jnp.concatenate(pieces, axis=0))
    got = product(table_in[0], stacked(jnp.concatenate(columns, axis=1)), ((1,), (0,)))
    inverse = 1.0 / scale_ref[...]
    none = jnp.zeros((LANES - EXTRA, LANES), F32)
    for tile in range(tiles):
        at = tile * LANES
        cosine, sine = got[:nodes, at : at + LANES], got[nodes:, at : at + LANES]
        values = near_ref[tile] + turn_ref[1] * cosine - turn_ref[0] * sine
        values = jnp.transpose(jnp.concatenate([values, none], axis=0))
        pack_ref[tile] = packed(values)
        number = step * tiles + tile
        wind = number < 2 * per_field
        top_weight = jnp.where(wind, inverse[:, :1], 1.0)
        bottom_weight = jnp.where(wind, inverse[:, rows - 1 :], 1.0)
        pair = LANES // rows
        for part in range(pair):
            line = number * pair + part
            top_ref[pl.ds(line, 1), :] = values[part * rows : part * rows + 1] * top_weight
            last = part * rows + rows - 1
            bottom_ref[pl.ds(line, 1), :] = values[last : last + 1] * bottom_weight


def finish_kernel(
    first, scale_ref, spread_ref, above_ref, below_ref, pack_ref, tracer_ref, *refs
):
    outs = refs[-9:-6]
    filtered_ref, edge_ref, column_ref, held_ref, load_sems, sems = refs[-6:]
    _, rows, width = tracer_ref.shape
    lanes = spread_ref.shape[1]
    count = above_ref.shape[0]
    levels = count // 3
    pair = LANES // rows
    steps = levels
    per_field = levels // pair
    tracer_slot = 6

    def load(step):
        return pltpu.make_async_copy(
            tracer_ref.at[first + step], held_ref.at[tracer_slot + step % 2], load_sems.at[step % 2]
        )

    def store(step, number):
        return pltpu.make_async_copy(
            held_ref.at[3 * (step % 2) + number], outs[number].at[first + step],
            sems.at[step % 2, number],
        )

    load(0).start()
    edges = jnp.concatenate([above_ref[...], below_ref[...]], axis=0)
    edge_ref[...] = spread_lines(packed(edges), spread_ref, slice(0, lanes))
    here = lax.broadcasted_iota(jnp.int32, (rows, rows), 0)
    there = lax.broadcasted_iota(jnp.int32, (rows, rows), 1)
    column = jnp.where(here == there, jnp.broadcast_to(scale_ref[...], (rows, rows)), 0.0)
    column = jnp.sum(column, axis=1, keepdims=True)
    column_ref[0] = jnp.broadcast_to(column, (rows, LANES))
    column_ref[1] = 1.0 / column_ref[0]
    row_number = lax.broadcasted_iota(jnp.int32, (rows, 1), 0)

    def fill(step, part):
        tile, at = step // pair, step % pair * rows
        pack = jnp.concatenate(
            [pack_ref[f * per_field + tile, at : at + rows] for f in range(3)], axis=0
        )
        columns = slice(part * 2 * LANES, (part + 1) * 2 * LANES)
        filtered_ref[step % 2, :, columns] = spread_lines(pack, spread_ref, columns)

    def east_west(values):
        return pltpu.roll(values, lanes - 1, 1) - pltpu.roll(values, 1, 1)

    def north_south(step, values, number):
        at = number * levels + step
        above = edge_ref[at : at + 1]
        below = edge_ref[count + at : count + at + 1]
        later = jnp.where(row_number == rows - 1, below, pltpu.roll(values, rows - 1, 0))
        earlier = jnp.where(row_number == 0, above, pltpu.roll(values, 1, 0))
        return later - earlier

    def field(step, number):
        return filtered_ref[step % 2, number * rows : (number + 1) * rows]

    def stencil(step, number):
        scale = column_ref[0][:, :1]
        inverse = column_ref[1][:, :1]
        base = 3 * (step % 2)
        if number == 0:
            across = north_south(step, field(step, 1) * inverse, 1)
            value = scale * (east_west(field(step, 0)) + across)
            held_ref[base + 1] = value[:, :width]
        elif number == 1:
            across = north_south(step, field(step, 0) * inverse, 0)
            value = scale * (east_west(field(step, 1)) - across)
            held_ref[base + 2] = value[:, :width]
        else:
            q = field(step, 2)
            change = field(step, 0) * (courant * scale) * east_west(q)
            change = change + (courant * field(step, 1)) * north_south(step, q, 2)
            held_ref[base] = held_ref[tracer_slot + step % 2] - change[:, :width]

    columns = lanes // (2 * LANES)
    for part in range(columns):
        fill(0, part)
    for step in range(steps):
        if step + 1 < steps:
            load(step + 1).start()
        load(step).wait()
        if step >= 2:
            for number in range(3):
                store(step - 2, number).wait()
        for part in range(max(columns, 3)):
            if step + 1 < steps and part < columns:
                fill(step + 1, part)
            if part * 3 % columns < 3 and part * 3 // columns < 3:
                stencil(step, part * 3 // columns)
        for number in range(3):
            store(step, number).start()
    for step in range(max(steps - 2, 0), steps):
        for number in range(3):
            store(step, number).wait()


def whole_spec():
    return pl.BlockSpec(memory_space=pltpu.VMEM)


def on_device(segments, lats, tables, wind_u, wind_v, tracer, cutoff, row_scale):
    levels, rows, width = wind_u.shape
    gather_table, local_table, far_table, spread_table, places = tables
    nodes = gather_table.shape[0] // 2
    lanes = spread_table.shape[1]
    wide = nodes - EXTRA + LANES
    nl = levels // CHUNKS
    pair = LANES // rows
    group = 2 * pair
    groups = nl // group
    tiles = 3 * nl // pair
    per_field = nl // pair
    count = 3 * nl
    device = lax.axis_index("lon").astype(jnp.int32)[None]
    cut = cutoff.reshape(1, rows)
    scale = row_scale.reshape(1, rows)

    smem = pl.BlockSpec(memory_space=pltpu.SMEM)
    anywhere = pl.BlockSpec(memory_space=pl.ANY)
    params = pltpu.CompilerParams(
        dimension_semantics=("arbitrary",), vmem_limit_bytes=VMEM_LIMIT
    )
    flat = pltpu.CompilerParams(vmem_limit_bytes=VMEM_LIMIT)

    def analyse(chunk):
        steps = 3 * groups
        extra = jax.ShapeDtypeStruct((tiles, 2 * NEAR, LANES), F32)
        return pl.pallas_call(
            functools.partial(analyse_kernel, segments, chunk * nl, groups),
            out_shape=(
                jax.ShapeDtypeStruct((tiles, nodes, LANES), F32),
                extra,
                extra,
                jax.ShapeDtypeStruct((segments, tiles, 2 * FAR, LANES), F32),
                jax.ShapeDtypeStruct((2, nodes, LANES), F32),
            ),
            in_specs=[smem] + [whole_spec()] * 4 + [anywhere] * 3,
            out_specs=(whole_spec(),) * 5,
            scratch_shapes=[
                pltpu.VMEM((steps, group, rows, width), F32),
                pltpu.VMEM((2, group * rows, width), BF),
                pltpu.VMEM((2, group * rows, width), BF),
                pltpu.VMEM((2, nodes, group * rows), F32),
                pltpu.VMEM((2, nodes, LANES), F32),
                pltpu.SemaphoreType.DMA((steps,)),
            ],
            compiler_params=flat,
            cost_estimate=pl.CostEstimate(flops=0, bytes_accessed=57600000 // CHUNKS, transcendentals=0),
            name="analyse",
        )(device, cut, places, gather_table, local_table, wind_u, wind_v, tracer)

    def exchange(ahead, behind, every):
        def shifted(array, by):
            return lax.ppermute(
                array, "lon", [(i, (i + by) % segments) for i in range(segments)]
            )

        got = lax.all_to_all(every, "lon", 0, 0)
        return shifted(ahead, 1), shifted(behind, -1), got

    def combine(near, turn, moments):
        step_tiles = 3
        edge = jax.ShapeDtypeStruct((count, wide), F32)
        extra_spec = pl.BlockSpec((step_tiles, 2 * NEAR, LANES), lambda s, d: (s, 0, 0))
        return pl.pallas_call(
            functools.partial(combine_kernel, per_field, rows),
            out_shape=(
                jax.ShapeDtypeStruct((tiles, LANES, 2 * wide - LANES), BF), edge, edge,
            ),
            grid_spec=pltpu.PrefetchScalarGridSpec(
                num_scalar_prefetch=1,
                grid=(tiles // step_tiles,),
                in_specs=[whole_spec()] * 2
                + [pl.BlockSpec((1,) + far_table.shape[1:], lambda s, d: (d[0], 0, 0))]
                + [pl.BlockSpec((step_tiles, nodes, LANES), lambda s, d: (s, 0, 0))]
                + [extra_spec, extra_spec]
                + [
                    pl.BlockSpec(
                        (segments, step_tiles, 2 * FAR, LANES), lambda s, d: (0, s, 0, 0)
                    )
                ],
                out_specs=(
                    pl.BlockSpec((step_tiles, LANES, 2 * wide - LANES), lambda s, d: (s, 0, 0)),
                    pl.BlockSpec((count, wide), lambda s, d: (0, 0)),
                    pl.BlockSpec((count, wide), lambda s, d: (0, 0)),
                ),
            ),
            compiler_params=params,
            cost_estimate=pl.CostEstimate(flops=0, bytes_accessed=21600000 // CHUNKS, transcendentals=0),
            name="combine",
        )(device, scale, turn, far_table, near, *moments)

    def finish(chunk, pack, above, below, before):
        return pl.pallas_call(
            functools.partial(finish_kernel, chunk * nl),
            out_shape=(jax.ShapeDtypeStruct((levels, rows, width), F32),) * 3,
            in_specs=[whole_spec()] * 5 + [anywhere] * (1 + len(before)),
            out_specs=(anywhere,) * 3,
            scratch_shapes=[
                pltpu.VMEM((2, 3 * rows, lanes), F32),
                pltpu.VMEM((2 * count, lanes), F32),
                pltpu.VMEM((2, rows, LANES), F32),
                pltpu.VMEM((8, rows, width), F32),
                pltpu.SemaphoreType.DMA((2,)),
                pltpu.SemaphoreType.DMA((2, 3)),
            ],
            input_output_aliases={6 + i: i for i in range(len(before))},
            compiler_params=flat,
            cost_estimate=pl.CostEstimate(flops=0, bytes_accessed=43200000 // CHUNKS, transcendentals=0),
            name="finish",
        )(scale, spread_table, above, below, pack, tracer, *before)

    analysed = [analyse(chunk) for chunk in range(CHUNKS)]
    moments = [exchange(*got[1:4]) for got in analysed]
    edges, packs = [], []
    for got, moment in zip(analysed, moments):
        pack, top, bottom = combine(got[0], got[4], moment)
        above = lax.ppermute(bottom, "lat", [(i, i + 1) for i in range(lats - 1)])
        below = lax.ppermute(top, "lat", [(i + 1, i) for i in range(lats - 1)])
        packs.append(pack)
        edges.append((above, below))
    out = ()
    for chunk in range(CHUNKS):
        out = finish(chunk, packs[chunk], *edges[chunk], out)
    return out


def solution(mesh):
    segments, lats = mesh.shape["lon"], mesh.shape["lat"]
    tables = tuple(make_tables(NLON // segments, segments))
    line = P(None, "lat", "lon")
    return jax.shard_map(
        functools.partial(on_device, segments, lats, tables),
        mesh=mesh,
        in_specs=(line, line, line, P("lat"), P("lat")),
        out_specs=(line, line, line),
        check_vma=False,
    )
```

```python
import functools
import math

import jax
import jax.numpy as jnp
import ml_dtypes
import numpy as np
from jax import lax
from jax.experimental import pallas as pl
from jax.experimental.pallas import tpu as pltpu
from jax.sharding import PartitionSpec as P

NLON = 12000
KMAX = 1024
NEAR = 12
FAR = 4
EXTRA = 32
LANES = 128
courant = 0.5
BF = jnp.bfloat16
F32 = jnp.float32
VMEM_LIMIT = 56 * 1024 * 1024


def prolate(points, band, count):
    i = np.arange(points)
    diag = ((points - 1 - 2 * i) / 2.0) ** 2 * np.cos(2 * np.pi * band)
    off = i[1:] * (points - i[1:]) / 2.0
    mid = points // 2
    half = (count + 1) // 2
    out = np.zeros((points, 2 * half))
    dd, ee = diag[mid:], off[mid:].copy()
    scaled = ee.copy()
    scaled[0] *= math.sqrt(2.0)
    even = np.linalg.eigh(np.diag(dd) + np.diag(scaled, 1) + np.diag(scaled, -1))[1]
    even = even[:, ::-1][:, :half]
    wing = even[1:] / math.sqrt(2.0)
    out[mid, 0::2] = even[0]
    out[mid + 1 :, 0::2] = wing
    out[:mid, 0::2] = wing[::-1]
    odd = np.linalg.eigh(np.diag(dd[1:]) + np.diag(ee[1:], 1) + np.diag(ee[1:], -1))[1]
    wing = odd[:, ::-1][:, :half] / math.sqrt(2.0)
    out[mid + 1 :, 1::2] = wing
    out[:mid, 1::2] = -wing[::-1]
    return out


def interpolation(low, high, nodes, snap):
    fine = prolate(2 * (high - low) + 1, (KMAX - 0.5) / NLON / 2, nodes + 2)
    wave = fine[:, nodes]
    at = np.nonzero(wave[:-1] * wave[1:] < 0)[0]
    roots = (at + wave[at] / (wave[at] - wave[at + 1]))[: nodes // 2] / 2 + low
    left = snap(roots)
    for i in range(1, len(left)):
        left[i] = max(left[i], left[i - 1] + 1)
    places = np.concatenate([left, (low + high) - left[::-1]])
    kept = nodes - 4
    index = np.round((places - low) * 2).astype(int)
    return places, fine[::2, :kept] @ np.linalg.pinv(fine[index, :kept])


def near_kernel(distance):
    return 1.0 / (NLON * np.sin(np.pi * distance / NLON))


def two_parts(table):
    high = table.astype(np.float32).astype(ml_dtypes.bfloat16)
    low = (table - high.astype(np.float64)).astype(np.float32).astype(ml_dtypes.bfloat16)
    return high, low


@functools.lru_cache(maxsize=4)
def make_tables(width, segments):
    main = -(-2 * KMAX * width // NLON // LANES) * LANES
    nodes = main + EXTRA
    source, gather = interpolation(0, width - 1, nodes, np.round)
    target, spread = interpolation(-1, width, nodes, lambda r: np.floor(r) + 0.5)
    local = near_kernel(target[:, None] - source[None])
    offsets = [d for d in range(-(segments - 1), segments) if d]
    far = {d: near_kernel(target[:, None] + width * d - source[None]) for d in offsets}

    def leading(kernel, count):
        found = np.linalg.svd(kernel, full_matrices=False)[2][:count]
        peak = np.take_along_axis(found, np.abs(found).argmax(1)[:, None], 1)
        return found * np.sign(peak)

    ahead = range(1, segments)
    basis = {s: leading(far[s], FAR) for s in ahead}
    for s in (1, segments - 1):
        both = leading(far[s], FAR + NEAR)
        basis[s], basis[-s] = both[:FAR], both[FAR:]

    high, low = two_parts(gather.T)
    gather_table = np.concatenate([high, low], 0)
    more = [basis[-1], basis[1 - segments]] + [basis[s] for s in ahead]
    rows = np.concatenate(more, 0)
    rows = np.pad(rows, ((0, -len(rows) % 8), (0, 0)))
    high, low = two_parts(rows)
    moment_table = np.concatenate([high, low, high], 1)
    high, low = two_parts(local)
    local_table = np.concatenate([high, low, high], 1)
    blocks = []
    for d in range(segments):
        pieces = [far[d - (d - s) % segments] @ basis[-s].T for s in (1, segments - 1)]
        for e in range(segments):
            if e == d:
                pieces.append(np.zeros((nodes, FAR)))
            else:
                pieces.append(far[d - e] @ basis[(d - e) % segments].T)
        pieces = [np.pad(piece, ((0, main + LANES - nodes), (0, 0))).T for piece in pieces]
        left = [p for piece in pieces for p in (piece, 0 * piece)]
        right = [p for piece in pieces for p in (0 * piece, piece)]
        both = np.concatenate([np.concatenate(left, 0), np.concatenate(right, 0)], 1)
        high, low = two_parts(both)
        blocks.append(np.concatenate([high, low, high], 0))
    far_table = np.stack(blocks)
    lanes = -(-(width + 2) // LANES) * LANES
    wide = np.zeros((nodes, lanes))
    wide[:, : width + 1] = spread.T[:, 1:]
    wide[:, lanes - 1] = spread.T[:, 0]
    high, low = two_parts(wide)
    none = np.zeros((LANES - 3 * EXTRA, lanes), high.dtype)
    spread_table = np.concatenate(
        [high[:main], low[:main], high[:main], high[main:], low[main:], high[main:], none], 0
    )
    places = np.stack([2 * source - width, 2 * target - width]).astype(np.float32)
    return gather_table, moment_table, local_table, far_table, spread_table, places[:, :, None]


def phases(cut, places, device, segments, width):
    full = 4.0 * NLON
    odd = 2.0 * cut - 1.0
    inner = odd * places
    inner = inner - full * jnp.floor(inner * (1.0 / full) + 0.5)
    base = odd * (2.0 * device + 1.0)
    cycle = 4.0 * segments
    base = (base - cycle * jnp.floor(base * (1.0 / cycle))) * float(width)
    total = inner + base
    total = total - full * jnp.floor(total * (1.0 / full) + 0.5)
    quarter = jnp.floor(total * (4.0 / full) + 0.5)
    x = (total - (full / 4.0) * quarter) * (2.0 * math.pi / full)
    y = x * x
    sine = x + x * y * (
        -1.0 / 6 + y * (1.0 / 120 + y * (-1.0 / 5040 + y * (1.0 / 362880)))
    )
    cosine = 1.0 + y * (
        -0.5 + y * (1.0 / 24 + y * (-1.0 / 720 + y * (1.0 / 40320 + y * (-1.0 / 3628800))))
    )
    odd_quarter = jnp.abs(quarter) == 1.0
    turned_c = jnp.where(odd_quarter, -quarter * sine, cosine)
    turned_s = jnp.where(odd_quarter, quarter * cosine, sine)
    flip = jnp.where(jnp.abs(quarter) == 2.0, -1.0, 1.0)
    return turned_c * flip, turned_s * flip


def parts(values):
    high = values.astype(BF)
    return high, (values - high.astype(F32)).astype(BF)


def stacked(values):
    high, low = parts(values)
    return jnp.concatenate([high, high, low], axis=0)


def product(a, b, dims):
    return lax.dot_general(a, b, (dims, ((), ())), preferred_element_type=F32)


def lane_cut(cut_ref):
    cut = cut_ref[...].astype(F32)
    return jnp.concatenate([cut] * (LANES // cut.shape[1]), axis=1)


def packed(values):
    main = values.shape[1] - LANES
    high, low = parts(values)
    last, last_low = high[:, main:].astype(F32), low[:, main:].astype(F32)
    last = last + pltpu.roll(last, EXTRA, 1) + pltpu.roll(last_low, 2 * EXTRA, 1)
    return jnp.concatenate([high[:, :main], low[:, :main], last.astype(BF)], axis=1)


def spread_lines(pack, spread_ref):
    main = (pack.shape[1] - LANES) // 2
    held = jnp.concatenate([pack[:, :main], pack], axis=1)
    return product(held, spread_ref[...], ((1,), (0,)))


def analyse_kernel(
    segments, groups, device_ref, cut_ref, places_ref, gather_ref, moment_ref,
    u_ref, v_ref, q_ref, node_ref, ahead_ref, behind_ref, every_ref, table_ref,
    lines_ref, high_ref, low_ref, sems,
):
    width = u_ref.shape[2]
    steps, levels, rows, _ = lines_ref.shape
    lines = levels * rows
    nodes = gather_ref.shape[0] // 2
    me = device_ref[0]

    copies = []
    for step in range(steps):
        ref = (u_ref, v_ref, q_ref)[step // groups]
        levels_at = pl.ds((step % groups) * levels, levels)
        copies.append(pltpu.make_async_copy(ref.at[levels_at], lines_ref.at[step], sems.at[step]))
        copies[-1].start()
    for side in range(2):
        cosine, sine = phases(
            lane_cut(cut_ref), places_ref[side], me.astype(F32), segments, width
        )
        table_ref[2 * side], table_ref[2 * side + 1] = cosine, sine
    every_ref[me] = jnp.zeros(every_ref.shape[1:], F32)

    def cast(step):
        values = lines_ref[step].reshape(lines, width)
        high, low = parts(values)
        high_ref[step % 2] = high
        low_ref[step % 2] = low

    def gather(step):
        both = product(gather_ref[...], high_ref[step % 2], ((1,), (1,)))
        rest = product(gather_ref[:nodes], low_ref[step % 2], ((1,), (1,)))
        held = both[:nodes] + both[nodes:] + rest
        for part in range(lines // LANES):
            node_ref[step * (lines // LANES) + part] = held[:, part * LANES : (part + 1) * LANES]

    def moments(step):
        for part in range(lines // LANES):
            tile = step * (lines // LANES) + part
            mine = node_ref[tile]
            turned = jnp.concatenate([mine * table_ref[0], mine * table_ref[1]], axis=1)
            out = product(moment_ref[...], stacked(turned), ((1,), (0,)))
            at = 0
            for ref in (ahead_ref, behind_ref):
                ref[tile, :NEAR] = out[at : at + NEAR, :LANES]
                ref[tile, NEAR:] = out[at : at + NEAR, LANES:]
                at += NEAR
            for s in range(1, segments):
                to = lax.rem(me + s, segments)
                every_ref[to, tile, :FAR] = out[at : at + FAR, :LANES]
                every_ref[to, tile, FAR:] = out[at : at + FAR, LANES:]
                at += FAR

    copies[0].wait()
    cast(0)
    for step in range(steps):
        if step + 1 < steps:
            copies[step + 1].wait()
        gather(step)
        if step + 1 < steps:
            cast(step + 1)
        if step > 0:
            moments(step - 1)
    moments(steps - 1)


def turned_over(values):
    none = jnp.zeros((LANES - EXTRA, LANES), F32)
    return jnp.transpose(jnp.concatenate([values, none], axis=0))


def near_kernel_call(local_ref, table_ref, node_ref, near_ref, turn_ref):
    tiles, nodes, _ = node_ref.shape

    @pl.when(pl.program_id(0) == 0)
    def _():
        turn_ref[0] = turned_over(table_ref[2])
        turn_ref[1] = turned_over(table_ref[3])

    columns = []
    for tile in range(tiles):
        columns += [node_ref[tile] * table_ref[0], node_ref[tile] * table_ref[1]]
    out = product(local_ref[...], stacked(jnp.concatenate(columns, axis=1)), ((1,), (0,)))
    for tile in range(tiles):
        at = 2 * tile * LANES
        cosine, sine = out[:, at : at + LANES], out[:, at + LANES : at + 2 * LANES]
        near_ref[tile] = turned_over(table_ref[3] * cosine - table_ref[2] * sine)


def combine_kernel(
    per_field, rows, device_ref, scale_ref, turn_ref, far_ref, near_ref, behind_ref, ahead_ref,
    every_ref, pack_ref, top_ref, bottom_ref,
):
    step = pl.program_id(0)
    tiles, _, wide = near_ref.shape
    segments = every_ref.shape[0]
    columns = []
    for tile in range(tiles):
        pieces = [behind_ref[tile], ahead_ref[tile]]
        pieces += [every_ref[e, tile] for e in range(segments)]
        columns.append(jnp.concatenate(pieces, axis=0))
    got = product(stacked(jnp.concatenate(columns, axis=1)), far_ref[0], ((0,), (0,)))
    inverse = 1.0 / scale_ref[...]
    for tile in range(tiles):
        mine = got[tile * LANES : (tile + 1) * LANES]
        values = near_ref[tile] + turn_ref[1] * mine[:, :wide] - turn_ref[0] * mine[:, wide:]
        pack_ref[tile] = packed(values)
        number = step * tiles + tile
        wind = number < 2 * per_field
        top_weight = jnp.where(wind, inverse[:, :1], 1.0)
        bottom_weight = jnp.where(wind, inverse[:, rows - 1 :], 1.0)
        pair = LANES // rows
        for part in range(pair):
            line = number * pair + part
            top_ref[pl.ds(line, 1), :] = values[part * rows : part * rows + 1] * top_weight
            last = part * rows + rows - 1
            bottom_ref[pl.ds(line, 1), :] = values[last : last + 1] * bottom_weight


def finish_kernel(
    scale_ref, spread_ref, above_ref, below_ref, pack_ref, tracer_ref, *refs
):
    outs = refs[:3]
    filtered_ref, edge_ref, column_ref, held_ref, load_sems, sems = refs[3:]
    levels, rows, width = tracer_ref.shape
    lanes = spread_ref.shape[1]
    count = above_ref.shape[0]
    tracer_slot = 6

    def load(step):
        return pltpu.make_async_copy(
            tracer_ref.at[step], held_ref.at[tracer_slot + step % 2], load_sems.at[step % 2]
        )

    def store(step, number):
        return pltpu.make_async_copy(
            held_ref.at[3 * (step % 2) + number], outs[number].at[step], sems.at[step % 2, number]
        )

    load(0).start()
    pack = pack_ref[...].reshape(filtered_ref.shape[0], pack_ref.shape[2])
    filtered_ref[...] = spread_lines(pack, spread_ref)
    edges = jnp.concatenate([above_ref[...], below_ref[...]], axis=0)
    edge_ref[...] = spread_lines(packed(edges), spread_ref)
    here = lax.broadcasted_iota(jnp.int32, (rows, rows), 0)
    there = lax.broadcasted_iota(jnp.int32, (rows, rows), 1)
    column = jnp.where(here == there, jnp.broadcast_to(scale_ref[...], (rows, rows)), 0.0)
    column = jnp.sum(column, axis=1, keepdims=True)
    column_ref[0] = jnp.broadcast_to(column, (rows, LANES))
    column_ref[1] = 1.0 / column_ref[0]
    row_number = lax.broadcasted_iota(jnp.int32, (rows, 1), 0)

    def east_west(values):
        return pltpu.roll(values, lanes - 1, 1) - pltpu.roll(values, 1, 1)

    def stencil(level):
        scale = column_ref[0][:, :1]
        inverse = column_ref[1][:, :1]

        def field(number):
            at = (number * levels + level) * rows
            return filtered_ref[at : at + rows]

        def north_south(values, number):
            at = number * levels + level
            above = edge_ref[at : at + 1]
            below = edge_ref[count + at : count + at + 1]
            later = jnp.where(row_number == rows - 1, below, pltpu.roll(values, rows - 1, 0))
            earlier = jnp.where(row_number == 0, above, pltpu.roll(values, 1, 0))
            return later - earlier

        u, v, q = field(0), field(1), field(2)
        div = scale * (east_west(u) + north_south(v * inverse, 1))
        vort = scale * (east_west(v) - north_south(u * inverse, 0))
        change = u * (courant * scale) * east_west(q) + (courant * v) * north_south(q, 2)
        base = 3 * (level % 2)
        held_ref[base] = held_ref[tracer_slot + level % 2] - change[:, :width]
        held_ref[base + 1] = div[:, :width]
        held_ref[base + 2] = vort[:, :width]

    for level in range(levels):
        if level + 1 < levels:
            load(level + 1).start()
        load(level).wait()
        if level >= 2:
            for number in range(3):
                store(level - 2, number).wait()
        stencil(level)
        for number in range(3):
            store(level, number).start()
    for level in range(max(levels - 2, 0), levels):
        for number in range(3):
            store(level, number).wait()


def whole_spec():
    return pl.BlockSpec(memory_space=pltpu.VMEM)


def on_device(segments, lats, tables, wind_u, wind_v, tracer, cutoff, row_scale):
    levels, rows, width = wind_u.shape
    gather_table, moment_table, local_table, far_table, spread_table, places = tables
    nodes = gather_table.shape[0] // 2
    lanes = spread_table.shape[1]
    wide = nodes - EXTRA + LANES
    pair = LANES // rows
    group = 2 * pair
    groups = levels // group
    per_field = levels // pair
    tiles = 3 * per_field
    count = 3 * levels
    device = lax.axis_index("lon").astype(jnp.int32)[None]
    cut = cutoff.reshape(1, rows)
    scale = row_scale.reshape(1, rows)

    smem = pl.BlockSpec(memory_space=pltpu.SMEM)
    anywhere = pl.BlockSpec(memory_space=pl.ANY)
    params = pltpu.CompilerParams(
        dimension_semantics=("arbitrary",), vmem_limit_bytes=VMEM_LIMIT
    )
    flat = pltpu.CompilerParams(vmem_limit_bytes=VMEM_LIMIT)

    def cost(us):
        return pl.CostEstimate(flops=0, bytes_accessed=us * 3600000, transcendentals=0)

    steps = 3 * groups
    extra = jax.ShapeDtypeStruct((tiles, 2 * NEAR, LANES), F32)
    values, ahead, behind, every, table = pl.pallas_call(
        functools.partial(analyse_kernel, segments, groups),
        out_shape=(
            jax.ShapeDtypeStruct((tiles, nodes, LANES), F32),
            extra,
            extra,
            jax.ShapeDtypeStruct((segments, tiles, 2 * FAR, LANES), F32),
            jax.ShapeDtypeStruct((4, nodes, LANES), F32),
        ),
        in_specs=[smem] + [whole_spec()] * 4 + [anywhere] * 3,
        out_specs=(whole_spec(),) * 5,
        scratch_shapes=[
            pltpu.VMEM((steps, group, rows, width), F32),
            pltpu.VMEM((2, group * rows, width), BF),
            pltpu.VMEM((2, group * rows, width), BF),
            pltpu.SemaphoreType.DMA((steps,)),
        ],
        compiler_params=flat,
        cost_estimate=cost(12),
        name="analyse",
    )(device, cut, places, gather_table, moment_table, wind_u, wind_v, tracer)

    def shifted(array, by):
        return lax.ppermute(array, "lon", [(i, (i + by) % segments) for i in range(segments)])

    every = lax.all_to_all(every, "lon", 0, 0)
    ahead, behind = shifted(ahead, 1), shifted(behind, -1)

    step_tiles = 4
    near, turn = pl.pallas_call(
        near_kernel_call,
        out_shape=(
            jax.ShapeDtypeStruct((tiles, LANES, wide), F32),
            jax.ShapeDtypeStruct((2, LANES, wide), F32),
        ),
        grid=(tiles // step_tiles,),
        in_specs=[whole_spec()] * 2
        + [pl.BlockSpec((step_tiles, nodes, LANES), lambda s: (s, 0, 0))],
        out_specs=(
            pl.BlockSpec((step_tiles, LANES, wide), lambda s: (s, 0, 0)),
            pl.BlockSpec((2, LANES, wide), lambda s: (0, 0, 0)),
        ),
        compiler_params=params,
        cost_estimate=cost(6),
        name="near",
    )(local_table, table, values)

    edge = jax.ShapeDtypeStruct((count, wide), F32)
    extra_spec = pl.BlockSpec((step_tiles, 2 * NEAR, LANES), lambda s, d: (s, 0, 0))
    pack, top, bottom = pl.pallas_call(
        functools.partial(combine_kernel, per_field, rows),
        out_shape=(jax.ShapeDtypeStruct((tiles, LANES, 2 * wide - LANES), BF), edge, edge),
        grid_spec=pltpu.PrefetchScalarGridSpec(
            num_scalar_prefetch=1,
            grid=(tiles // step_tiles,),
            in_specs=[whole_spec()] * 2
            + [pl.BlockSpec((1,) + far_table.shape[1:], lambda s, d: (d[0], 0, 0))]
            + [pl.BlockSpec((step_tiles, LANES, wide), lambda s, d: (s, 0, 0))]
            + [extra_spec, extra_spec]
            + [pl.BlockSpec((segments, step_tiles, 2 * FAR, LANES), lambda s, d: (0, s, 0, 0))],
            out_specs=(
                pl.BlockSpec((step_tiles, LANES, 2 * wide - LANES), lambda s, d: (s, 0, 0)),
                pl.BlockSpec((count, wide), lambda s, d: (0, 0)),
                pl.BlockSpec((count, wide), lambda s, d: (0, 0)),
            ),
        ),
        compiler_params=params,
        cost_estimate=cost(4),
        name="combine",
    )(device, scale, turn, far_table, near, ahead, behind, every)

    above = lax.ppermute(bottom, "lat", [(i, i + 1) for i in range(lats - 1)])
    below = lax.ppermute(top, "lat", [(i + 1, i) for i in range(lats - 1)])

    return pl.pallas_call(
        finish_kernel,
        out_shape=(jax.ShapeDtypeStruct((levels, rows, width), F32),) * 3,
        in_specs=[whole_spec()] * 5 + [anywhere],
        out_specs=(anywhere,) * 3,
        scratch_shapes=[
            pltpu.VMEM((tiles * LANES, lanes), F32),
            pltpu.VMEM((2 * count, lanes), F32),
            pltpu.VMEM((2, rows, LANES), F32),
            pltpu.VMEM((8, rows, width), F32),
            pltpu.SemaphoreType.DMA((2,)),
            pltpu.SemaphoreType.DMA((2, 3)),
        ],
        compiler_params=flat,
        cost_estimate=cost(12),
        name="finish",
    )(scale, spread_table, above, below, pack, tracer)


def solution(mesh):
    segments, lats = mesh.shape["lon"], mesh.shape["lat"]
    tables = tuple(make_tables(NLON // segments, segments))
    line = P(None, "lat", "lon")
    return jax.shard_map(
        functools.partial(on_device, segments, lats, tables),
        mesh=mesh,
        in_specs=(line, line, line, P("lat"), P("lat")),
        out_specs=(line, line, line),
        check_vma=False,
    )
```

```python
import functools
import math

import jax
import jax.numpy as jnp
import ml_dtypes
import numpy as np
from jax import lax
from jax.experimental import pallas as pl
from jax.experimental.pallas import tpu as pltpu
from jax.sharding import PartitionSpec as P

NLON = 12000
KMAX = 1024
NEAR = 12
FAR = 4
EXTRA = 32
LANES = 128
GROUP = 4
courant = 0.5
BF = jnp.bfloat16
F32 = jnp.float32


def prolate(points, band, count):
    i = np.arange(points)
    diag = ((points - 1 - 2 * i) / 2.0) ** 2 * np.cos(2 * np.pi * band)
    off = i[1:] * (points - i[1:]) / 2.0
    mid = points // 2
    half = (count + 1) // 2
    out = np.zeros((points, 2 * half))
    dd, ee = diag[mid:], off[mid:].copy()
    scaled = ee.copy()
    scaled[0] *= math.sqrt(2.0)
    even = np.linalg.eigh(np.diag(dd) + np.diag(scaled, 1) + np.diag(scaled, -1))[1]
    even = even[:, ::-1][:, :half]
    wing = even[1:] / math.sqrt(2.0)
    out[mid, 0::2] = even[0]
    out[mid + 1 :, 0::2] = wing
    out[:mid, 0::2] = wing[::-1]
    odd = np.linalg.eigh(np.diag(dd[1:]) + np.diag(ee[1:], 1) + np.diag(ee[1:], -1))[1]
    wing = odd[:, ::-1][:, :half] / math.sqrt(2.0)
    out[mid + 1 :, 1::2] = wing
    out[:mid, 1::2] = -wing[::-1]
    return out


def interpolation(low, high, nodes, snap):
    fine = prolate(2 * (high - low) + 1, (KMAX - 0.5) / NLON / 2, nodes + 2)
    wave = fine[:, nodes]
    at = np.nonzero(wave[:-1] * wave[1:] < 0)[0]
    roots = (at + wave[at] / (wave[at] - wave[at + 1]))[: nodes // 2] / 2 + low
    left = snap(roots)
    for i in range(1, len(left)):
        left[i] = max(left[i], left[i - 1] + 1)
    places = np.concatenate([left, (low + high) - left[::-1]])
    kept = nodes - 4
    index = np.round((places - low) * 2).astype(int)
    return places, fine[::2, :kept] @ np.linalg.pinv(fine[index, :kept])


def near_kernel(distance):
    return 1.0 / (NLON * np.sin(np.pi * distance / NLON))


def two_parts(table):
    high = table.astype(np.float32).astype(ml_dtypes.bfloat16)
    low = (table - high.astype(np.float64)).astype(np.float32).astype(ml_dtypes.bfloat16)
    return high, low


@functools.lru_cache(maxsize=4)
def make_tables(width, segments):
    main = -(-2 * KMAX * width // NLON // LANES) * LANES
    nodes = main + EXTRA
    source, gather = interpolation(0, width - 1, nodes, np.round)
    target, spread = interpolation(-1, width, nodes, lambda r: np.floor(r) + 0.5)
    local = near_kernel(target[:, None] - source[None])
    offsets = [d for d in range(-(segments - 1), segments) if d]
    far = {d: near_kernel(target[:, None] + width * d - source[None]) for d in offsets}

    def leading(kernel, count):
        found = np.linalg.svd(kernel, full_matrices=False)[2][:count]
        peak = np.take_along_axis(found, np.abs(found).argmax(1)[:, None], 1)
        return found * np.sign(peak)

    ahead = range(1, segments)
    basis = {s: leading(far[s], FAR) for s in ahead}
    for s in (1, segments - 1):
        both = leading(far[s], FAR + NEAR)
        basis[s], basis[-s] = both[:FAR], both[FAR:]

    high, low = two_parts(gather.T)
    gather_table = np.concatenate([high, low], 0)
    more = [basis[-1], basis[1 - segments]] + [basis[s] for s in ahead]
    rows = np.concatenate(more, 0)
    rows = np.pad(rows, ((0, -len(rows) % 8), (0, 0)))
    high, low = two_parts(rows)
    moment_table = np.concatenate([high, low, high], 1)
    high, low = two_parts(local)
    local_table = np.concatenate([high, low, high], 1)
    blocks = []
    for d in range(segments):
        pieces = [far[d - (d - s) % segments] @ basis[-s].T for s in (1, segments - 1)]
        for e in range(segments):
            if e == d:
                pieces.append(np.zeros((nodes, FAR)))
            else:
                pieces.append(far[d - e] @ basis[(d - e) % segments].T)
        pieces = [np.pad(piece, ((0, main + LANES - nodes), (0, 0))).T for piece in pieces]
        left = [p for piece in pieces for p in (piece, 0 * piece)]
        right = [p for piece in pieces for p in (0 * piece, piece)]
        both = np.concatenate([np.concatenate(left, 0), np.concatenate(right, 0)], 1)
        high, low = two_parts(both)
        blocks.append(np.concatenate([high, low, high], 0))
    far_table = np.stack(blocks)
    lanes = -(-(width + 2) // LANES) * LANES
    wide = np.zeros((nodes, lanes))
    wide[:, : width + 1] = spread.T[:, 1:]
    wide[:, lanes - 1] = spread.T[:, 0]
    high, low = two_parts(wide)
    none = np.zeros((LANES - 3 * EXTRA, lanes), high.dtype)
    spread_table = np.concatenate(
        [high[:main], low[:main], high[:main], high[main:], low[main:], high[main:], none], 0
    )
    places = np.stack([2 * source - width, 2 * target - width]).astype(np.float32)
    return gather_table, moment_table, local_table, far_table, spread_table, places[:, :, None]


def phases(cut, places, device, segments, width):
    full = 4.0 * NLON
    odd = 2.0 * cut - 1.0
    inner = odd * places
    inner = inner - full * jnp.floor(inner * (1.0 / full) + 0.5)
    base = odd * (2.0 * device + 1.0)
    cycle = 4.0 * segments
    base = (base - cycle * jnp.floor(base * (1.0 / cycle))) * float(width)
    total = inner + base
    total = total - full * jnp.floor(total * (1.0 / full) + 0.5)
    quarter = jnp.floor(total * (4.0 / full) + 0.5)
    x = (total - (full / 4.0) * quarter) * (2.0 * math.pi / full)
    y = x * x
    sine = x + x * y * (
        -1.0 / 6 + y * (1.0 / 120 + y * (-1.0 / 5040 + y * (1.0 / 362880)))
    )
    cosine = 1.0 + y * (
        -0.5 + y * (1.0 / 24 + y * (-1.0 / 720 + y * (1.0 / 40320 + y * (-1.0 / 3628800))))
    )
    odd_quarter = jnp.abs(quarter) == 1.0
    turned_c = jnp.where(odd_quarter, -quarter * sine, cosine)
    turned_s = jnp.where(odd_quarter, quarter * cosine, sine)
    flip = jnp.where(jnp.abs(quarter) == 2.0, -1.0, 1.0)
    return turned_c * flip, turned_s * flip


def parts(values):
    high = values.astype(BF)
    return high, (values - high.astype(F32)).astype(BF)


def stacked(values):
    high, low = parts(values)
    return jnp.concatenate([high, high, low], axis=0)


def product(a, b, dims):
    return lax.dot_general(a, b, (dims, ((), ())), preferred_element_type=F32)


def lane_cut(cut_ref):
    cut = cut_ref[...].astype(F32)
    return jnp.concatenate([cut] * (LANES // cut.shape[1]), axis=1)


def packed(values):
    main = values.shape[1] - LANES
    high, low = parts(values)
    last, last_low = high[:, main:].astype(F32), low[:, main:].astype(F32)
    last = last + pltpu.roll(last, EXTRA, 1) + pltpu.roll(last_low, 2 * EXTRA, 1)
    return jnp.concatenate([high[:, :main], low[:, :main], last.astype(BF)], axis=1)


def spread_lines(pack, spread_ref):
    main = (pack.shape[1] - LANES) // 2
    held = jnp.concatenate([pack[:, :main], pack], axis=1)
    return product(held, spread_ref[...], ((1,), (0,)))


def analyse_kernel(
    segments, groups, device_ref, cut_ref, places_ref, gather_ref, moment_ref,
    u_ref, v_ref, q_ref, node_ref, ahead_ref, behind_ref, every_ref, table_ref,
    lines_ref, high_ref, low_ref, sems,
):
    width = u_ref.shape[2]
    steps, levels, rows, _ = lines_ref.shape
    lines = levels * rows
    nodes = gather_ref.shape[0] // 2
    me = device_ref[0]

    copies = []
    for step in range(steps):
        ref = (u_ref, v_ref, q_ref)[step // groups]
        levels_at = pl.ds((step % groups) * levels, levels)
        copies.append(pltpu.make_async_copy(ref.at[levels_at], lines_ref.at[step], sems.at[step]))
        copies[-1].start()
    for side in range(2):
        cosine, sine = phases(
            lane_cut(cut_ref), places_ref[side], me.astype(F32), segments, width
        )
        table_ref[2 * side], table_ref[2 * side + 1] = cosine, sine
    every_ref[me] = jnp.zeros(every_ref.shape[1:], F32)

    def cast(step):
        values = lines_ref[step].reshape(lines, width)
        high, low = parts(values)
        high_ref[step % 2] = high
        low_ref[step % 2] = low

    def gather(step):
        both = product(gather_ref[...], high_ref[step % 2], ((1,), (1,)))
        rest = product(gather_ref[:nodes], low_ref[step % 2], ((1,), (1,)))
        held = both[:nodes] + both[nodes:] + rest
        for part in range(lines // LANES):
            node_ref[step * (lines // LANES) + part] = held[:, part * LANES : (part + 1) * LANES]

    def moments(step):
        for part in range(lines // LANES):
            tile = step * (lines // LANES) + part
            mine = node_ref[tile]
            turned = jnp.concatenate([mine * table_ref[0], mine * table_ref[1]], axis=1)
            out = product(moment_ref[...], stacked(turned), ((1,), (0,)))
            at = 0
            for ref in (ahead_ref, behind_ref):
                ref[tile, :NEAR] = out[at : at + NEAR, :LANES]
                ref[tile, NEAR:] = out[at : at + NEAR, LANES:]
                at += NEAR
            for s in range(1, segments):
                to = lax.rem(me + s, segments)
                every_ref[to, tile, :FAR] = out[at : at + FAR, :LANES]
                every_ref[to, tile, FAR:] = out[at : at + FAR, LANES:]
                at += FAR

    copies[0].wait()
    cast(0)
    for step in range(steps):
        if step + 1 < steps:
            copies[step + 1].wait()
        gather(step)
        if step + 1 < steps:
            cast(step + 1)
        if step > 0:
            moments(step - 1)
    moments(steps - 1)


def turned_over(values):
    none = jnp.zeros((LANES - EXTRA, LANES), F32)
    return jnp.transpose(jnp.concatenate([values, none], axis=0))


def near_kernel_call(local_ref, table_ref, node_ref, near_ref, turn_ref):
    turn_ref[0] = turned_over(table_ref[2])
    turn_ref[1] = turned_over(table_ref[3])
    for start in range(0, node_ref.shape[0], GROUP):
        columns = []
        for tile in range(start, start + GROUP):
            columns += [node_ref[tile] * table_ref[0], node_ref[tile] * table_ref[1]]
        out = product(local_ref[...], stacked(jnp.concatenate(columns, axis=1)), ((1,), (0,)))
        for tile in range(GROUP):
            at = 2 * tile * LANES
            cosine, sine = out[:, at : at + LANES], out[:, at + LANES : at + 2 * LANES]
            near_ref[start + tile] = turned_over(table_ref[3] * cosine - table_ref[2] * sine)


def combine_kernel(
    per_field, rows, device_ref, scale_ref, turn_ref, far_ref, near_ref, before_ref, after_ref,
    every_ref, pack_ref, top_ref, bottom_ref,
):
    tiles, _, wide = near_ref.shape
    segments = every_ref.shape[0]
    inverse = 1.0 / scale_ref[...]
    pair = LANES // rows
    for start in range(0, tiles, GROUP):
        columns = []
        for tile in range(start, start + GROUP):
            pieces = [before_ref[tile], after_ref[tile]]
            pieces += [every_ref[e, tile] for e in range(segments)]
            columns.append(jnp.concatenate(pieces, axis=0))
        got = product(stacked(jnp.concatenate(columns, axis=1)), far_ref[0], ((0,), (0,)))
        for tile in range(start, start + GROUP):
            mine = got[(tile - start) * LANES : (tile - start + 1) * LANES]
            values = near_ref[tile] + turn_ref[1] * mine[:, :wide] - turn_ref[0] * mine[:, wide:]
            pack_ref[tile] = packed(values)
            wind = tile < 2 * per_field
            for part in range(pair):
                line = tile * pair + part
                first, last = part * rows, part * rows + rows - 1
                top, bottom = values[first : first + 1], values[last : last + 1]
                if wind:
                    top, bottom = top * inverse[:, :1], bottom * inverse[:, rows - 1 :]
                top_ref[line : line + 1] = top
                bottom_ref[line : line + 1] = bottom


def early_kernel(early, spread_ref, pack_ref, filtered_ref):
    per_field = pack_ref.shape[0] // 3
    pack = [pack_ref[f * per_field + tile] for tile in range(early) for f in range(3)]
    values = spread_lines(jnp.concatenate(pack, axis=0), spread_ref)
    filtered_ref[...] = values.reshape(filtered_ref.shape)


def finish_kernel(
    scale_ref, spread_ref, above_ref, below_ref, pack_ref, early_ref, tracer_ref, *refs
):
    outs = refs[:3]
    filtered_ref, edge_ref, column_ref, held_ref, load_sems, sems = refs[3:]
    levels, rows, width = tracer_ref.shape
    lanes = spread_ref.shape[1]
    count = above_ref.shape[0]
    pair = LANES // rows
    steps = levels // pair
    early = early_ref.shape[0]
    tracer_slot = 6 * pair

    def load(step):
        return pltpu.make_async_copy(
            tracer_ref.at[pl.ds(step * pair, pair)],
            held_ref.at[pl.ds(tracer_slot + step % 2 * pair, pair)],
            load_sems.at[step % 2],
        )

    def store(step, number):
        return pltpu.make_async_copy(
            held_ref.at[pl.ds((3 * (step % 2) + number) * pair, pair)],
            outs[number].at[pl.ds(step * pair, pair)],
            sems.at[step % 2, number],
        )

    load(0).start()
    edges = jnp.concatenate([above_ref[...], below_ref[...]], axis=0)
    edge_ref[...] = spread_lines(packed(edges), spread_ref)
    here = lax.broadcasted_iota(jnp.int32, (rows, rows), 0)
    there = lax.broadcasted_iota(jnp.int32, (rows, rows), 1)
    column = jnp.where(here == there, jnp.broadcast_to(scale_ref[...], (rows, rows)), 0.0)
    column = jnp.sum(column, axis=1, keepdims=True)
    column_ref[0] = jnp.broadcast_to(column, (rows, LANES))
    column_ref[1] = 1.0 / column_ref[0]
    row_number = lax.broadcasted_iota(jnp.int32, (rows, 1), 0)

    def fill(step):
        pack = jnp.concatenate([pack_ref[f * steps + step] for f in range(3)], axis=0)
        filtered_ref[step - early] = spread_lines(pack, spread_ref)

    def east_west(values):
        return pltpu.roll(values, lanes - 1, 1) - pltpu.roll(values, 1, 1)

    def stencil(step):
        scale = column_ref[0][:, :1]
        inverse = column_ref[1][:, :1]
        for part in range(pair):
            level = step * pair + part

            def field(number):
                at = number * pair * rows + part * rows
                if step < early:
                    return early_ref[step, at : at + rows]
                return filtered_ref[step - early, at : at + rows]

            def north_south(values, number):
                at = number * levels + level
                above = edge_ref[at : at + 1]
                below = edge_ref[count + at : count + at + 1]
                later = jnp.where(row_number == rows - 1, below, pltpu.roll(values, rows - 1, 0))
                earlier = jnp.where(row_number == 0, above, pltpu.roll(values, 1, 0))
                return later - earlier

            u, v, q = field(0), field(1), field(2)
            div = scale * (east_west(u) + north_south(v * inverse, 1))
            vort = scale * (east_west(v) - north_south(u * inverse, 0))
            change = u * (courant * scale) * east_west(q) + (courant * v) * north_south(q, 2)
            base = 3 * (step % 2) * pair + part
            held_ref[base] = held_ref[tracer_slot + step % 2 * pair + part] - change[:, :width]
            held_ref[base + pair] = div[:, :width]
            held_ref[base + 2 * pair] = vort[:, :width]

    for step in range(steps):
        if step + 1 < steps:
            load(step + 1).start()
        load(step).wait()
        if step >= 2:
            for number in range(3):
                store(step - 2, number).wait()
        stencil(step)
        if step + early < steps:
            fill(step + early)
        for number in range(3):
            store(step, number).start()
    for step in range(max(steps - 2, 0), steps):
        for number in range(3):
            store(step, number).wait()


def whole_spec():
    return pl.BlockSpec(memory_space=pltpu.VMEM)


def on_device(segments, lats, tables, wind_u, wind_v, tracer, cutoff, row_scale):
    levels, rows, width = wind_u.shape
    gather_table, moment_table, local_table, far_table, spread_table, places = tables
    nodes = gather_table.shape[0] // 2
    lanes = spread_table.shape[1]
    wide = nodes - EXTRA + LANES
    pair = LANES // rows
    group = 2 * pair
    groups = levels // group
    per_field = levels // pair
    tiles = 3 * per_field
    count = 3 * levels
    device = lax.axis_index("lon").astype(jnp.int32)[None]
    cut = cutoff.reshape(1, rows)
    scale = row_scale.reshape(1, rows)

    smem = pl.BlockSpec(memory_space=pltpu.SMEM)
    anywhere = pl.BlockSpec(memory_space=pl.ANY)
    def limit(mib):
        return pltpu.CompilerParams(vmem_limit_bytes=mib * 1024 * 1024)

    def cost(us):
        return pl.CostEstimate(flops=0, bytes_accessed=us * 3600000, transcendentals=0)

    steps = 3 * groups
    extra = jax.ShapeDtypeStruct((tiles, 2 * NEAR, LANES), F32)
    values, ahead, behind, every, table = pl.pallas_call(
        functools.partial(analyse_kernel, segments, groups),
        out_shape=(
            jax.ShapeDtypeStruct((tiles, nodes, LANES), F32),
            extra,
            extra,
            jax.ShapeDtypeStruct((segments, tiles, 2 * FAR, LANES), F32),
            jax.ShapeDtypeStruct((4, nodes, LANES), F32),
        ),
        in_specs=[smem] + [whole_spec()] * 4 + [anywhere] * 3,
        out_specs=(whole_spec(),) * 5,
        scratch_shapes=[
            pltpu.VMEM((steps, group, rows, width), F32),
            pltpu.VMEM((2, group * rows, width), BF),
            pltpu.VMEM((2, group * rows, width), BF),
            pltpu.SemaphoreType.DMA((steps,)),
        ],
        compiler_params=limit(50),
        cost_estimate=cost(12),
        name="analyse",
    )(device, cut, places, gather_table, moment_table, wind_u, wind_v, tracer)

    def shifted(array, by):
        return lax.ppermute(array, "lon", [(i, (i + by) % segments) for i in range(segments)])

    every = lax.all_to_all(every, "lon", 0, 0)
    ahead, behind = shifted(ahead, 1), shifted(behind, -1)

    near, turn = pl.pallas_call(
        near_kernel_call,
        out_shape=(
            jax.ShapeDtypeStruct((tiles, LANES, wide), F32),
            jax.ShapeDtypeStruct((2, LANES, wide), F32),
        ),
        in_specs=[whole_spec()] * 3,
        out_specs=(whole_spec(),) * 2,
        compiler_params=limit(24),
        cost_estimate=cost(6),
        name="near",
    )(local_table, table, values)

    edge = jax.ShapeDtypeStruct((count, wide), F32)
    pack, top, bottom = pl.pallas_call(
        functools.partial(combine_kernel, per_field, rows),
        out_shape=(jax.ShapeDtypeStruct((tiles, LANES, 2 * wide - LANES), BF), edge, edge),
        grid_spec=pltpu.PrefetchScalarGridSpec(
            num_scalar_prefetch=1,
            grid=(1,),
            in_specs=[whole_spec()] * 2
            + [pl.BlockSpec((1,) + far_table.shape[1:], lambda s, d: (d[0], 0, 0))]
            + [whole_spec()] * 4,
            out_specs=(whole_spec(),) * 3,
        ),
        compiler_params=limit(24),
        cost_estimate=cost(4),
        name="combine",
    )(device, scale, turn, far_table, near, ahead, behind, every)

    above = lax.ppermute(bottom, "lat", [(i, i + 1) for i in range(lats - 1)])
    below = lax.ppermute(top, "lat", [(i + 1, i) for i in range(lats - 1)])

    early = per_field // 2
    filtered = pl.pallas_call(
        functools.partial(early_kernel, early),
        out_shape=jax.ShapeDtypeStruct((early, 3 * LANES, lanes), F32),
        in_specs=[whole_spec()] * 2,
        out_specs=whole_spec(),
        compiler_params=limit(24),
        cost_estimate=cost(4),
        name="early",
    )(spread_table, pack)

    return pl.pallas_call(
        finish_kernel,
        out_shape=(jax.ShapeDtypeStruct((levels, rows, width), F32),) * 3,
        in_specs=[whole_spec()] * 6 + [anywhere],
        out_specs=(anywhere,) * 3,
        scratch_shapes=[
            pltpu.VMEM((per_field - early, 3 * LANES, lanes), F32),
            pltpu.VMEM((2 * count, lanes), F32),
            pltpu.VMEM((2, rows, LANES), F32),
            pltpu.VMEM((8 * pair, rows, width), F32),
            pltpu.SemaphoreType.DMA((2,)),
            pltpu.SemaphoreType.DMA((2, 3)),
        ],
        compiler_params=limit(32),
        cost_estimate=cost(10),
        name="finish",
    )(scale, spread_table, above, below, pack, filtered, tracer)


def solution(mesh):
    segments, lats = mesh.shape["lon"], mesh.shape["lat"]
    tables = tuple(make_tables(NLON // segments, segments))
    line = P(None, "lat", "lon")
    return jax.shard_map(
        functools.partial(on_device, segments, lats, tables),
        mesh=mesh,
        in_specs=(line, line, line, P("lat"), P("lat")),
        out_specs=(line, line, line),
        check_vma=False,
    )
```

```python
import functools
import math

import jax
import jax.numpy as jnp
import ml_dtypes
import numpy as np
from jax import lax
from jax.experimental import pallas as pl
from jax.experimental.pallas import tpu as pltpu
from jax.sharding import PartitionSpec as P

NLON = 12000
KMAX = 1024
NEAR = 12
FAR = 4
EXTRA = 32
LANES = 128
GROUP = 4
courant = 0.5
BF = jnp.bfloat16
F32 = jnp.float32


def prolate(points, band, count):
    i = np.arange(points)
    diag = ((points - 1 - 2 * i) / 2.0) ** 2 * np.cos(2 * np.pi * band)
    off = i[1:] * (points - i[1:]) / 2.0
    mid = points // 2
    half = (count + 1) // 2
    out = np.zeros((points, 2 * half))
    dd, ee = diag[mid:], off[mid:].copy()
    scaled = ee.copy()
    scaled[0] *= math.sqrt(2.0)
    even = np.linalg.eigh(np.diag(dd) + np.diag(scaled, 1) + np.diag(scaled, -1))[1]
    even = even[:, ::-1][:, :half]
    wing = even[1:] / math.sqrt(2.0)
    out[mid, 0::2] = even[0]
    out[mid + 1 :, 0::2] = wing
    out[:mid, 0::2] = wing[::-1]
    odd = np.linalg.eigh(np.diag(dd[1:]) + np.diag(ee[1:], 1) + np.diag(ee[1:], -1))[1]
    wing = odd[:, ::-1][:, :half] / math.sqrt(2.0)
    out[mid + 1 :, 1::2] = wing
    out[:mid, 1::2] = -wing[::-1]
    return out


def interpolation(low, high, nodes, snap):
    fine = prolate(2 * (high - low) + 1, (KMAX - 0.5) / NLON / 2, nodes + 2)
    wave = fine[:, nodes]
    at = np.nonzero(wave[:-1] * wave[1:] < 0)[0]
    roots = (at + wave[at] / (wave[at] - wave[at + 1]))[: nodes // 2] / 2 + low
    left = snap(roots)
    for i in range(1, len(left)):
        left[i] = max(left[i], left[i - 1] + 1)
    places = np.concatenate([left, (low + high) - left[::-1]])
    kept = nodes - 4
    index = np.round((places - low) * 2).astype(int)
    return places, fine[::2, :kept] @ np.linalg.pinv(fine[index, :kept])


def near_kernel(distance):
    return 1.0 / (NLON * np.sin(np.pi * distance / NLON))


def two_parts(table):
    high = table.astype(np.float32).astype(ml_dtypes.bfloat16)
    low = (table - high.astype(np.float64)).astype(np.float32).astype(ml_dtypes.bfloat16)
    return high, low


@functools.lru_cache(maxsize=4)
def make_tables(width, segments):
    main = -(-2 * KMAX * width // NLON // LANES) * LANES
    nodes = main + EXTRA
    source, gather = interpolation(0, width - 1, nodes, np.round)
    target, spread = interpolation(-1, width, nodes, lambda r: np.floor(r) + 0.5)
    local = near_kernel(target[:, None] - source[None])
    offsets = [d for d in range(-(segments - 1), segments) if d]
    far = {d: near_kernel(target[:, None] + width * d - source[None]) for d in offsets}

    def leading(kernel, count):
        found = np.linalg.svd(kernel, full_matrices=False)[2][:count]
        peak = np.take_along_axis(found, np.abs(found).argmax(1)[:, None], 1)
        return found * np.sign(peak)

    ahead = range(1, segments)
    basis = {s: leading(far[s], FAR) for s in ahead}
    for s in (1, segments - 1):
        both = leading(far[s], FAR + NEAR)
        basis[s], basis[-s] = both[:FAR], both[FAR:]

    high, low = two_parts(gather.T)
    gather_table = np.concatenate([high, low], 0)
    more = [basis[-1], basis[1 - segments]] + [basis[s] for s in ahead]
    rows = np.concatenate(more, 0)
    rows = np.pad(rows, ((0, -len(rows) % 8), (0, 0)))
    high, low = two_parts(rows)
    moment_table = np.concatenate([high, low, high], 1)
    high, low = two_parts(local)
    local_table = np.concatenate([high, low, high], 1)
    blocks = []
    for d in range(segments):
        pieces = [far[d - (d - s) % segments] @ basis[-s].T for s in (1, segments - 1)]
        for e in range(segments):
            if e == d:
                pieces.append(np.zeros((nodes, FAR)))
            else:
                pieces.append(far[d - e] @ basis[(d - e) % segments].T)
        pieces = [np.pad(piece, ((0, main + LANES - nodes), (0, 0))).T for piece in pieces]
        left = [p for piece in pieces for p in (piece, 0 * piece)]
        right = [p for piece in pieces for p in (0 * piece, piece)]
        both = np.concatenate([np.concatenate(left, 0), np.concatenate(right, 0)], 1)
        high, low = two_parts(both)
        blocks.append(np.concatenate([high, low, high], 0))
    far_table = np.stack(blocks)
    lanes = -(-(width + 2) // LANES) * LANES
    wide = np.zeros((nodes, lanes))
    wide[:, : width + 1] = spread.T[:, 1:]
    wide[:, lanes - 1] = spread.T[:, 0]
    high, low = two_parts(wide)
    none = np.zeros((LANES - 3 * EXTRA, lanes), high.dtype)
    spread_table = np.concatenate(
        [high[:main], low[:main], high[:main], high[main:], low[main:], high[main:], none], 0
    )
    places = np.stack([2 * source - width, 2 * target - width]).astype(np.float32)
    return gather_table, moment_table, local_table, far_table, spread_table, places[:, :, None]


def phases(cut, places, device, segments, width):
    full = 4.0 * NLON
    odd = 2.0 * cut - 1.0
    inner = odd * places
    inner = inner - full * jnp.floor(inner * (1.0 / full) + 0.5)
    base = odd * (2.0 * device + 1.0)
    cycle = 4.0 * segments
    base = (base - cycle * jnp.floor(base * (1.0 / cycle))) * float(width)
    total = inner + base
    total = total - full * jnp.floor(total * (1.0 / full) + 0.5)
    quarter = jnp.floor(total * (4.0 / full) + 0.5)
    x = (total - (full / 4.0) * quarter) * (2.0 * math.pi / full)
    y = x * x
    sine = x + x * y * (
        -1.0 / 6 + y * (1.0 / 120 + y * (-1.0 / 5040 + y * (1.0 / 362880)))
    )
    cosine = 1.0 + y * (
        -0.5 + y * (1.0 / 24 + y * (-1.0 / 720 + y * (1.0 / 40320 + y * (-1.0 / 3628800))))
    )
    odd_quarter = jnp.abs(quarter) == 1.0
    turned_c = jnp.where(odd_quarter, -quarter * sine, cosine)
    turned_s = jnp.where(odd_quarter, quarter * cosine, sine)
    flip = jnp.where(jnp.abs(quarter) == 2.0, -1.0, 1.0)
    return turned_c * flip, turned_s * flip


def parts(values):
    high = values.astype(BF)
    return high, (values - high.astype(F32)).astype(BF)


def stacked(values):
    high, low = parts(values)
    return jnp.concatenate([high, high, low], axis=0)


def product(a, b, dims):
    return lax.dot_general(a, b, (dims, ((), ())), preferred_element_type=F32)


def lane_cut(cut_ref):
    cut = cut_ref[...].astype(F32)
    return jnp.concatenate([cut] * (LANES // cut.shape[1]), axis=1)


def packed(values):
    main = values.shape[1] - LANES
    high, low = parts(values)
    last, last_low = high[:, main:].astype(F32), low[:, main:].astype(F32)
    last = last + pltpu.roll(last, EXTRA, 1) + pltpu.roll(last_low, 2 * EXTRA, 1)
    return jnp.concatenate([high[:, :main], low[:, :main], last.astype(BF)], axis=1)


def spread_lines(pack, spread_ref):
    main = (pack.shape[1] - LANES) // 2
    held = jnp.concatenate([pack[:, :main], pack], axis=1)
    return product(held, spread_ref[...], ((1,), (0,)))


def analyse_kernel(
    segments, groups, device_ref, cut_ref, places_ref, gather_ref, moment_ref,
    u_ref, v_ref, q_ref, node_ref, inner_ref, outer_ref, every_ref, table_ref,
    lines_ref, high_ref, low_ref, sems,
):
    width = u_ref.shape[2]
    steps, levels, rows, _ = lines_ref.shape
    lines = levels * rows
    nodes = gather_ref.shape[0] // 2
    me = device_ref[0]
    even = lax.rem(me, 2) == 0

    copies = []
    for step in range(steps):
        ref = (u_ref, v_ref, q_ref)[step // groups]
        levels_at = pl.ds((step % groups) * levels, levels)
        copies.append(pltpu.make_async_copy(ref.at[levels_at], lines_ref.at[step], sems.at[step]))
        copies[-1].start()
    for side in range(2):
        cosine, sine = phases(
            lane_cut(cut_ref), places_ref[side], me.astype(F32), segments, width
        )
        table_ref[2 * side], table_ref[2 * side + 1] = cosine, sine
    every_ref[me] = jnp.zeros(every_ref.shape[1:], F32)

    def cast(step):
        values = lines_ref[step].reshape(lines, width)
        high, low = parts(values)
        high_ref[step % 2] = high
        low_ref[step % 2] = low

    def gather(step):
        both = product(gather_ref[...], high_ref[step % 2], ((1,), (1,)))
        rest = product(gather_ref[:nodes], low_ref[step % 2], ((1,), (1,)))
        held = both[:nodes] + both[nodes:] + rest
        for part in range(lines // LANES):
            node_ref[step * (lines // LANES) + part] = held[:, part * LANES : (part + 1) * LANES]

    def moments(step):
        for part in range(lines // LANES):
            tile = step * (lines // LANES) + part
            mine = node_ref[tile]
            turned = jnp.concatenate([mine * table_ref[0], mine * table_ref[1]], axis=1)
            out = product(moment_ref[...], stacked(turned), ((1,), (0,)))
            ahead, behind = out[:NEAR], out[NEAR : 2 * NEAR]
            inner, outer = jnp.where(even, ahead, behind), jnp.where(even, behind, ahead)
            for ref, mine in ((inner_ref, inner), (outer_ref, outer)):
                ref[tile, :NEAR] = mine[:, :LANES]
                ref[tile, NEAR:] = mine[:, LANES:]
            at = 2 * NEAR
            for s in range(1, segments):
                to = lax.rem(me + s, segments)
                every_ref[to, tile, :FAR] = out[at : at + FAR, :LANES]
                every_ref[to, tile, FAR:] = out[at : at + FAR, LANES:]
                at += FAR

    copies[0].wait()
    cast(0)
    for step in range(steps):
        if step + 1 < steps:
            copies[step + 1].wait()
        gather(step)
        if step + 1 < steps:
            cast(step + 1)
        if step > 0:
            moments(step - 1)
    moments(steps - 1)


def turned_over(values):
    none = jnp.zeros((LANES - EXTRA, LANES), F32)
    return jnp.transpose(jnp.concatenate([values, none], axis=0))


def near_kernel_call(local_ref, table_ref, node_ref, near_ref, turn_ref):
    turn_ref[0] = turned_over(table_ref[2])
    turn_ref[1] = turned_over(table_ref[3])
    for start in range(0, node_ref.shape[0], GROUP):
        columns = []
        for tile in range(start, start + GROUP):
            columns += [node_ref[tile] * table_ref[0], node_ref[tile] * table_ref[1]]
        out = product(local_ref[...], stacked(jnp.concatenate(columns, axis=1)), ((1,), (0,)))
        for tile in range(GROUP):
            at = 2 * tile * LANES
            cosine, sine = out[:, at : at + LANES], out[:, at + LANES : at + 2 * LANES]
            near_ref[start + tile] = turned_over(table_ref[3] * cosine - table_ref[2] * sine)


def combine_kernel(
    per_field, rows, lon_ref, lat_ref, scale_ref, turn_ref, far_ref, near_ref, inner_ref, outer_ref,
    every_ref, pack_ref, first_ref, second_ref,
):
    tiles, _, wide = near_ref.shape
    segments = every_ref.shape[0]
    even, even_lat = lax.rem(lon_ref[0], 2) == 0, lax.rem(lat_ref[0], 2) == 0
    inverse = 1.0 / scale_ref[...]
    pair = LANES // rows
    for start in range(0, tiles, GROUP):
        columns = []
        for tile in range(start, start + GROUP):
            inner, outer = inner_ref[tile], outer_ref[tile]
            pieces = [jnp.where(even, outer, inner), jnp.where(even, inner, outer)]
            pieces += [every_ref[e, tile] for e in range(segments)]
            columns.append(jnp.concatenate(pieces, axis=0))
        got = product(stacked(jnp.concatenate(columns, axis=1)), far_ref[...], ((0,), (0,)))
        for tile in range(start, start + GROUP):
            mine = got[(tile - start) * LANES : (tile - start + 1) * LANES]
            values = near_ref[tile] + turn_ref[1] * mine[:, :wide] - turn_ref[0] * mine[:, wide:]
            pack_ref[tile] = packed(values)
            wind = tile < 2 * per_field
            for part in range(pair):
                line = tile * pair + part
                first, last = part * rows, part * rows + rows - 1
                top, bottom = values[first : first + 1], values[last : last + 1]
                if wind:
                    top, bottom = top * inverse[:, :1], bottom * inverse[:, rows - 1 :]
                first_ref[line : line + 1] = jnp.where(even_lat, bottom, top)
                second_ref[line : line + 1] = jnp.where(even_lat, top, bottom)


def early_kernel(early, spread_ref, pack_ref, filtered_ref):
    per_field = pack_ref.shape[0] // 3
    pack = [pack_ref[f * per_field + tile] for tile in range(early) for f in range(3)]
    values = spread_lines(jnp.concatenate(pack, axis=0), spread_ref)
    filtered_ref[...] = values.reshape(filtered_ref.shape)


def finish_kernel(
    lat_ref, scale_ref, spread_ref, first_ref, second_ref, pack_ref, early_ref, tracer_ref, *refs
):
    outs = refs[:3]
    filtered_ref, edge_ref, column_ref, held_ref, load_sems, sems = refs[3:]
    levels, rows, width = tracer_ref.shape
    lanes = spread_ref.shape[1]
    count = first_ref.shape[0]
    pair = LANES // rows
    steps = levels // pair
    early = early_ref.shape[0]
    tracer_slot = 6 * pair

    def load(step):
        return pltpu.make_async_copy(
            tracer_ref.at[pl.ds(step * pair, pair)],
            held_ref.at[pl.ds(tracer_slot + step % 2 * pair, pair)],
            load_sems.at[step % 2],
        )

    def store(step, number):
        return pltpu.make_async_copy(
            held_ref.at[pl.ds((3 * (step % 2) + number) * pair, pair)],
            outs[number].at[pl.ds(step * pair, pair)],
            sems.at[step % 2, number],
        )

    load(0).start()
    even_lat = lax.rem(lat_ref[0], 2) == 0
    first, second = first_ref[...], second_ref[...]
    above, below = jnp.where(even_lat, second, first), jnp.where(even_lat, first, second)
    edges = jnp.concatenate([above, below], axis=0)
    edge_ref[...] = spread_lines(packed(edges), spread_ref)
    here = lax.broadcasted_iota(jnp.int32, (rows, rows), 0)
    there = lax.broadcasted_iota(jnp.int32, (rows, rows), 1)
    column = jnp.where(here == there, jnp.broadcast_to(scale_ref[...], (rows, rows)), 0.0)
    column = jnp.sum(column, axis=1, keepdims=True)
    column_ref[0] = jnp.broadcast_to(column, (rows, LANES))
    column_ref[1] = 1.0 / column_ref[0]
    row_number = lax.broadcasted_iota(jnp.int32, (rows, 1), 0)

    def fill(step):
        pack = jnp.concatenate([pack_ref[f * steps + step] for f in range(3)], axis=0)
        filtered_ref[step - early] = spread_lines(pack, spread_ref)

    def east_west(values):
        return pltpu.roll(values, lanes - 1, 1) - pltpu.roll(values, 1, 1)

    def stencil(step):
        scale = column_ref[0][:, :1]
        inverse = column_ref[1][:, :1]
        for part in range(pair):
            level = step * pair + part

            def field(number):
                at = number * pair * rows + part * rows
                if step < early:
                    return early_ref[step, at : at + rows]
                return filtered_ref[step - early, at : at + rows]

            def north_south(values, number):
                at = number * levels + level
                above = edge_ref[at : at + 1]
                below = edge_ref[count + at : count + at + 1]
                later = jnp.where(row_number == rows - 1, below, pltpu.roll(values, rows - 1, 0))
                earlier = jnp.where(row_number == 0, above, pltpu.roll(values, 1, 0))
                return later - earlier

            u, v, q = field(0), field(1), field(2)
            div = scale * (east_west(u) + north_south(v * inverse, 1))
            vort = scale * (east_west(v) - north_south(u * inverse, 0))
            change = u * (courant * scale) * east_west(q) + (courant * v) * north_south(q, 2)
            base = 3 * (step % 2) * pair + part
            held_ref[base] = held_ref[tracer_slot + step % 2 * pair + part] - change[:, :width]
            held_ref[base + pair] = div[:, :width]
            held_ref[base + 2 * pair] = vort[:, :width]

    for step in range(steps):
        if step + 1 < steps:
            load(step + 1).start()
        load(step).wait()
        if step >= 2:
            for number in range(3):
                store(step - 2, number).wait()
        stencil(step)
        if step + early < steps:
            fill(step + early)
        for number in range(3):
            store(step, number).start()
    for step in range(max(steps - 2, 0), steps):
        for number in range(3):
            store(step, number).wait()


def whole_spec():
    return pl.BlockSpec(memory_space=pltpu.VMEM)


def on_device(segments, lats, tables, wind_u, wind_v, tracer, cutoff, row_scale):
    levels, rows, width = wind_u.shape
    gather_table, moment_table, local_table, far_table, spread_table, places = tables
    nodes = gather_table.shape[0] // 2
    lanes = spread_table.shape[1]
    wide = nodes - EXTRA + LANES
    pair = LANES // rows
    group = 2 * pair
    groups = levels // group
    per_field = levels // pair
    tiles = 3 * per_field
    count = 3 * levels
    lon, lat = lax.axis_index("lon").astype(jnp.int32), lax.axis_index("lat").astype(jnp.int32)
    lon, lat = lon[None], lat[None]
    cut = cutoff.reshape(1, rows)
    scale = row_scale.reshape(1, rows)

    smem = pl.BlockSpec(memory_space=pltpu.SMEM)
    anywhere = pl.BlockSpec(memory_space=pl.ANY)
    def limit(mib):
        return pltpu.CompilerParams(vmem_limit_bytes=mib * 1024 * 1024)

    def cost(us):
        return pl.CostEstimate(flops=0, bytes_accessed=us * 3600000, transcendentals=0)

    steps = 3 * groups
    extra = jax.ShapeDtypeStruct((tiles, 2 * NEAR, LANES), F32)
    values, inner, outer, every, table = pl.pallas_call(
        functools.partial(analyse_kernel, segments, groups),
        out_shape=(
            jax.ShapeDtypeStruct((tiles, nodes, LANES), F32),
            extra,
            extra,
            jax.ShapeDtypeStruct((segments, tiles, 2 * FAR, LANES), F32),
            jax.ShapeDtypeStruct((4, nodes, LANES), F32),
        ),
        in_specs=[smem] + [whole_spec()] * 4 + [anywhere] * 3,
        out_specs=(whole_spec(),) * 5,
        scratch_shapes=[
            pltpu.VMEM((steps, group, rows, width), F32),
            pltpu.VMEM((2, group * rows, width), BF),
            pltpu.VMEM((2, group * rows, width), BF),
            pltpu.SemaphoreType.DMA((steps,)),
        ],
        compiler_params=limit(56),
        cost_estimate=cost(12),
        name="analyse",
    )(lon, cut, places, gather_table, moment_table, wind_u, wind_v, tracer)

    def swapped(array, axis, start, closed):
        size = segments if axis == "lon" else lats
        pairs = [(i, (i + 1) % size) for i in range(start, size if closed else size - 1, 2)]
        return lax.ppermute(array, axis, pairs + [(b, a) for a, b in pairs])

    every = lax.all_to_all(every, "lon", 0, 0)
    inner, outer = swapped(inner, "lon", 0, True), swapped(outer, "lon", 1, True)
    far_mine = lax.dynamic_index_in_dim(jnp.asarray(far_table), lon[0], 0, False)

    near, turn = pl.pallas_call(
        near_kernel_call,
        out_shape=(
            jax.ShapeDtypeStruct((tiles, LANES, wide), F32),
            jax.ShapeDtypeStruct((2, LANES, wide), F32),
        ),
        in_specs=[whole_spec()] * 3,
        out_specs=(whole_spec(),) * 2,
        compiler_params=limit(24),
        cost_estimate=cost(6),
        name="near",
    )(local_table, table, values)

    edge = jax.ShapeDtypeStruct((count, wide), F32)
    pack, first, second = pl.pallas_call(
        functools.partial(combine_kernel, per_field, rows),
        out_shape=(jax.ShapeDtypeStruct((tiles, LANES, 2 * wide - LANES), BF), edge, edge),
        in_specs=[smem] * 2 + [whole_spec()] * 7,
        out_specs=(whole_spec(),) * 3,
        compiler_params=limit(24),
        cost_estimate=cost(4),
        name="combine",
    )(lon, lat, scale, turn, far_mine, near, inner, outer, every)

    first, second = swapped(first, "lat", 0, False), swapped(second, "lat", 1, False)

    early = per_field // 2
    filtered = pl.pallas_call(
        functools.partial(early_kernel, early),
        out_shape=jax.ShapeDtypeStruct((early, 3 * LANES, lanes), F32),
        in_specs=[whole_spec()] * 2,
        out_specs=whole_spec(),
        compiler_params=limit(24),
        cost_estimate=cost(4),
        name="early",
    )(spread_table, pack)

    return pl.pallas_call(
        finish_kernel,
        out_shape=(jax.ShapeDtypeStruct((levels, rows, width), F32),) * 3,
        in_specs=[smem] + [whole_spec()] * 6 + [anywhere],
        out_specs=(anywhere,) * 3,
        scratch_shapes=[
            pltpu.VMEM((per_field - early, 3 * LANES, lanes), F32),
            pltpu.VMEM((2 * count, lanes), F32),
            pltpu.VMEM((2, rows, LANES), F32),
            pltpu.VMEM((8 * pair, rows, width), F32),
            pltpu.SemaphoreType.DMA((2,)),
            pltpu.SemaphoreType.DMA((2, 3)),
        ],
        compiler_params=limit(32),
        cost_estimate=cost(10),
        name="finish",
    )(lat, scale, spread_table, first, second, pack, filtered, tracer)


def solution(mesh):
    segments, lats = mesh.shape["lon"], mesh.shape["lat"]
    tables = tuple(make_tables(NLON // segments, segments))
    line = P(None, "lat", "lon")
    return jax.shard_map(
        functools.partial(on_device, segments, lats, tables),
        mesh=mesh,
        in_specs=(line, line, line, P("lat"), P("lat")),
        out_specs=(line, line, line),
        check_vma=False,
    )
```

```python
import functools
import math

import jax
import jax.numpy as jnp
import ml_dtypes
import numpy as np
from jax import lax
from jax.experimental import pallas as pl
from jax.experimental.pallas import tpu as pltpu
from jax.sharding import PartitionSpec as P

NLON = 12000
KMAX = 1024
NEAR = 12
FAR = 4
EXTRA = 32
LANES = 128
SUB = 8
GROUP = 4
courant = 0.5
BF = jnp.bfloat16
F32 = jnp.float32


def prolate(points, band, count):
    i = np.arange(points)
    diag = ((points - 1 - 2 * i) / 2.0) ** 2 * np.cos(2 * np.pi * band)
    off = i[1:] * (points - i[1:]) / 2.0
    mid = points // 2
    half = (count + 1) // 2
    out = np.zeros((points, 2 * half))
    dd, ee = diag[mid:], off[mid:].copy()
    scaled = ee.copy()
    scaled[0] *= math.sqrt(2.0)
    even = np.linalg.eigh(np.diag(dd) + np.diag(scaled, 1) + np.diag(scaled, -1))[1]
    even = even[:, ::-1][:, :half]
    wing = even[1:] / math.sqrt(2.0)
    out[mid, 0::2] = even[0]
    out[mid + 1 :, 0::2] = wing
    out[:mid, 0::2] = wing[::-1]
    odd = np.linalg.eigh(np.diag(dd[1:]) + np.diag(ee[1:], 1) + np.diag(ee[1:], -1))[1]
    wing = odd[:, ::-1][:, :half] / math.sqrt(2.0)
    out[mid + 1 :, 1::2] = wing
    out[:mid, 1::2] = -wing[::-1]
    return out


def interpolation(low, high, nodes, snap):
    fine = prolate(2 * (high - low) + 1, (KMAX - 0.5) / NLON / 2, nodes + 2)
    wave = fine[:, nodes]
    at = np.nonzero(wave[:-1] * wave[1:] < 0)[0]
    roots = (at + wave[at] / (wave[at] - wave[at + 1]))[: nodes // 2] / 2 + low
    left = snap(roots)
    for i in range(1, len(left)):
        left[i] = max(left[i], left[i - 1] + 1)
    places = np.concatenate([left, (low + high) - left[::-1]])
    kept = nodes - 4
    index = np.round((places - low) * 2).astype(int)
    return places, fine[::2, :kept] @ np.linalg.pinv(fine[index, :kept])


def near_kernel(distance):
    return 1.0 / (NLON * np.sin(np.pi * distance / NLON))


def two_parts(table):
    high = table.astype(np.float32).astype(ml_dtypes.bfloat16)
    low = (table - high.astype(np.float64)).astype(np.float32).astype(ml_dtypes.bfloat16)
    return high, low


@functools.lru_cache(maxsize=4)
def make_tables(width, segments):
    main = -(-2 * KMAX * width // NLON // LANES) * LANES
    nodes = main + EXTRA
    source, gather = interpolation(0, width - 1, nodes, np.round)
    target, spread = interpolation(-1, width, nodes, lambda r: np.floor(r) + 0.5)
    local = near_kernel(target[:, None] - source[None])
    offsets = [d for d in range(-(segments - 1), segments) if d]
    far = {d: near_kernel(target[:, None] + width * d - source[None]) for d in offsets}

    def leading(kernel, count):
        found = np.linalg.svd(kernel, full_matrices=False)[2][:count]
        peak = np.take_along_axis(found, np.abs(found).argmax(1)[:, None], 1)
        return found * np.sign(peak)

    ahead = range(1, segments)
    basis = {s: leading(far[s], FAR) for s in ahead}
    for s in (1, segments - 1):
        both = leading(far[s], FAR + NEAR)
        basis[s], basis[-s] = both[:FAR], both[FAR:]

    high, low = two_parts(gather.T)
    gather_table = np.concatenate([high, low], 0)
    more = [basis[-1], basis[1 - segments]] + [basis[s] for s in ahead]
    rows = np.concatenate(more, 0)
    rows = np.pad(rows, ((0, -len(rows) % 8), (0, 0)))
    high, low = two_parts(rows)
    moment_table = np.concatenate([high, low, high], 1)
    high, low = two_parts(local)
    local_table = np.concatenate([high, low, high], 1)
    blocks = []
    for d in range(segments):
        pieces = [far[d - (d - s) % segments] @ basis[-s].T for s in (1, segments - 1)]
        for e in range(segments):
            if e == d:
                pieces.append(np.zeros((nodes, FAR)))
            else:
                pieces.append(far[d - e] @ basis[(d - e) % segments].T)
        pieces = [np.pad(piece, ((0, main + LANES - nodes), (0, 0))).T for piece in pieces]
        left = [p for piece in pieces for p in (piece, 0 * piece)]
        right = [p for piece in pieces for p in (0 * piece, piece)]
        both = np.concatenate([np.concatenate(left, 0), np.concatenate(right, 0)], 1)
        high, low = two_parts(both)
        blocks.append(np.concatenate([high, low, high], 0))
    far_table = np.stack(blocks)
    lanes = -(-(width + 2) // LANES) * LANES
    wide = np.zeros((nodes, lanes))
    wide[:, : width + 1] = spread.T[:, 1:]
    wide[:, lanes - 1] = spread.T[:, 0]
    high, low = two_parts(wide)
    none = np.zeros((LANES - 3 * EXTRA, lanes), high.dtype)
    spread_table = np.concatenate(
        [high[:main], low[:main], high[:main], high[main:], low[main:], high[main:], none], 0
    )
    places = np.stack([2 * source - width, 2 * target - width]).astype(np.float32)
    return gather_table, moment_table, local_table, far_table, spread_table, places[:, :, None]


def phases(cut, places, device, segments, width):
    full = 4.0 * NLON
    odd = 2.0 * cut - 1.0
    inner = odd * places
    inner = inner - full * jnp.floor(inner * (1.0 / full) + 0.5)
    base = odd * (2.0 * device + 1.0)
    cycle = 4.0 * segments
    base = (base - cycle * jnp.floor(base * (1.0 / cycle))) * float(width)
    total = inner + base
    total = total - full * jnp.floor(total * (1.0 / full) + 0.5)
    quarter = jnp.floor(total * (4.0 / full) + 0.5)
    x = (total - (full / 4.0) * quarter) * (2.0 * math.pi / full)
    y = x * x
    sine = x + x * y * (
        -1.0 / 6 + y * (1.0 / 120 + y * (-1.0 / 5040 + y * (1.0 / 362880)))
    )
    cosine = 1.0 + y * (
        -0.5 + y * (1.0 / 24 + y * (-1.0 / 720 + y * (1.0 / 40320 + y * (-1.0 / 3628800))))
    )
    odd_quarter = jnp.abs(quarter) == 1.0
    turned_c = jnp.where(odd_quarter, -quarter * sine, cosine)
    turned_s = jnp.where(odd_quarter, quarter * cosine, sine)
    flip = jnp.where(jnp.abs(quarter) == 2.0, -1.0, 1.0)
    return turned_c * flip, turned_s * flip


def parts(values):
    high = values.astype(BF)
    return high, (values - high.astype(F32)).astype(BF)


def stacked(values):
    high, low = parts(values)
    return jnp.concatenate([high, high, low], axis=0)


def product(a, b, dims):
    return lax.dot_general(a, b, (dims, ((), ())), preferred_element_type=F32)


def lane_cut(cut_ref):
    cut = cut_ref[...].astype(F32)
    return jnp.concatenate([cut] * (LANES // cut.shape[1]), axis=1)


def packed(values):
    main = values.shape[1] - LANES
    high, low = parts(values)
    last, last_low = high[:, main:].astype(F32), low[:, main:].astype(F32)
    last = last + pltpu.roll(last, EXTRA, 1) + pltpu.roll(last_low, 2 * EXTRA, 1)
    return jnp.concatenate([high[:, :main], low[:, :main], last.astype(BF)], axis=1)


def spread_lines(pack, spread_ref):
    main = (pack.shape[1] - LANES) // 2
    held = jnp.concatenate([pack[:, :main], pack], axis=1)
    return product(held, spread_ref[...], ((1,), (0,)))


def analyse_kernel(
    segments, groups, device_ref, cut_ref, places_ref, moment_ref, gather_in, far_in,
    u_ref, v_ref, q_ref, node_out, inner_ref, outer_ref, every_ref, table_out, far_out,
    lines_ref, high_ref, low_ref, gather_ref, node_ref, table_ref, sems, node_sems,
):
    width = u_ref.shape[2]
    steps, levels, rows, _ = lines_ref.shape
    lines = levels * rows
    nodes = gather_ref.shape[0] // 2
    me = device_ref[0]
    even = lax.rem(me, 2) == 0

    gather_copy = pltpu.make_async_copy(gather_in, gather_ref, sems.at[steps])
    far_copy = pltpu.make_async_copy(far_in.at[me], far_out, sems.at[steps + 1])
    table_copy = pltpu.make_async_copy(table_ref, table_out, sems.at[steps + 2])
    copies, node_copies = [], []
    for step in range(steps):
        ref = (u_ref, v_ref, q_ref)[step // groups]
        levels_at = pl.ds((step % groups) * levels, levels)
        copies.append(pltpu.make_async_copy(ref.at[levels_at], lines_ref.at[step], sems.at[step]))
        copies[-1].start()
        if step == 0:
            gather_copy.start()
    far_copy.start()
    for side in range(2):
        cosine, sine = phases(
            lane_cut(cut_ref), places_ref[side], me.astype(F32), segments, width
        )
        table_ref[2 * side], table_ref[2 * side + 1] = cosine, sine
    table_copy.start()
    every_ref[me] = jnp.zeros(every_ref.shape[1:], F32)

    def cast(step):
        values = lines_ref[step].reshape(lines, width)
        high, low = parts(values)
        high_ref[step % 2] = high
        low_ref[step % 2] = low

    def gather(step):
        both = product(gather_ref[...], high_ref[step % 2], ((1,), (1,)))
        rest = product(gather_ref[:nodes], low_ref[step % 2], ((1,), (1,)))
        held = both[:nodes] + both[nodes:] + rest
        for part in range(lines // LANES):
            node_ref[step * (lines // LANES) + part] = held[:, part * LANES : (part + 1) * LANES]

    def moments(step):
        for part in range(lines // LANES):
            tile = step * (lines // LANES) + part
            mine = node_ref[tile]
            turned = jnp.concatenate([mine * table_ref[0], mine * table_ref[1]], axis=1)
            out = product(moment_ref[...], stacked(turned), ((1,), (0,)))
            ahead, behind = out[:NEAR], out[NEAR : 2 * NEAR]
            inner, outer = jnp.where(even, ahead, behind), jnp.where(even, behind, ahead)
            for ref, mine in ((inner_ref, inner), (outer_ref, outer)):
                ref[tile, :NEAR] = mine[:, :LANES]
                ref[tile, NEAR:] = mine[:, LANES:]
            at = 2 * NEAR
            for s in range(1, segments):
                to = lax.rem(me + s, segments)
                every_ref[to, tile, :FAR] = out[at : at + FAR, :LANES]
                every_ref[to, tile, FAR:] = out[at : at + FAR, LANES:]
                at += FAR

    copies[0].wait()
    cast(0)
    gather_copy.wait()
    for step in range(steps):
        if step + 1 < steps:
            copies[step + 1].wait()
        gather(step)
        if step + 1 < steps:
            cast(step + 1)
        if step > 0:
            moments(step - 1)
        tiles_at = pl.ds(step * (lines // LANES), lines // LANES)
        node_copies.append(
            pltpu.make_async_copy(node_ref.at[tiles_at], node_out.at[tiles_at], node_sems.at[step])
        )
        node_copies[-1].start()
    moments(steps - 1)
    for copy in [table_copy, far_copy] + node_copies:
        copy.wait()


def turned_over(values):
    none = jnp.zeros((LANES - EXTRA, LANES), F32)
    return jnp.transpose(jnp.concatenate([values, none], axis=0))


def near_kernel_call(local_ref, table_ref, node_ref, near_ref, turn_ref):
    turn_ref[0] = turned_over(table_ref[2])
    turn_ref[1] = turned_over(table_ref[3])
    for start in range(0, node_ref.shape[0], GROUP):
        columns = []
        for tile in range(start, start + GROUP):
            columns += [node_ref[tile] * table_ref[0], node_ref[tile] * table_ref[1]]
        out = product(local_ref[...], stacked(jnp.concatenate(columns, axis=1)), ((1,), (0,)))
        for tile in range(GROUP):
            at = 2 * tile * LANES
            cosine, sine = out[:, at : at + LANES], out[:, at + LANES : at + 2 * LANES]
            near_ref[start + tile] = turned_over(table_ref[3] * cosine - table_ref[2] * sine)


def combine_kernel(
    per_field, rows, lon_ref, lat_ref, scale_ref, turn_ref, far_ref, near_ref, inner_ref, outer_ref,
    every_ref, pack_ref, first_ref, second_ref,
):
    tiles, _, wide = near_ref.shape
    segments = every_ref.shape[0]
    even, even_lat = lax.rem(lon_ref[0], 2) == 0, lax.rem(lat_ref[0], 2) == 0
    inverse = 1.0 / scale_ref[...]
    pair = LANES // rows
    for start in range(0, tiles, GROUP):
        columns = []
        for tile in range(start, start + GROUP):
            inner, outer = inner_ref[tile], outer_ref[tile]
            pieces = [jnp.where(even, outer, inner), jnp.where(even, inner, outer)]
            pieces += [every_ref[e, tile] for e in range(segments)]
            columns.append(jnp.concatenate(pieces, axis=0))
        got = product(stacked(jnp.concatenate(columns, axis=1)), far_ref[...], ((0,), (0,)))
        for tile in range(start, start + GROUP):
            mine = got[(tile - start) * LANES : (tile - start + 1) * LANES]
            values = near_ref[tile] + turn_ref[1] * mine[:, :wide] - turn_ref[0] * mine[:, wide:]
            pack_ref[tile] = packed(values)
            wind = tile < 2 * per_field
            for part in range(pair):
                line = tile * pair + part
                first, last = part * rows, part * rows + rows - 1
                top, bottom = values[first : first + 1], values[last : last + 1]
                if wind:
                    top, bottom = top * inverse[:, :1], bottom * inverse[:, rows - 1 :]
                first_ref[line : line + 1] = jnp.where(even_lat, bottom, top)
                second_ref[line : line + 1] = jnp.where(even_lat, top, bottom)


def early_kernel(early, spread_ref, pack_ref, filtered_ref):
    per_field = pack_ref.shape[0] // 3
    pack = [pack_ref[f * per_field + tile] for tile in range(early) for f in range(3)]
    values = spread_lines(jnp.concatenate(pack, axis=0), spread_ref)
    filtered_ref[...] = values.reshape(filtered_ref.shape)


def finish_kernel(
    lat_ref, scale_ref, spread_ref, first_ref, second_ref, pack_ref, early_ref, tracer_ref, *refs
):
    outs = refs[:3]
    filtered_ref, edge_ref, column_ref, held_ref, load_sems, sems = refs[3:]
    levels, rows, width = tracer_ref.shape
    lanes = spread_ref.shape[1]
    count = first_ref.shape[0]
    pair = LANES // rows
    steps = levels // pair
    early = early_ref.shape[0]
    tracer_slot = 6 * pair

    def load(step):
        return pltpu.make_async_copy(
            tracer_ref.at[pl.ds(step * pair, pair)],
            held_ref.at[pl.ds(tracer_slot + step % 2 * pair, pair)],
            load_sems.at[step % 2],
        )

    def store(step, number):
        return pltpu.make_async_copy(
            held_ref.at[pl.ds((3 * (step % 2) + number) * pair, pair)],
            outs[number].at[pl.ds(step * pair, pair)],
            sems.at[step % 2, number],
        )

    load(0).start()
    even_lat = lax.rem(lat_ref[0], 2) == 0
    first, second = first_ref[...], second_ref[...]
    above, below = jnp.where(even_lat, second, first), jnp.where(even_lat, first, second)
    edges = jnp.concatenate([above, below], axis=0)
    edge_ref[...] = spread_lines(packed(edges), spread_ref)
    here = lax.broadcasted_iota(jnp.int32, (rows, rows), 0)
    there = lax.broadcasted_iota(jnp.int32, (rows, rows), 1)
    column = jnp.where(here == there, jnp.broadcast_to(scale_ref[...], (rows, rows)), 0.0)
    column = jnp.sum(column, axis=1, keepdims=True)
    column_ref[0] = jnp.broadcast_to(column, (rows, LANES))
    column_ref[1] = 1.0 / column_ref[0]
    row_number = lax.broadcasted_iota(jnp.int32, (SUB, 1), 0)

    def fill(step):
        pack = jnp.concatenate([pack_ref[f * steps + step] for f in range(3)], axis=0)
        filtered_ref[step - early] = spread_lines(pack, spread_ref)

    def east_west(values):
        return pltpu.roll(values, lanes - 1, 1) - pltpu.roll(values, 1, 1)

    def stencil(step):
        scale = column_ref[0][:, :1]
        inverse = column_ref[1][:, :1]
        for part in range(pair):
            level = step * pair + part

            def field(number):
                at = number * pair * rows + part * rows
                if step < early:
                    return early_ref[step, at : at + rows]
                return filtered_ref[step - early, at : at + rows]

            def north_south(values, number):
                at = number * levels + level
                above = edge_ref[at : at + 1]
                below = edge_ref[count + at : count + at + 1]
                later, earlier = pltpu.roll(values, rows - 1, 0), pltpu.roll(values, 1, 0)
                low, high = slice(0, SUB), slice(rows - SUB, rows)
                first = later[low] - jnp.where(row_number == 0, above, earlier[low])
                last = jnp.where(row_number == SUB - 1, below, later[high]) - earlier[high]
                inside = slice(SUB, rows - SUB)
                return jnp.concatenate([first, later[inside] - earlier[inside], last], axis=0)

            u, v, q = field(0), field(1), field(2)
            div = scale * (east_west(u) + north_south(v * inverse, 1))
            vort = scale * (east_west(v) - north_south(u * inverse, 0))
            change = u * (courant * scale) * east_west(q) + (courant * v) * north_south(q, 2)
            base = 3 * (step % 2) * pair + part
            held_ref[base] = held_ref[tracer_slot + step % 2 * pair + part] - change[:, :width]
            held_ref[base + pair] = div[:, :width]
            held_ref[base + 2 * pair] = vort[:, :width]

    for step in range(steps):
        if step + 1 < steps:
            load(step + 1).start()
        load(step).wait()
        if step >= 2:
            for number in range(3):
                store(step - 2, number).wait()
        stencil(step)
        if step + early < steps:
            fill(step + early)
        for number in range(3):
            store(step, number).start()
    for step in range(max(steps - 2, 0), steps):
        for number in range(3):
            store(step, number).wait()


def whole_spec():
    return pl.BlockSpec(memory_space=pltpu.VMEM)


def on_device(segments, lats, tables, wind_u, wind_v, tracer, cutoff, row_scale):
    levels, rows, width = wind_u.shape
    gather_table, moment_table, local_table, far_table, spread_table, places = tables
    nodes = gather_table.shape[0] // 2
    lanes = spread_table.shape[1]
    wide = nodes - EXTRA + LANES
    pair = LANES // rows
    group = 2 * pair
    groups = levels // group
    per_field = levels // pair
    tiles = 3 * per_field
    count = 3 * levels
    lon, lat = lax.axis_index("lon").astype(jnp.int32), lax.axis_index("lat").astype(jnp.int32)
    lon, lat = lon[None], lat[None]
    cut = cutoff.reshape(1, rows)
    scale = row_scale.reshape(1, rows)

    smem = pl.BlockSpec(memory_space=pltpu.SMEM)
    anywhere = pl.BlockSpec(memory_space=pl.ANY)
    def limit(mib):
        return pltpu.CompilerParams(vmem_limit_bytes=mib * 1024 * 1024)

    def cost(us):
        return pl.CostEstimate(flops=0, bytes_accessed=us * 3600000, transcendentals=0)

    steps = 3 * groups
    extra = jax.ShapeDtypeStruct((tiles, 2 * NEAR, LANES), F32)
    values, inner, outer, every, table, far_mine = pl.pallas_call(
        functools.partial(analyse_kernel, segments, groups),
        out_shape=(
            jax.ShapeDtypeStruct((tiles, nodes, LANES), F32),
            extra,
            extra,
            jax.ShapeDtypeStruct((segments, tiles, 2 * FAR, LANES), F32),
            jax.ShapeDtypeStruct((4, nodes, LANES), F32),
            jax.ShapeDtypeStruct(far_table.shape[1:], BF),
        ),
        in_specs=[smem] + [whole_spec()] * 3 + [anywhere] * 5,
        out_specs=(anywhere,) + (whole_spec(),) * 3 + (anywhere,) * 2,
        scratch_shapes=[
            pltpu.VMEM((steps, group, rows, width), F32),
            pltpu.VMEM((2, group * rows, width), BF),
            pltpu.VMEM((2, group * rows, width), BF),
            pltpu.VMEM(gather_table.shape, BF),
            pltpu.VMEM((tiles, nodes, LANES), F32),
            pltpu.VMEM((4, nodes, LANES), F32),
            pltpu.SemaphoreType.DMA((steps + 3,)),
            pltpu.SemaphoreType.DMA((steps,)),
        ],
        compiler_params=limit(56),
        cost_estimate=cost(12),
        name="analyse",
    )(lon, cut, places, moment_table, gather_table, far_table, wind_u, wind_v, tracer)

    def swapped(array, axis, start, closed):
        size = segments if axis == "lon" else lats
        pairs = [(i, (i + 1) % size) for i in range(start, size if closed else size - 1, 2)]
        return lax.ppermute(array, axis, pairs + [(b, a) for a, b in pairs])

    every = lax.all_to_all(every, "lon", 0, 0)
    inner, outer = swapped(inner, "lon", 0, True), swapped(outer, "lon", 1, True)

    near, turn = pl.pallas_call(
        near_kernel_call,
        out_shape=(
            jax.ShapeDtypeStruct((tiles, LANES, wide), F32),
            jax.ShapeDtypeStruct((2, LANES, wide), F32),
        ),
        in_specs=[whole_spec()] * 3,
        out_specs=(whole_spec(),) * 2,
        compiler_params=limit(24),
        cost_estimate=cost(6),
        name="near",
    )(local_table, table, values)

    edge = jax.ShapeDtypeStruct((count, wide), F32)
    pack, first, second = pl.pallas_call(
        functools.partial(combine_kernel, per_field, rows),
        out_shape=(jax.ShapeDtypeStruct((tiles, LANES, 2 * wide - LANES), BF), edge, edge),
        in_specs=[smem] * 2 + [whole_spec()] * 7,
        out_specs=(whole_spec(),) * 3,
        compiler_params=limit(24),
        cost_estimate=cost(4),
        name="combine",
    )(lon, lat, scale, turn, far_mine, near, inner, outer, every)

    first, second = swapped(first, "lat", 0, False), swapped(second, "lat", 1, False)

    early = per_field // 2
    filtered = pl.pallas_call(
        functools.partial(early_kernel, early),
        out_shape=jax.ShapeDtypeStruct((early, 3 * LANES, lanes), F32),
        in_specs=[whole_spec()] * 2,
        out_specs=whole_spec(),
        compiler_params=limit(24),
        cost_estimate=cost(4),
        name="early",
    )(spread_table, pack)

    return pl.pallas_call(
        finish_kernel,
        out_shape=(jax.ShapeDtypeStruct((levels, rows, width), F32),) * 3,
        in_specs=[smem] + [whole_spec()] * 6 + [anywhere],
        out_specs=(anywhere,) * 3,
        scratch_shapes=[
            pltpu.VMEM((per_field - early, 3 * LANES, lanes), F32),
            pltpu.VMEM((2 * count, lanes), F32),
            pltpu.VMEM((2, rows, LANES), F32),
            pltpu.VMEM((8 * pair, rows, width), F32),
            pltpu.SemaphoreType.DMA((2,)),
            pltpu.SemaphoreType.DMA((2, 3)),
        ],
        compiler_params=limit(32),
        cost_estimate=cost(10),
        name="finish",
    )(lat, scale, spread_table, first, second, pack, filtered, tracer)


def solution(mesh):
    segments, lats = mesh.shape["lon"], mesh.shape["lat"]
    tables = tuple(make_tables(NLON // segments, segments))
    line = P(None, "lat", "lon")
    return jax.shard_map(
        functools.partial(on_device, segments, lats, tables),
        mesh=mesh,
        in_specs=(line, line, line, P("lat"), P("lat")),
        out_specs=(line, line, line),
        check_vma=False,
    )
```

```python
import functools
import math

import jax
import jax.numpy as jnp
import ml_dtypes
import numpy as np
from jax import lax
from jax.experimental import pallas as pl
from jax.experimental.pallas import tpu as pltpu
from jax.sharding import PartitionSpec as P

NLON = 12000
KMAX = 1024
NEAR = 12
FAR = 4
EXTRA = 32
LANES = 128
SUB = 8
GROUP = 4
courant = 0.5
BF = jnp.bfloat16
F32 = jnp.float32


def prolate(points, band, count):
    i = np.arange(points)
    diag = ((points - 1 - 2 * i) / 2.0) ** 2 * np.cos(2 * np.pi * band)
    off = i[1:] * (points - i[1:]) / 2.0
    mid = points // 2
    half = (count + 1) // 2
    out = np.zeros((points, 2 * half))
    dd, ee = diag[mid:], off[mid:].copy()
    scaled = ee.copy()
    scaled[0] *= math.sqrt(2.0)
    even = np.linalg.eigh(np.diag(dd) + np.diag(scaled, 1) + np.diag(scaled, -1))[1]
    even = even[:, ::-1][:, :half]
    wing = even[1:] / math.sqrt(2.0)
    out[mid, 0::2] = even[0]
    out[mid + 1 :, 0::2] = wing
    out[:mid, 0::2] = wing[::-1]
    odd = np.linalg.eigh(np.diag(dd[1:]) + np.diag(ee[1:], 1) + np.diag(ee[1:], -1))[1]
    wing = odd[:, ::-1][:, :half] / math.sqrt(2.0)
    out[mid + 1 :, 1::2] = wing
    out[:mid, 1::2] = -wing[::-1]
    return out


def interpolation(low, high, nodes, snap):
    fine = prolate(2 * (high - low) + 1, (KMAX - 0.5) / NLON / 2, nodes + 2)
    wave = fine[:, nodes]
    at = np.nonzero(wave[:-1] * wave[1:] < 0)[0]
    roots = (at + wave[at] / (wave[at] - wave[at + 1]))[: nodes // 2] / 2 + low
    left = snap(roots)
    for i in range(1, len(left)):
        left[i] = max(left[i], left[i - 1] + 1)
    places = np.concatenate([left, (low + high) - left[::-1]])
    kept = nodes - 4
    index = np.round((places - low) * 2).astype(int)
    return places, fine[::2, :kept] @ np.linalg.pinv(fine[index, :kept])


def near_kernel(distance):
    return 1.0 / (NLON * np.sin(np.pi * distance / NLON))


def two_parts(table):
    high = table.astype(np.float32).astype(ml_dtypes.bfloat16)
    low = (table - high.astype(np.float64)).astype(np.float32).astype(ml_dtypes.bfloat16)
    return high, low


@functools.lru_cache(maxsize=4)
def make_tables(width, segments):
    main = -(-2 * KMAX * width // NLON // LANES) * LANES
    nodes = main + EXTRA
    source, gather = interpolation(0, width - 1, nodes, np.round)
    target, spread = interpolation(-1, width, nodes, lambda r: np.floor(r) + 0.5)
    local = near_kernel(target[:, None] - source[None])
    offsets = [d for d in range(-(segments - 1), segments) if d]
    far = {d: near_kernel(target[:, None] + width * d - source[None]) for d in offsets}

    def leading(kernel, count):
        found = np.linalg.svd(kernel, full_matrices=False)[2][:count]
        peak = np.take_along_axis(found, np.abs(found).argmax(1)[:, None], 1)
        return found * np.sign(peak)

    ahead = range(1, segments)
    basis = {s: leading(far[s], FAR) for s in ahead}
    for s in (1, segments - 1):
        both = leading(far[s], FAR + NEAR)
        basis[s], basis[-s] = both[:FAR], both[FAR:]

    high, low = two_parts(gather.T)
    gather_table = np.concatenate([high, low], 0)
    more = [basis[-1], basis[1 - segments]] + [basis[s] for s in ahead]
    rows = np.concatenate(more, 0)
    rows = np.pad(rows, ((0, -len(rows) % 8), (0, 0)))
    high, low = two_parts(rows)
    moment_table = np.concatenate([high, low, high], 1)
    high, low = two_parts(local)
    local_table = np.concatenate([high, low, high], 1)
    blocks = []
    for d in range(segments):
        pieces = [far[d - (d - s) % segments] @ basis[-s].T for s in (1, segments - 1)]
        for e in range(segments):
            if e == d:
                pieces.append(np.zeros((nodes, FAR)))
            else:
                pieces.append(far[d - e] @ basis[(d - e) % segments].T)
        pieces = [np.pad(piece, ((0, main + LANES - nodes), (0, 0))).T for piece in pieces]
        left = [p for piece in pieces for p in (piece, 0 * piece)]
        right = [p for piece in pieces for p in (0 * piece, piece)]
        both = np.concatenate([np.concatenate(left, 0), np.concatenate(right, 0)], 1)
        high, low = two_parts(both)
        blocks.append(np.concatenate([high, low, high], 0))
    far_table = np.stack(blocks)
    lanes = -(-(width + 2) // LANES) * LANES
    wide = np.zeros((nodes, lanes))
    wide[:, : width + 1] = spread.T[:, 1:]
    wide[:, lanes - 1] = spread.T[:, 0]
    high, low = two_parts(wide)
    none = np.zeros((LANES - 3 * EXTRA, lanes), high.dtype)
    spread_table = np.concatenate(
        [high[:main], low[:main], high[:main], high[main:], low[main:], high[main:], none], 0
    )
    places = np.stack([2 * source - width, 2 * target - width]).astype(np.float32)
    return gather_table, moment_table, local_table, far_table, spread_table, places[:, :, None]


def phases(cut, places, device, segments, width):
    full = 4.0 * NLON
    odd = 2.0 * cut - 1.0
    inner = odd * places
    inner = inner - full * jnp.floor(inner * (1.0 / full) + 0.5)
    base = odd * (2.0 * device + 1.0)
    cycle = 4.0 * segments
    base = (base - cycle * jnp.floor(base * (1.0 / cycle))) * float(width)
    total = inner + base
    total = total - full * jnp.floor(total * (1.0 / full) + 0.5)
    quarter = jnp.floor(total * (4.0 / full) + 0.5)
    x = (total - (full / 4.0) * quarter) * (2.0 * math.pi / full)
    y = x * x
    sine = x + x * y * (
        -1.0 / 6 + y * (1.0 / 120 + y * (-1.0 / 5040 + y * (1.0 / 362880)))
    )
    cosine = 1.0 + y * (
        -0.5 + y * (1.0 / 24 + y * (-1.0 / 720 + y * (1.0 / 40320 + y * (-1.0 / 3628800))))
    )
    odd_quarter = jnp.abs(quarter) == 1.0
    turned_c = jnp.where(odd_quarter, -quarter * sine, cosine)
    turned_s = jnp.where(odd_quarter, quarter * cosine, sine)
    flip = jnp.where(jnp.abs(quarter) == 2.0, -1.0, 1.0)
    return turned_c * flip, turned_s * flip


def parts(values):
    high = values.astype(BF)
    return high, (values - high.astype(F32)).astype(BF)


def stacked(values):
    high, low = parts(values)
    return jnp.concatenate([high, high, low], axis=0)


def product(a, b, dims):
    return lax.dot_general(a, b, (dims, ((), ())), preferred_element_type=F32)


def lane_cut(cut_ref):
    cut = cut_ref[...].astype(F32)
    return jnp.concatenate([cut] * (LANES // cut.shape[1]), axis=1)


def packed(values):
    main = values.shape[1] - LANES
    high, low = parts(values)
    last, last_low = high[:, main:].astype(F32), low[:, main:].astype(F32)
    last = last + pltpu.roll(last, EXTRA, 1) + pltpu.roll(last_low, 2 * EXTRA, 1)
    return jnp.concatenate([high[:, :main], low[:, :main], last.astype(BF)], axis=1)


def spread_lines(pack, spread_ref):
    main = (pack.shape[1] - LANES) // 2
    held = jnp.concatenate([pack[:, :main], pack], axis=1)
    return product(held, spread_ref[...], ((1,), (0,)))


def analyse_kernel(
    segments, groups, device_ref, cut_ref, places_ref, gather_ref, moment_ref,
    u_ref, v_ref, q_ref, node_ref, inner_ref, outer_ref, every_ref, table_ref,
    lines_ref, high_ref, low_ref, sems,
):
    width = u_ref.shape[2]
    steps, levels, rows, _ = lines_ref.shape
    lines = levels * rows
    nodes = gather_ref.shape[0] // 2
    me = device_ref[0]
    even = lax.rem(me, 2) == 0

    copies = []
    for step in range(steps):
        ref = (u_ref, v_ref, q_ref)[step // groups]
        levels_at = pl.ds((step % groups) * levels, levels)
        copies.append(pltpu.make_async_copy(ref.at[levels_at], lines_ref.at[step], sems.at[step]))
        copies[-1].start()
    for side in range(2):
        cosine, sine = phases(
            lane_cut(cut_ref), places_ref[side], me.astype(F32), segments, width
        )
        table_ref[2 * side], table_ref[2 * side + 1] = cosine, sine
    every_ref[me] = jnp.zeros(every_ref.shape[1:], F32)

    def cast(step):
        values = lines_ref[step].reshape(lines, width)
        high, low = parts(values)
        high_ref[step % 2] = high
        low_ref[step % 2] = low

    def gather(step):
        both = product(gather_ref[...], high_ref[step % 2], ((1,), (1,)))
        rest = product(gather_ref[:nodes], low_ref[step % 2], ((1,), (1,)))
        held = both[:nodes] + both[nodes:] + rest
        for part in range(lines // LANES):
            node_ref[step * (lines // LANES) + part] = held[:, part * LANES : (part + 1) * LANES]

    def moments(step):
        for part in range(lines // LANES):
            tile = step * (lines // LANES) + part
            mine = node_ref[tile]
            turned = jnp.concatenate([mine * table_ref[0], mine * table_ref[1]], axis=1)
            out = product(moment_ref[...], stacked(turned), ((1,), (0,)))
            ahead, behind = out[:NEAR], out[NEAR : 2 * NEAR]
            inner, outer = jnp.where(even, ahead, behind), jnp.where(even, behind, ahead)
            for ref, mine in ((inner_ref, inner), (outer_ref, outer)):
                ref[tile, :NEAR] = mine[:, :LANES]
                ref[tile, NEAR:] = mine[:, LANES:]
            at = 2 * NEAR
            for s in range(1, segments):
                to = lax.rem(me + s, segments)
                every_ref[to, tile, :FAR] = out[at : at + FAR, :LANES]
                every_ref[to, tile, FAR:] = out[at : at + FAR, LANES:]
                at += FAR

    copies[0].wait()
    cast(0)
    for step in range(steps):
        if step + 1 < steps:
            copies[step + 1].wait()
        gather(step)
        if step + 1 < steps:
            cast(step + 1)
        if step > 0:
            moments(step - 1)
    moments(steps - 1)


def turned_over(values):
    none = jnp.zeros((LANES - EXTRA, LANES), F32)
    return jnp.transpose(jnp.concatenate([values, none], axis=0))


def near_kernel_call(local_ref, table_ref, node_ref, near_ref, turn_ref):
    turn_ref[0] = turned_over(table_ref[2])
    turn_ref[1] = turned_over(table_ref[3])
    for start in range(0, node_ref.shape[0], GROUP):
        columns = []
        for tile in range(start, start + GROUP):
            columns += [node_ref[tile] * table_ref[0], node_ref[tile] * table_ref[1]]
        out = product(local_ref[...], stacked(jnp.concatenate(columns, axis=1)), ((1,), (0,)))
        for tile in range(GROUP):
            at = 2 * tile * LANES
            cosine, sine = out[:, at : at + LANES], out[:, at + LANES : at + 2 * LANES]
            near_ref[start + tile] = turned_over(table_ref[3] * cosine - table_ref[2] * sine)


def combine_kernel(
    per_field, rows, lon_ref, lat_ref, scale_ref, turn_ref, far_ref, inner_ref, outer_ref, every_ref,
    near_in, pack_out, first_ref, second_ref, near_ref, pack_ref, in_sems, out_sems,
):
    tiles, _, wide = near_ref.shape
    segments = every_ref.shape[0]
    even, even_lat = lax.rem(lon_ref[0], 2) == 0, lax.rem(lat_ref[0], 2) == 0
    inverse = 1.0 / scale_ref[...]
    pair = LANES // rows

    def moved(start, source, target, sems):
        at = pl.ds(start, GROUP)
        return pltpu.make_async_copy(source.at[at], target.at[at], sems.at[start // GROUP])

    starts = range(0, tiles, GROUP)
    for start in starts:
        moved(start, near_in, near_ref, in_sems).start()
    for start in starts:
        columns = []
        for tile in range(start, start + GROUP):
            inner, outer = inner_ref[tile], outer_ref[tile]
            pieces = [jnp.where(even, outer, inner), jnp.where(even, inner, outer)]
            pieces += [every_ref[e, tile] for e in range(segments)]
            columns.append(jnp.concatenate(pieces, axis=0))
        got = product(stacked(jnp.concatenate(columns, axis=1)), far_ref[0], ((0,), (0,)))
        moved(start, near_in, near_ref, in_sems).wait()
        for tile in range(start, start + GROUP):
            mine = got[(tile - start) * LANES : (tile - start + 1) * LANES]
            values = near_ref[tile] + turn_ref[1] * mine[:, :wide] - turn_ref[0] * mine[:, wide:]
            pack_ref[tile] = packed(values)
            wind = tile < 2 * per_field
            for part in range(pair):
                line = tile * pair + part
                first, last = part * rows, part * rows + rows - 1
                top, bottom = values[first : first + 1], values[last : last + 1]
                if wind:
                    top, bottom = top * inverse[:, :1], bottom * inverse[:, rows - 1 :]
                first_ref[line : line + 1] = jnp.where(even_lat, bottom, top)
                second_ref[line : line + 1] = jnp.where(even_lat, top, bottom)
        moved(start, pack_ref, pack_out, out_sems).start()
    for start in starts:
        moved(start, pack_ref, pack_out, out_sems).wait()


def early_kernel(early, spread_ref, pack_ref, filtered_ref):
    per_field = pack_ref.shape[0] // 3
    pack = [pack_ref[f * per_field + tile] for tile in range(early) for f in range(3)]
    values = spread_lines(jnp.concatenate(pack, axis=0), spread_ref)
    filtered_ref[...] = values.reshape(filtered_ref.shape)


def finish_kernel(
    lat_ref, scale_ref, spread_ref, first_ref, second_ref, pack_ref, early_ref, tracer_ref, *refs
):
    outs = refs[:3]
    filtered_ref, edge_ref, column_ref, held_ref, load_sems, sems = refs[3:]
    levels, rows, width = tracer_ref.shape
    lanes = spread_ref.shape[1]
    count = first_ref.shape[0]
    pair = LANES // rows
    steps = levels // pair
    early = early_ref.shape[0]
    tracer_slot = 6 * pair

    def load(step):
        return pltpu.make_async_copy(
            tracer_ref.at[pl.ds(step * pair, pair)],
            held_ref.at[pl.ds(tracer_slot + step % 2 * pair, pair)],
            load_sems.at[step % 2],
        )

    def store(step, number):
        return pltpu.make_async_copy(
            held_ref.at[pl.ds((3 * (step % 2) + number) * pair, pair)],
            outs[number].at[pl.ds(step * pair, pair)],
            sems.at[step % 2, number],
        )

    load(0).start()
    even_lat = lax.rem(lat_ref[0], 2) == 0
    first, second = first_ref[...], second_ref[...]
    above, below = jnp.where(even_lat, second, first), jnp.where(even_lat, first, second)
    edges = jnp.concatenate([above, below], axis=0)
    edge_ref[...] = spread_lines(packed(edges), spread_ref)
    here = lax.broadcasted_iota(jnp.int32, (rows, rows), 0)
    there = lax.broadcasted_iota(jnp.int32, (rows, rows), 1)
    column = jnp.where(here == there, jnp.broadcast_to(scale_ref[...], (rows, rows)), 0.0)
    column = jnp.sum(column, axis=1, keepdims=True)
    column_ref[0] = jnp.broadcast_to(column, (rows, LANES))
    column_ref[1] = 1.0 / column_ref[0]
    row_number = lax.broadcasted_iota(jnp.int32, (SUB, 1), 0)

    def fill(step):
        pack = jnp.concatenate([pack_ref[f * steps + step] for f in range(3)], axis=0)
        filtered_ref[step - early] = spread_lines(pack, spread_ref)

    def east_west(values):
        return pltpu.roll(values, lanes - 1, 1) - pltpu.roll(values, 1, 1)

    def stencil(step):
        scale = column_ref[0][:, :1]
        inverse = column_ref[1][:, :1]
        for part in range(pair):
            level = step * pair + part

            def field(number):
                at = number * pair * rows + part * rows
                if step < early:
                    return early_ref[step, at : at + rows]
                return filtered_ref[step - early, at : at + rows]

            def north_south(values, number):
                at = number * levels + level
                above = edge_ref[at : at + 1]
                below = edge_ref[count + at : count + at + 1]
                later, earlier = pltpu.roll(values, rows - 1, 0), pltpu.roll(values, 1, 0)
                low, high = slice(0, SUB), slice(rows - SUB, rows)
                first = later[low] - jnp.where(row_number == 0, above, earlier[low])
                last = jnp.where(row_number == SUB - 1, below, later[high]) - earlier[high]
                inside = slice(SUB, rows - SUB)
                return jnp.concatenate([first, later[inside] - earlier[inside], last], axis=0)

            u, v, q = field(0), field(1), field(2)
            div = scale * (east_west(u) + north_south(v * inverse, 1))
            vort = scale * (east_west(v) - north_south(u * inverse, 0))
            change = u * (courant * scale) * east_west(q) + (courant * v) * north_south(q, 2)
            base = 3 * (step % 2) * pair + part
            held_ref[base] = held_ref[tracer_slot + step % 2 * pair + part] - change[:, :width]
            held_ref[base + pair] = div[:, :width]
            held_ref[base + 2 * pair] = vort[:, :width]

    for step in range(steps):
        if step + 1 < steps:
            load(step + 1).start()
        load(step).wait()
        if step >= 2:
            for number in range(3):
                store(step - 2, number).wait()
        stencil(step)
        if step + early < steps:
            fill(step + early)
        for number in range(3):
            store(step, number).start()
    for step in range(max(steps - 2, 0), steps):
        for number in range(3):
            store(step, number).wait()


def whole_spec():
    return pl.BlockSpec(memory_space=pltpu.VMEM)


def on_device(segments, lats, tables, wind_u, wind_v, tracer, cutoff, row_scale):
    levels, rows, width = wind_u.shape
    gather_table, moment_table, local_table, far_table, spread_table, places = tables
    nodes = gather_table.shape[0] // 2
    lanes = spread_table.shape[1]
    wide = nodes - EXTRA + LANES
    pair = LANES // rows
    group = 2 * pair
    groups = levels // group
    per_field = levels // pair
    tiles = 3 * per_field
    count = 3 * levels
    lon, lat = lax.axis_index("lon").astype(jnp.int32), lax.axis_index("lat").astype(jnp.int32)
    lon, lat = lon[None], lat[None]
    cut = cutoff.reshape(1, rows)
    scale = row_scale.reshape(1, rows)

    smem = pl.BlockSpec(memory_space=pltpu.SMEM)
    anywhere = pl.BlockSpec(memory_space=pl.ANY)
    def limit(mib):
        return pltpu.CompilerParams(vmem_limit_bytes=mib * 1024 * 1024)

    def cost(us):
        return pl.CostEstimate(flops=0, bytes_accessed=us * 3600000, transcendentals=0)

    steps = 3 * groups
    extra = jax.ShapeDtypeStruct((tiles, 2 * NEAR, LANES), F32)
    values, inner, outer, every, table = pl.pallas_call(
        functools.partial(analyse_kernel, segments, groups),
        out_shape=(
            jax.ShapeDtypeStruct((tiles, nodes, LANES), F32),
            extra,
            extra,
            jax.ShapeDtypeStruct((segments, tiles, 2 * FAR, LANES), F32),
            jax.ShapeDtypeStruct((4, nodes, LANES), F32),
        ),
        in_specs=[smem] + [whole_spec()] * 4 + [anywhere] * 3,
        out_specs=(whole_spec(),) * 5,
        scratch_shapes=[
            pltpu.VMEM((steps, group, rows, width), F32),
            pltpu.VMEM((2, group * rows, width), BF),
            pltpu.VMEM((2, group * rows, width), BF),
            pltpu.SemaphoreType.DMA((steps,)),
        ],
        compiler_params=limit(56),
        cost_estimate=cost(12),
        name="analyse",
    )(lon, cut, places, gather_table, moment_table, wind_u, wind_v, tracer)

    def swapped(array, axis, start, closed):
        size = segments if axis == "lon" else lats
        pairs = [(i, (i + 1) % size) for i in range(start, size if closed else size - 1, 2)]
        return lax.ppermute(array, axis, pairs + [(b, a) for a, b in pairs])

    every = lax.all_to_all(every, "lon", 0, 0)
    inner, outer = swapped(inner, "lon", 0, True), swapped(outer, "lon", 1, True)

    near, turn = pl.pallas_call(
        near_kernel_call,
        out_shape=(
            jax.ShapeDtypeStruct((tiles, LANES, wide), F32),
            jax.ShapeDtypeStruct((2, LANES, wide), F32),
        ),
        in_specs=[whole_spec()] * 3,
        out_specs=(whole_spec(),) * 2,
        compiler_params=limit(56),
        cost_estimate=cost(6),
        name="near",
    )(local_table, table, values)

    edge = jax.ShapeDtypeStruct((count, wide), F32)
    pack, first, second = pl.pallas_call(
        functools.partial(combine_kernel, per_field, rows),
        out_shape=(jax.ShapeDtypeStruct((tiles, LANES, 2 * wide - LANES), BF), edge, edge),
        grid_spec=pltpu.PrefetchScalarGridSpec(
            num_scalar_prefetch=2,
            grid=(1,),
            in_specs=[whole_spec()] * 2
            + [pl.BlockSpec((1,) + far_table.shape[1:], lambda s, d, e: (d[0], 0, 0))]
            + [whole_spec()] * 3
            + [anywhere],
            out_specs=(anywhere, whole_spec(), whole_spec()),
            scratch_shapes=[
                pltpu.VMEM((tiles, LANES, wide), F32),
                pltpu.VMEM((tiles, LANES, 2 * wide - LANES), BF),
                pltpu.SemaphoreType.DMA((tiles // GROUP,)),
                pltpu.SemaphoreType.DMA((tiles // GROUP,)),
            ],
        ),
        compiler_params=limit(56),
        cost_estimate=cost(4),
        name="combine",
    )(lon, lat, scale, turn, far_table, inner, outer, every, near)

    first, second = swapped(first, "lat", 0, False), swapped(second, "lat", 1, False)

    early = per_field // 2
    filtered = pl.pallas_call(
        functools.partial(early_kernel, early),
        out_shape=jax.ShapeDtypeStruct((early, 3 * LANES, lanes), F32),
        in_specs=[whole_spec()] * 2,
        out_specs=whole_spec(),
        compiler_params=limit(24),
        cost_estimate=cost(4),
        name="early",
    )(spread_table, pack)

    return pl.pallas_call(
        finish_kernel,
        out_shape=(jax.ShapeDtypeStruct((levels, rows, width), F32),) * 3,
        in_specs=[smem] + [whole_spec()] * 6 + [anywhere],
        out_specs=(anywhere,) * 3,
        scratch_shapes=[
            pltpu.VMEM((per_field - early, 3 * LANES, lanes), F32),
            pltpu.VMEM((2 * count, lanes), F32),
            pltpu.VMEM((2, rows, LANES), F32),
            pltpu.VMEM((8 * pair, rows, width), F32),
            pltpu.SemaphoreType.DMA((2,)),
            pltpu.SemaphoreType.DMA((2, 3)),
        ],
        compiler_params=limit(32),
        cost_estimate=cost(10),
        name="finish",
    )(lat, scale, spread_table, first, second, pack, filtered, tracer)


def solution(mesh):
    segments, lats = mesh.shape["lon"], mesh.shape["lat"]
    tables = tuple(make_tables(NLON // segments, segments))
    line = P(None, "lat", "lon")
    return jax.shard_map(
        functools.partial(on_device, segments, lats, tables),
        mesh=mesh,
        in_specs=(line, line, line, P("lat"), P("lat")),
        out_specs=(line, line, line),
        check_vma=False,
    )
```

```python
import functools
import math

import jax
import jax.numpy as jnp
import ml_dtypes
import numpy as np
from jax import lax
from jax.experimental import pallas as pl
from jax.experimental.pallas import tpu as pltpu
from jax.sharding import PartitionSpec as P

NLON = 12000
KMAX = 1024
NEAR = 12
FAR = 4
EXTRA = 32
LANES = 128
SUB = 8
GROUP = 4
courant = 0.5
BF = jnp.bfloat16
F32 = jnp.float32


def prolate(points, band, count):
    i = np.arange(points)
    diag = ((points - 1 - 2 * i) / 2.0) ** 2 * np.cos(2 * np.pi * band)
    off = i[1:] * (points - i[1:]) / 2.0
    mid = points // 2
    half = (count + 1) // 2
    out = np.zeros((points, 2 * half))
    dd, ee = diag[mid:], off[mid:].copy()
    scaled = ee.copy()
    scaled[0] *= math.sqrt(2.0)
    even = np.linalg.eigh(np.diag(dd) + np.diag(scaled, 1) + np.diag(scaled, -1))[1]
    even = even[:, ::-1][:, :half]
    wing = even[1:] / math.sqrt(2.0)
    out[mid, 0::2] = even[0]
    out[mid + 1 :, 0::2] = wing
    out[:mid, 0::2] = wing[::-1]
    odd = np.linalg.eigh(np.diag(dd[1:]) + np.diag(ee[1:], 1) + np.diag(ee[1:], -1))[1]
    wing = odd[:, ::-1][:, :half] / math.sqrt(2.0)
    out[mid + 1 :, 1::2] = wing
    out[:mid, 1::2] = -wing[::-1]
    return out


def interpolation(low, high, nodes, snap):
    fine = prolate(2 * (high - low) + 1, (KMAX - 0.5) / NLON / 2, nodes + 2)
    wave = fine[:, nodes]
    at = np.nonzero(wave[:-1] * wave[1:] < 0)[0]
    roots = (at + wave[at] / (wave[at] - wave[at + 1]))[: nodes // 2] / 2 + low
    left = snap(roots)
    for i in range(1, len(left)):
        left[i] = max(left[i], left[i - 1] + 1)
    places = np.concatenate([left, (low + high) - left[::-1]])
    kept = nodes - 4
    index = np.round((places - low) * 2).astype(int)
    return places, fine[::2, :kept] @ np.linalg.pinv(fine[index, :kept])


def near_kernel(distance):
    return 1.0 / (NLON * np.sin(np.pi * distance / NLON))


def two_parts(table):
    high = table.astype(np.float32).astype(ml_dtypes.bfloat16)
    low = (table - high.astype(np.float64)).astype(np.float32).astype(ml_dtypes.bfloat16)
    return high, low


@functools.lru_cache(maxsize=4)
def make_tables(width, segments):
    main = -(-2 * KMAX * width // NLON // LANES) * LANES
    nodes = main + EXTRA
    source, gather = interpolation(0, width - 1, nodes, np.round)
    target, spread = interpolation(-1, width, nodes, lambda r: np.floor(r) + 0.5)
    local = near_kernel(target[:, None] - source[None])
    offsets = [d for d in range(-(segments - 1), segments) if d]
    far = {d: near_kernel(target[:, None] + width * d - source[None]) for d in offsets}

    def leading(kernel, count):
        found = np.linalg.svd(kernel, full_matrices=False)[2][:count]
        peak = np.take_along_axis(found, np.abs(found).argmax(1)[:, None], 1)
        return found * np.sign(peak)

    ahead = range(1, segments)
    basis = {s: leading(far[s], FAR) for s in ahead}
    for s in (1, segments - 1):
        both = leading(far[s], FAR + NEAR)
        basis[s], basis[-s] = both[:FAR], both[FAR:]

    high, low = two_parts(gather.T)
    gather_table = np.concatenate([high, low], 0)
    more = [basis[-1], basis[1 - segments]] + [basis[s] for s in ahead]
    rows = np.concatenate(more, 0)
    rows = np.pad(rows, ((0, -len(rows) % 8), (0, 0)))
    high, low = two_parts(rows)
    moment_table = np.concatenate([high, low, high], 1)
    high, low = two_parts(local)
    local_table = np.concatenate([high, low, high], 1)
    blocks = []
    for d in range(segments):
        pieces = [far[d - (d - s) % segments] @ basis[-s].T for s in (1, segments - 1)]
        for e in range(segments):
            if e == d:
                pieces.append(np.zeros((nodes, FAR)))
            else:
                pieces.append(far[d - e] @ basis[(d - e) % segments].T)
        pieces = [np.pad(piece, ((0, main + LANES - nodes), (0, 0))).T for piece in pieces]
        left = [p for piece in pieces for p in (piece, 0 * piece)]
        right = [p for piece in pieces for p in (0 * piece, piece)]
        both = np.concatenate([np.concatenate(left, 0), np.concatenate(right, 0)], 1)
        high, low = two_parts(both)
        blocks.append(np.concatenate([high, low, high], 0))
    far_table = np.stack(blocks)
    lanes = -(-(width + 2) // LANES) * LANES
    wide = np.zeros((nodes, lanes))
    wide[:, : width + 1] = spread.T[:, 1:]
    wide[:, lanes - 1] = spread.T[:, 0]
    high, low = two_parts(wide)
    none = np.zeros((LANES - 3 * EXTRA, lanes), high.dtype)
    spread_table = np.concatenate(
        [high[:main], low[:main], high[:main], high[main:], low[main:], high[main:], none], 0
    )
    places = np.stack([2 * source - width, 2 * target - width]).astype(np.float32)
    return gather_table, moment_table, local_table, far_table, spread_table, places[:, :, None]


def phases(cut, places, device, segments, width):
    full = 4.0 * NLON
    odd = 2.0 * cut - 1.0
    inner = odd * places
    inner = inner - full * jnp.floor(inner * (1.0 / full) + 0.5)
    base = odd * (2.0 * device + 1.0)
    cycle = 4.0 * segments
    base = (base - cycle * jnp.floor(base * (1.0 / cycle))) * float(width)
    total = inner + base
    total = total - full * jnp.floor(total * (1.0 / full) + 0.5)
    quarter = jnp.floor(total * (4.0 / full) + 0.5)
    x = (total - (full / 4.0) * quarter) * (2.0 * math.pi / full)
    y = x * x
    sine = x + x * y * (
        -1.0 / 6 + y * (1.0 / 120 + y * (-1.0 / 5040 + y * (1.0 / 362880)))
    )
    cosine = 1.0 + y * (
        -0.5 + y * (1.0 / 24 + y * (-1.0 / 720 + y * (1.0 / 40320 + y * (-1.0 / 3628800))))
    )
    odd_quarter = jnp.abs(quarter) == 1.0
    turned_c = jnp.where(odd_quarter, -quarter * sine, cosine)
    turned_s = jnp.where(odd_quarter, quarter * cosine, sine)
    flip = jnp.where(jnp.abs(quarter) == 2.0, -1.0, 1.0)
    return turned_c * flip, turned_s * flip


def parts(values):
    high = values.astype(BF)
    return high, (values - high.astype(F32)).astype(BF)


def stacked(values):
    high, low = parts(values)
    return jnp.concatenate([high, high, low], axis=0)


def product(a, b, dims):
    return lax.dot_general(a, b, (dims, ((), ())), preferred_element_type=F32)


def lane_cut(cut_ref):
    cut = cut_ref[...].astype(F32)
    return jnp.concatenate([cut] * (LANES // cut.shape[1]), axis=1)


def packed(values):
    main = values.shape[1] - LANES
    high, low = parts(values)
    last, last_low = high[:, main:].astype(F32), low[:, main:].astype(F32)
    last = last + pltpu.roll(last, EXTRA, 1) + pltpu.roll(last_low, 2 * EXTRA, 1)
    return jnp.concatenate([high[:, :main], low[:, :main], last.astype(BF)], axis=1)


def spread_lines(pack, spread_ref):
    main = (pack.shape[1] - LANES) // 2
    held = jnp.concatenate([pack[:, :main], pack], axis=1)
    return product(held, spread_ref[...], ((1,), (0,)))


def analyse_kernel(
    segments, groups, cut_ref, places_ref, gather_ref, moment_ref,
    u_ref, v_ref, q_ref, node_ref, inner_ref, outer_ref, every_ref, table_ref,
    lines_ref, high_ref, low_ref, sems,
):
    width = u_ref.shape[2]
    steps, levels, rows, _ = lines_ref.shape
    lines = levels * rows
    nodes = gather_ref.shape[0] // 2
    me = lax.axis_index("lon")
    even = lax.rem(me, 2) == 0

    copies = []
    for step in range(steps):
        ref = (u_ref, v_ref, q_ref)[step // groups]
        levels_at = pl.ds((step % groups) * levels, levels)
        copies.append(pltpu.make_async_copy(ref.at[levels_at], lines_ref.at[step], sems.at[step]))
        copies[-1].start()
    for side in range(2):
        cosine, sine = phases(
            lane_cut(cut_ref), places_ref[side], me.astype(F32), segments, width
        )
        table_ref[2 * side], table_ref[2 * side + 1] = cosine, sine
    every_ref[me] = jnp.zeros(every_ref.shape[1:], F32)

    def cast(step):
        values = lines_ref[step].reshape(lines, width)
        high, low = parts(values)
        high_ref[step % 2] = high
        low_ref[step % 2] = low

    def gather(step):
        both = product(gather_ref[...], high_ref[step % 2], ((1,), (1,)))
        rest = product(gather_ref[:nodes], low_ref[step % 2], ((1,), (1,)))
        held = both[:nodes] + both[nodes:] + rest
        for part in range(lines // LANES):
            node_ref[step * (lines // LANES) + part] = held[:, part * LANES : (part + 1) * LANES]

    def moments(step):
        for part in range(lines // LANES):
            tile = step * (lines // LANES) + part
            mine = node_ref[tile]
            turned = jnp.concatenate([mine * table_ref[0], mine * table_ref[1]], axis=1)
            out = product(moment_ref[...], stacked(turned), ((1,), (0,)))
            ahead, behind = out[:NEAR], out[NEAR : 2 * NEAR]
            inner, outer = jnp.where(even, ahead, behind), jnp.where(even, behind, ahead)
            for ref, mine in ((inner_ref, inner), (outer_ref, outer)):
                ref[tile, :NEAR] = mine[:, :LANES]
                ref[tile, NEAR:] = mine[:, LANES:]
            at = 2 * NEAR
            for s in range(1, segments):
                to = lax.rem(me + s, segments)
                every_ref[to, tile, :FAR] = out[at : at + FAR, :LANES]
                every_ref[to, tile, FAR:] = out[at : at + FAR, LANES:]
                at += FAR

    copies[0].wait()
    cast(0)
    for step in range(steps):
        if step + 1 < steps:
            copies[step + 1].wait()
        gather(step)
        if step + 1 < steps:
            cast(step + 1)
        if step > 0:
            moments(step - 1)
    moments(steps - 1)


def turned_over(values):
    none = jnp.zeros((LANES - EXTRA, LANES), F32)
    return jnp.transpose(jnp.concatenate([values, none], axis=0))


def near_kernel_call(local_ref, table_ref, node_ref, near_ref):
    tiles = node_ref.shape[0]
    near_ref[tiles] = turned_over(table_ref[2])
    near_ref[tiles + 1] = turned_over(table_ref[3])
    for start in range(0, node_ref.shape[0], GROUP):
        columns = []
        for tile in range(start, start + GROUP):
            columns += [node_ref[tile] * table_ref[0], node_ref[tile] * table_ref[1]]
        out = product(local_ref[...], stacked(jnp.concatenate(columns, axis=1)), ((1,), (0,)))
        for tile in range(GROUP):
            at = 2 * tile * LANES
            cosine, sine = out[:, at : at + LANES], out[:, at + LANES : at + 2 * LANES]
            near_ref[start + tile] = turned_over(table_ref[3] * cosine - table_ref[2] * sine)


def combine_kernel(
    per_field, rows, scale_ref, far_ref, near_ref, inner_ref, outer_ref,
    every_ref, pack_ref, first_ref, second_ref,
):
    segments, tiles = every_ref.shape[:2]
    wide = near_ref.shape[2]
    even = lax.rem(lax.axis_index("lon"), 2) == 0
    even_lat = lax.rem(lax.axis_index("lat"), 2) == 0
    inverse = 1.0 / scale_ref[...]
    pair = LANES // rows
    for start in range(0, tiles, GROUP):
        columns = []
        for tile in range(start, start + GROUP):
            inner, outer = inner_ref[tile], outer_ref[tile]
            pieces = [jnp.where(even, outer, inner), jnp.where(even, inner, outer)]
            pieces += [every_ref[e, tile] for e in range(segments)]
            columns.append(jnp.concatenate(pieces, axis=0))
        got = product(stacked(jnp.concatenate(columns, axis=1)), far_ref[...], ((0,), (0,)))
        for tile in range(start, start + GROUP):
            mine = got[(tile - start) * LANES : (tile - start + 1) * LANES]
            values = near_ref[tile] + near_ref[tiles + 1] * mine[:, :wide]
            values = values - near_ref[tiles] * mine[:, wide:]
            pack_ref[tile] = packed(values)
            wind = tile < 2 * per_field
            for part in range(pair):
                line = tile * pair + part
                first, last = part * rows, part * rows + rows - 1
                top, bottom = values[first : first + 1], values[last : last + 1]
                if wind:
                    top, bottom = top * inverse[:, :1], bottom * inverse[:, rows - 1 :]
                first_ref[line : line + 1] = jnp.where(even_lat, bottom, top)
                second_ref[line : line + 1] = jnp.where(even_lat, top, bottom)


def early_kernel(early, spread_ref, pack_ref, filtered_ref):
    per_field = pack_ref.shape[0] // 3
    pack = [pack_ref[f * per_field + tile] for tile in range(early) for f in range(3)]
    values = spread_lines(jnp.concatenate(pack, axis=0), spread_ref)
    filtered_ref[...] = values.reshape(filtered_ref.shape)


def finish_kernel(
    scale_ref, spread_ref, first_ref, second_ref, pack_ref, early_ref, tracer_ref, *refs
):
    outs = refs[:3]
    filtered_ref, edge_ref, column_ref, held_ref, load_sems, sems = refs[3:]
    levels, rows, width = tracer_ref.shape
    lanes = spread_ref.shape[1]
    count = first_ref.shape[0]
    pair = LANES // rows
    steps = levels // pair
    early = early_ref.shape[0]
    tracer_slot = 6 * pair

    def load(step):
        return pltpu.make_async_copy(
            tracer_ref.at[pl.ds(step * pair, pair)],
            held_ref.at[pl.ds(tracer_slot + step % 2 * pair, pair)],
            load_sems.at[step % 2],
        )

    def store(step, number):
        return pltpu.make_async_copy(
            held_ref.at[pl.ds((3 * (step % 2) + number) * pair, pair)],
            outs[number].at[pl.ds(step * pair, pair)],
            sems.at[step % 2, number],
        )

    load(0).start()
    even_lat = lax.rem(lax.axis_index("lat"), 2) == 0
    first, second = first_ref[...], second_ref[...]
    above, below = jnp.where(even_lat, second, first), jnp.where(even_lat, first, second)
    edges = jnp.concatenate([above, below], axis=0)
    edge_ref[...] = spread_lines(packed(edges), spread_ref)
    here = lax.broadcasted_iota(jnp.int32, (rows, rows), 0)
    there = lax.broadcasted_iota(jnp.int32, (rows, rows), 1)
    column = jnp.where(here == there, jnp.broadcast_to(scale_ref[...], (rows, rows)), 0.0)
    column = jnp.sum(column, axis=1, keepdims=True)
    column_ref[0] = jnp.broadcast_to(column, (rows, LANES))
    column_ref[1] = 1.0 / column_ref[0]
    row_number = lax.broadcasted_iota(jnp.int32, (SUB, 1), 0)

    def fill(step):
        pack = jnp.concatenate([pack_ref[f * steps + step] for f in range(3)], axis=0)
        filtered_ref[step - early] = spread_lines(pack, spread_ref)

    def east_west(values):
        return pltpu.roll(values, lanes - 1, 1) - pltpu.roll(values, 1, 1)

    def stencil(step):
        scale = column_ref[0][:, :1]
        inverse = column_ref[1][:, :1]
        for part in range(pair):
            level = step * pair + part

            def field(number):
                at = number * pair * rows + part * rows
                if step < early:
                    return early_ref[step, at : at + rows]
                return filtered_ref[step - early, at : at + rows]

            def north_south(values, number):
                at = number * levels + level
                above = edge_ref[at : at + 1]
                below = edge_ref[count + at : count + at + 1]
                later, earlier = pltpu.roll(values, rows - 1, 0), pltpu.roll(values, 1, 0)
                low, high = slice(0, SUB), slice(rows - SUB, rows)
                first = later[low] - jnp.where(row_number == 0, above, earlier[low])
                last = jnp.where(row_number == SUB - 1, below, later[high]) - earlier[high]
                inside = slice(SUB, rows - SUB)
                return jnp.concatenate([first, later[inside] - earlier[inside], last], axis=0)

            u, v, q = field(0), field(1), field(2)
            div = scale * (east_west(u) + north_south(v * inverse, 1))
            vort = scale * (east_west(v) - north_south(u * inverse, 0))
            change = u * (courant * scale) * east_west(q) + (courant * v) * north_south(q, 2)
            base = 3 * (step % 2) * pair + part
            held_ref[base] = held_ref[tracer_slot + step % 2 * pair + part] - change[:, :width]
            held_ref[base + pair] = div[:, :width]
            held_ref[base + 2 * pair] = vort[:, :width]

    for step in range(steps):
        if step + 1 < steps:
            load(step + 1).start()
        load(step).wait()
        if step >= 2:
            for number in range(3):
                store(step - 2, number).wait()
        stencil(step)
        if step + early < steps:
            fill(step + early)
        for number in range(3):
            store(step, number).start()
    for step in range(max(steps - 2, 0), steps):
        for number in range(3):
            store(step, number).wait()


def whole_spec():
    return pl.BlockSpec(memory_space=pltpu.VMEM)


def on_device(segments, lats, tables, wind_u, wind_v, tracer, cutoff, row_scale):
    levels, rows, width = wind_u.shape
    gather_table, moment_table, local_table, far_table, spread_table, places = tables
    nodes = gather_table.shape[0] // 2
    lanes = spread_table.shape[1]
    wide = nodes - EXTRA + LANES
    pair = LANES // rows
    group = 2 * pair
    groups = levels // group
    per_field = levels // pair
    tiles = 3 * per_field
    count = 3 * levels
    lon = lax.axis_index("lon").astype(jnp.int32)
    cut = cutoff.reshape(1, rows)
    scale = row_scale.reshape(1, rows)

    anywhere = pl.BlockSpec(memory_space=pl.ANY)
    def limit(mib):
        return pltpu.CompilerParams(vmem_limit_bytes=mib * 1024 * 1024)

    def cost(us):
        return pl.CostEstimate(flops=0, bytes_accessed=us * 3600000, transcendentals=0)

    steps = 3 * groups
    extra = jax.ShapeDtypeStruct((tiles, 2 * NEAR, LANES), F32)
    values, inner, outer, every, table = pl.pallas_call(
        functools.partial(analyse_kernel, segments, groups),
        out_shape=(
            jax.ShapeDtypeStruct((tiles, nodes, LANES), F32),
            extra,
            extra,
            jax.ShapeDtypeStruct((segments, tiles, 2 * FAR, LANES), F32),
            jax.ShapeDtypeStruct((4, nodes, LANES), F32),
        ),
        in_specs=[whole_spec()] * 4 + [anywhere] * 3,
        out_specs=(whole_spec(),) * 5,
        scratch_shapes=[
            pltpu.VMEM((steps, group, rows, width), F32),
            pltpu.VMEM((2, group * rows, width), BF),
            pltpu.VMEM((2, group * rows, width), BF),
            pltpu.SemaphoreType.DMA((steps,)),
        ],
        compiler_params=limit(56),
        cost_estimate=cost(12),
        name="analyse",
    )(cut, places, gather_table, moment_table, wind_u, wind_v, tracer)

    def swapped(array, axis, start, closed):
        size = segments if axis == "lon" else lats
        pairs = [(i, (i + 1) % size) for i in range(start, size if closed else size - 1, 2)]
        return lax.ppermute(array, axis, pairs + [(b, a) for a, b in pairs])

    every = lax.all_to_all(every, "lon", 0, 0)
    inner, outer = swapped(inner, "lon", 0, True), swapped(outer, "lon", 1, True)
    far_mine = lax.dynamic_index_in_dim(jnp.asarray(far_table), lon, 0, False)

    near = pl.pallas_call(
        near_kernel_call,
        out_shape=jax.ShapeDtypeStruct((tiles + 2, LANES, wide), F32),
        in_specs=[whole_spec()] * 3,
        out_specs=whole_spec(),
        compiler_params=limit(24),
        cost_estimate=cost(6),
        name="near",
    )(local_table, table, values)

    edge = jax.ShapeDtypeStruct((count, wide), F32)
    pack, first, second = pl.pallas_call(
        functools.partial(combine_kernel, per_field, rows),
        out_shape=(jax.ShapeDtypeStruct((tiles, LANES, 2 * wide - LANES), BF), edge, edge),
        in_specs=[whole_spec()] * 6,
        out_specs=(whole_spec(),) * 3,
        compiler_params=limit(24),
        cost_estimate=cost(4),
        name="combine",
    )(scale, far_mine, near, inner, outer, every)

    first, second = swapped(first, "lat", 0, False), swapped(second, "lat", 1, False)

    early = per_field // 2
    filtered = pl.pallas_call(
        functools.partial(early_kernel, early),
        out_shape=jax.ShapeDtypeStruct((early, 3 * LANES, lanes), F32),
        in_specs=[whole_spec()] * 2,
        out_specs=whole_spec(),
        compiler_params=limit(24),
        cost_estimate=cost(4),
        name="early",
    )(spread_table, pack)

    return pl.pallas_call(
        finish_kernel,
        out_shape=(jax.ShapeDtypeStruct((levels, rows, width), F32),) * 3,
        in_specs=[whole_spec()] * 6 + [anywhere],
        out_specs=(anywhere,) * 3,
        scratch_shapes=[
            pltpu.VMEM((per_field - early, 3 * LANES, lanes), F32),
            pltpu.VMEM((2 * count, lanes), F32),
            pltpu.VMEM((2, rows, LANES), F32),
            pltpu.VMEM((8 * pair, rows, width), F32),
            pltpu.SemaphoreType.DMA((2,)),
            pltpu.SemaphoreType.DMA((2, 3)),
        ],
        compiler_params=limit(32),
        cost_estimate=cost(10),
        name="finish",
    )(scale, spread_table, first, second, pack, filtered, tracer)


def solution(mesh):
    segments, lats = mesh.shape["lon"], mesh.shape["lat"]
    tables = tuple(make_tables(NLON // segments, segments))
    line = P(None, "lat", "lon")
    return jax.shard_map(
        functools.partial(on_device, segments, lats, tables),
        mesh=mesh,
        in_specs=(line, line, line, P("lat"), P("lat")),
        out_specs=(line, line, line),
        check_vma=False,
    )
```

```python
import functools
import math

import jax
import jax.numpy as jnp
import ml_dtypes
import numpy as np
from jax import lax
from jax.experimental import pallas as pl
from jax.experimental.pallas import tpu as pltpu
from jax.sharding import PartitionSpec as P

NLON = 12000
KMAX = 1024
NEAR = 12
FAR = 4
EXTRA = 32
LANES = 128
SUB = 8
GROUP = 4
courant = 0.5
BF = jnp.bfloat16
F32 = jnp.float32


def prolate(points, band, count):
    i = np.arange(points)
    diag = ((points - 1 - 2 * i) / 2.0) ** 2 * np.cos(2 * np.pi * band)
    off = i[1:] * (points - i[1:]) / 2.0
    mid = points // 2
    half = (count + 1) // 2
    out = np.zeros((points, 2 * half))
    dd, ee = diag[mid:], off[mid:].copy()
    scaled = ee.copy()
    scaled[0] *= math.sqrt(2.0)
    even = np.linalg.eigh(np.diag(dd) + np.diag(scaled, 1) + np.diag(scaled, -1))[1]
    even = even[:, ::-1][:, :half]
    wing = even[1:] / math.sqrt(2.0)
    out[mid, 0::2] = even[0]
    out[mid + 1 :, 0::2] = wing
    out[:mid, 0::2] = wing[::-1]
    odd = np.linalg.eigh(np.diag(dd[1:]) + np.diag(ee[1:], 1) + np.diag(ee[1:], -1))[1]
    wing = odd[:, ::-1][:, :half] / math.sqrt(2.0)
    out[mid + 1 :, 1::2] = wing
    out[:mid, 1::2] = -wing[::-1]
    return out


def interpolation(low, high, nodes, snap):
    fine = prolate(2 * (high - low) + 1, (KMAX - 0.5) / NLON / 2, nodes + 2)
    wave = fine[:, nodes]
    at = np.nonzero(wave[:-1] * wave[1:] < 0)[0]
    roots = (at + wave[at] / (wave[at] - wave[at + 1]))[: nodes // 2] / 2 + low
    left = snap(roots)
    for i in range(1, len(left)):
        left[i] = max(left[i], left[i - 1] + 1)
    places = np.concatenate([left, (low + high) - left[::-1]])
    kept = nodes - 4
    index = np.round((places - low) * 2).astype(int)
    return places, fine[::2, :kept] @ np.linalg.pinv(fine[index, :kept])


def near_kernel(distance):
    return 1.0 / (NLON * np.sin(np.pi * distance / NLON))


def two_parts(table):
    high = table.astype(np.float32).astype(ml_dtypes.bfloat16)
    low = (table - high.astype(np.float64)).astype(np.float32).astype(ml_dtypes.bfloat16)
    return high, low


@functools.lru_cache(maxsize=4)
def make_tables(width, segments):
    main = -(-2 * KMAX * width // NLON // LANES) * LANES
    nodes = main + EXTRA
    source, gather = interpolation(0, width - 1, nodes, np.round)
    target, spread = interpolation(-1, width, nodes, lambda r: np.floor(r) + 0.5)
    local = near_kernel(target[:, None] - source[None])
    offsets = [d for d in range(-(segments - 1), segments) if d]
    far = {d: near_kernel(target[:, None] + width * d - source[None]) for d in offsets}

    def leading(kernel, count):
        found = np.linalg.svd(kernel, full_matrices=False)[2][:count]
        peak = np.take_along_axis(found, np.abs(found).argmax(1)[:, None], 1)
        return found * np.sign(peak)

    ahead = range(1, segments)
    basis = {s: leading(far[s], FAR) for s in ahead}
    for s in (1, segments - 1):
        both = leading(far[s], FAR + NEAR)
        basis[s], basis[-s] = both[:FAR], both[FAR:]

    high, low = two_parts(gather.T)
    gather_table = np.concatenate([high, low], 0)
    more = [basis[-1], basis[1 - segments]] + [basis[s] for s in ahead]
    rows = np.concatenate(more, 0)
    rows = np.pad(rows, ((0, -len(rows) % 8), (0, 0)))
    high, low = two_parts(rows)
    moment_table = np.concatenate([high, low, high], 1)
    high, low = two_parts(local)
    local_table = np.concatenate([high, low, high], 1)
    blocks = []
    for d in range(segments):
        order = (segments - 1, 1) if d % 2 == 0 else (1, segments - 1)
        pieces = [far[d - (d - s) % segments] @ basis[-s].T for s in order]
        for e in range(segments):
            if e == d:
                pieces.append(np.zeros((nodes, FAR)))
            else:
                pieces.append(far[d - e] @ basis[(d - e) % segments].T)
        pieces = [np.pad(piece, ((0, main + LANES - nodes), (0, 0))).T for piece in pieces]
        left = [p for piece in pieces for p in (piece, 0 * piece)]
        right = [p for piece in pieces for p in (0 * piece, piece)]
        both = np.concatenate([np.concatenate(left, 0), np.concatenate(right, 0)], 1)
        high, low = two_parts(both)
        blocks.append(np.concatenate([high, low, high], 0))
    far_table = np.stack(blocks)
    lanes = -(-(width + 2) // LANES) * LANES
    wide = np.zeros((nodes, lanes))
    wide[:, : width + 1] = spread.T[:, 1:]
    wide[:, lanes - 1] = spread.T[:, 0]
    high, low = two_parts(wide)
    none = np.zeros((LANES - 3 * EXTRA, lanes), high.dtype)
    spread_table = np.concatenate(
        [high[:main], low[:main], high[:main], high[main:], low[main:], high[main:], none], 0
    )
    places = np.stack([2 * source - width, 2 * target - width]).astype(np.float32)
    return gather_table, moment_table, local_table, far_table, spread_table, places[:, :, None]


def phases(cut, places, device, segments, width):
    full = 4.0 * NLON
    odd = 2.0 * cut - 1.0
    inner = odd * places
    inner = inner - full * jnp.floor(inner * (1.0 / full) + 0.5)
    base = odd * (2.0 * device + 1.0)
    cycle = 4.0 * segments
    base = (base - cycle * jnp.floor(base * (1.0 / cycle))) * float(width)
    total = inner + base
    total = total - full * jnp.floor(total * (1.0 / full) + 0.5)
    quarter = jnp.floor(total * (4.0 / full) + 0.5)
    x = (total - (full / 4.0) * quarter) * (2.0 * math.pi / full)
    y = x * x
    sine = x + x * y * (
        -1.0 / 6 + y * (1.0 / 120 + y * (-1.0 / 5040 + y * (1.0 / 362880)))
    )
    cosine = 1.0 + y * (
        -0.5 + y * (1.0 / 24 + y * (-1.0 / 720 + y * (1.0 / 40320 + y * (-1.0 / 3628800))))
    )
    odd_quarter = jnp.abs(quarter) == 1.0
    turned_c = jnp.where(odd_quarter, -quarter * sine, cosine)
    turned_s = jnp.where(odd_quarter, quarter * cosine, sine)
    flip = jnp.where(jnp.abs(quarter) == 2.0, -1.0, 1.0)
    return turned_c * flip, turned_s * flip


def parts(values):
    high = values.astype(BF)
    return high, (values - high.astype(F32)).astype(BF)


def stacked(values):
    high, low = parts(values)
    return jnp.concatenate([high, high, low], axis=0)


def product(a, b, dims):
    return lax.dot_general(a, b, (dims, ((), ())), preferred_element_type=F32)


def lane_cut(cut_ref):
    cut = cut_ref[...].astype(F32)
    return jnp.concatenate([cut] * (LANES // cut.shape[1]), axis=1)


def packed(values):
    main = values.shape[1] - LANES
    high, low = parts(values)
    last, last_low = high[:, main:].astype(F32), low[:, main:].astype(F32)
    last = last + pltpu.roll(last, EXTRA, 1) + pltpu.roll(last_low, 2 * EXTRA, 1)
    return jnp.concatenate([high[:, :main], low[:, :main], last.astype(BF)], axis=1)


def spread_lines(pack, spread_ref):
    main = (pack.shape[1] - LANES) // 2
    held = jnp.concatenate([pack[:, :main], pack], axis=1)
    return product(held, spread_ref[...], ((1,), (0,)))


def analyse_kernel(
    segments, groups, cut_ref, places_ref, gather_ref, moment_ref,
    u_ref, v_ref, q_ref, node_ref, inner_ref, outer_ref, every_ref, table_ref,
    lines_ref, high_ref, low_ref, sems,
):
    width = u_ref.shape[2]
    steps, levels, rows, _ = lines_ref.shape
    lines = levels * rows
    nodes = gather_ref.shape[0] // 2
    me = lax.axis_index("lon")
    even = lax.rem(me, 2) == 0

    copies = []
    for step in range(steps):
        ref = (u_ref, v_ref, q_ref)[step // groups]
        levels_at = pl.ds((step % groups) * levels, levels)
        copies.append(pltpu.make_async_copy(ref.at[levels_at], lines_ref.at[step], sems.at[step]))
        copies[-1].start()
    for side in range(2):
        cosine, sine = phases(
            lane_cut(cut_ref), places_ref[side], me.astype(F32), segments, width
        )
        table_ref[2 * side], table_ref[2 * side + 1] = cosine, sine
    every_ref[me] = jnp.zeros(every_ref.shape[1:], F32)

    def cast(step):
        values = lines_ref[step].reshape(lines, width)
        high, low = parts(values)
        high_ref[step % 2] = high
        low_ref[step % 2] = low

    def gather(step):
        both = product(gather_ref[...], high_ref[step % 2], ((1,), (1,)))
        rest = product(gather_ref[:nodes], low_ref[step % 2], ((1,), (1,)))
        held = both[:nodes] + both[nodes:] + rest
        for part in range(lines // LANES):
            node_ref[step * (lines // LANES) + part] = held[:, part * LANES : (part + 1) * LANES]

    def moments(step):
        for part in range(lines // LANES):
            tile = step * (lines // LANES) + part
            mine = node_ref[tile]
            turned = jnp.concatenate([mine * table_ref[0], mine * table_ref[1]], axis=1)
            out = product(moment_ref[...], stacked(turned), ((1,), (0,)))
            ahead, behind = out[:NEAR], out[NEAR : 2 * NEAR]
            inner, outer = jnp.where(even, ahead, behind), jnp.where(even, behind, ahead)
            for ref, mine in ((inner_ref, inner), (outer_ref, outer)):
                ref[tile, :NEAR] = mine[:, :LANES]
                ref[tile, NEAR:] = mine[:, LANES:]
            at = 2 * NEAR
            for s in range(1, segments):
                to = lax.rem(me + s, segments)
                every_ref[to, tile, :FAR] = out[at : at + FAR, :LANES]
                every_ref[to, tile, FAR:] = out[at : at + FAR, LANES:]
                at += FAR

    copies[0].wait()
    cast(0)
    for step in range(steps):
        if step + 1 < steps:
            copies[step + 1].wait()
        gather(step)
        if step + 1 < steps:
            cast(step + 1)
        if step > 0:
            moments(step - 1)
    moments(steps - 1)


def turned_over(values):
    none = jnp.zeros((LANES - EXTRA, LANES), F32)
    return jnp.transpose(jnp.concatenate([values, none], axis=0))


def near_kernel_call(local_ref, table_ref, node_ref, far_ref, near_ref):
    del far_ref
    tiles = node_ref.shape[0]
    half = LANES // 2
    near_ref[tiles, :half] = turned_over(table_ref[2])[:half]
    near_ref[tiles, half:] = turned_over(table_ref[3])[:half]
    for start in range(0, node_ref.shape[0], GROUP):
        columns = []
        for tile in range(start, start + GROUP):
            columns += [node_ref[tile] * table_ref[0], node_ref[tile] * table_ref[1]]
        out = product(local_ref[...], stacked(jnp.concatenate(columns, axis=1)), ((1,), (0,)))
        for tile in range(GROUP):
            at = 2 * tile * LANES
            cosine, sine = out[:, at : at + LANES], out[:, at + LANES : at + 2 * LANES]
            near_ref[start + tile] = turned_over(table_ref[3] * cosine - table_ref[2] * sine)


def combine_kernel(
    per_field, rows, scale_ref, far_ref, near_ref, inner_ref, outer_ref,
    every_ref, pack_ref, first_ref, second_ref,
):
    segments, tiles = every_ref.shape[:2]
    wide = near_ref.shape[2]
    even_lat = lax.rem(lax.axis_index("lat"), 2) == 0
    inverse = 1.0 / scale_ref[...]
    pair = LANES // rows
    cosine = jnp.concatenate([near_ref[tiles, :rows]] * pair, axis=0)
    sine = jnp.concatenate([near_ref[tiles, LANES // 2 : LANES // 2 + rows]] * pair, axis=0)
    for start in range(0, tiles, GROUP):
        columns = []
        for tile in range(start, start + GROUP):
            pieces = [inner_ref[tile], outer_ref[tile]]
            pieces += [every_ref[e, tile] for e in range(segments)]
            columns.append(jnp.concatenate(pieces, axis=0))
        got = product(stacked(jnp.concatenate(columns, axis=1)), far_ref[...], ((0,), (0,)))
        for tile in range(start, start + GROUP):
            mine = got[(tile - start) * LANES : (tile - start + 1) * LANES]
            values = near_ref[tile] + sine * mine[:, :wide] - cosine * mine[:, wide:]
            pack_ref[tile] = packed(values)
            wind = tile < 2 * per_field
            for part in range(pair):
                line = tile * pair + part
                first, last = part * rows, part * rows + rows - 1
                top, bottom = values[first : first + 1], values[last : last + 1]
                if wind:
                    top, bottom = top * inverse[:, :1], bottom * inverse[:, rows - 1 :]
                first_ref[line : line + 1] = jnp.where(even_lat, bottom, top)
                second_ref[line : line + 1] = jnp.where(even_lat, top, bottom)


def early_kernel(early, spread_ref, pack_ref, filtered_ref):
    per_field = pack_ref.shape[0] // 3
    pack = [pack_ref[f * per_field + tile] for tile in range(early) for f in range(3)]
    values = spread_lines(jnp.concatenate(pack, axis=0), spread_ref)
    filtered_ref[...] = values.reshape(filtered_ref.shape)


def finish_kernel(
    scale_ref, spread_ref, first_ref, second_ref, pack_ref, early_ref, tracer_ref, *refs
):
    outs = refs[:3]
    filtered_ref, edge_ref, column_ref, held_ref, load_sems, sems = refs[3:]
    levels, rows, width = tracer_ref.shape
    lanes = spread_ref.shape[1]
    count = first_ref.shape[0]
    pair = LANES // rows
    steps = levels // pair
    early = early_ref.shape[0]
    tracer_slot = 6 * pair

    def load(step):
        return pltpu.make_async_copy(
            tracer_ref.at[pl.ds(step * pair, pair)],
            held_ref.at[pl.ds(tracer_slot + step % 2 * pair, pair)],
            load_sems.at[step % 2],
        )

    def store(step, number):
        return pltpu.make_async_copy(
            held_ref.at[pl.ds((3 * (step % 2) + number) * pair, pair)],
            outs[number].at[pl.ds(step * pair, pair)],
            sems.at[step % 2, number],
        )

    load(0).start()
    even_lat = lax.rem(lax.axis_index("lat"), 2) == 0
    first, second = first_ref[...], second_ref[...]
    above, below = jnp.where(even_lat, second, first), jnp.where(even_lat, first, second)
    edges = jnp.concatenate([above, below], axis=0)
    edge_ref[...] = spread_lines(packed(edges), spread_ref)
    here = lax.broadcasted_iota(jnp.int32, (rows, rows), 0)
    there = lax.broadcasted_iota(jnp.int32, (rows, rows), 1)
    column = jnp.where(here == there, jnp.broadcast_to(scale_ref[...], (rows, rows)), 0.0)
    column = jnp.sum(column, axis=1, keepdims=True)
    column_ref[0] = jnp.broadcast_to(column, (rows, LANES))
    column_ref[1] = 1.0 / column_ref[0]
    row_number = lax.broadcasted_iota(jnp.int32, (SUB, 1), 0)

    def fill(step):
        pack = jnp.concatenate([pack_ref[f * steps + step] for f in range(3)], axis=0)
        filtered_ref[step - early] = spread_lines(pack, spread_ref)

    def east_west(values):
        return pltpu.roll(values, lanes - 1, 1) - pltpu.roll(values, 1, 1)

    def stencil(step):
        scale = column_ref[0][:, :1]
        inverse = column_ref[1][:, :1]
        for part in range(pair):
            level = step * pair + part

            def field(number):
                at = number * pair * rows + part * rows
                if step < early:
                    return early_ref[step, at : at + rows]
                return filtered_ref[step - early, at : at + rows]

            def north_south(values, number):
                at = number * levels + level
                above = edge_ref[at : at + 1]
                below = edge_ref[count + at : count + at + 1]
                later, earlier = pltpu.roll(values, rows - 1, 0), pltpu.roll(values, 1, 0)
                low, high = slice(0, SUB), slice(rows - SUB, rows)
                first = later[low] - jnp.where(row_number == 0, above, earlier[low])
                last = jnp.where(row_number == SUB - 1, below, later[high]) - earlier[high]
                inside = slice(SUB, rows - SUB)
                return jnp.concatenate([first, later[inside] - earlier[inside], last], axis=0)

            u, v, q = field(0), field(1), field(2)
            div = scale * (east_west(u) + north_south(v * inverse, 1))
            vort = scale * (east_west(v) - north_south(u * inverse, 0))
            change = u * (courant * scale) * east_west(q) + (courant * v) * north_south(q, 2)
            base = 3 * (step % 2) * pair + part
            held_ref[base] = held_ref[tracer_slot + step % 2 * pair + part] - change[:, :width]
            held_ref[base + pair] = div[:, :width]
            held_ref[base + 2 * pair] = vort[:, :width]

    for step in range(steps):
        if step + 1 < steps:
            load(step + 1).start()
        load(step).wait()
        if step >= 2:
            for number in range(3):
                store(step - 2, number).wait()
        stencil(step)
        if step + early < steps:
            fill(step + early)
        for number in range(3):
            store(step, number).start()
    for step in range(max(steps - 2, 0), steps):
        for number in range(3):
            store(step, number).wait()


def whole_spec():
    return pl.BlockSpec(memory_space=pltpu.VMEM)


def on_device(segments, lats, tables, wind_u, wind_v, tracer, cutoff, row_scale):
    levels, rows, width = wind_u.shape
    gather_table, moment_table, local_table, far_table, spread_table, places = tables
    nodes = gather_table.shape[0] // 2
    lanes = spread_table.shape[1]
    wide = nodes - EXTRA + LANES
    pair = LANES // rows
    group = 2 * pair
    groups = levels // group
    per_field = levels // pair
    tiles = 3 * per_field
    count = 3 * levels
    lon = lax.axis_index("lon").astype(jnp.int32)
    cut = cutoff.reshape(1, rows)
    scale = row_scale.reshape(1, rows)

    anywhere = pl.BlockSpec(memory_space=pl.ANY)
    def limit(mib):
        return pltpu.CompilerParams(vmem_limit_bytes=mib * 1024 * 1024)

    def cost(us):
        return pl.CostEstimate(flops=0, bytes_accessed=us * 3600000, transcendentals=0)

    steps = 3 * groups
    extra = jax.ShapeDtypeStruct((tiles, 2 * NEAR, LANES), F32)
    values, inner, outer, every, table = pl.pallas_call(
        functools.partial(analyse_kernel, segments, groups),
        out_shape=(
            jax.ShapeDtypeStruct((tiles, nodes, LANES), F32),
            extra,
            extra,
            jax.ShapeDtypeStruct((segments, tiles, 2 * FAR, LANES), F32),
            jax.ShapeDtypeStruct((4, nodes, LANES), F32),
        ),
        in_specs=[whole_spec()] * 4 + [anywhere] * 3,
        out_specs=(whole_spec(),) * 5,
        scratch_shapes=[
            pltpu.VMEM((steps, group, rows, width), F32),
            pltpu.VMEM((2, group * rows, width), BF),
            pltpu.VMEM((2, group * rows, width), BF),
            pltpu.SemaphoreType.DMA((steps,)),
        ],
        compiler_params=limit(56),
        cost_estimate=cost(12),
        name="analyse",
    )(cut, places, gather_table, moment_table, wind_u, wind_v, tracer)

    def swapped(array, axis, start, closed):
        size = segments if axis == "lon" else lats
        pairs = [(i, (i + 1) % size) for i in range(start, size if closed else size - 1, 2)]
        return lax.ppermute(array, axis, pairs + [(b, a) for a, b in pairs])

    every = lax.all_to_all(every, "lon", 0, 0)
    inner, outer = swapped(inner, "lon", 0, True), swapped(outer, "lon", 1, True)
    far_mine = lax.dynamic_index_in_dim(jnp.asarray(far_table), lon, 0, False)

    near = pl.pallas_call(
        near_kernel_call,
        out_shape=jax.ShapeDtypeStruct((tiles + 1, LANES, wide), F32),
        in_specs=[whole_spec()] * 4,
        out_specs=whole_spec(),
        compiler_params=limit(24),
        cost_estimate=cost(6),
        name="near",
    )(local_table, table, values, far_mine)

    edge = jax.ShapeDtypeStruct((count, wide), F32)
    pack, first, second = pl.pallas_call(
        functools.partial(combine_kernel, per_field, rows),
        out_shape=(jax.ShapeDtypeStruct((tiles, LANES, 2 * wide - LANES), BF), edge, edge),
        in_specs=[whole_spec()] * 6,
        out_specs=(whole_spec(),) * 3,
        compiler_params=limit(24),
        cost_estimate=cost(4),
        name="combine",
    )(scale, far_mine, near, inner, outer, every)

    first, second = swapped(first, "lat", 0, False), swapped(second, "lat", 1, False)

    early = per_field // 2
    filtered = pl.pallas_call(
        functools.partial(early_kernel, early),
        out_shape=jax.ShapeDtypeStruct((early, 3 * LANES, lanes), F32),
        in_specs=[whole_spec()] * 2,
        out_specs=whole_spec(),
        compiler_params=limit(24),
        cost_estimate=cost(4),
        name="early",
    )(spread_table, pack)

    return pl.pallas_call(
        finish_kernel,
        out_shape=(jax.ShapeDtypeStruct((levels, rows, width), F32),) * 3,
        in_specs=[whole_spec()] * 6 + [anywhere],
        out_specs=(anywhere,) * 3,
        scratch_shapes=[
            pltpu.VMEM((per_field - early, 3 * LANES, lanes), F32),
            pltpu.VMEM((2 * count, lanes), F32),
            pltpu.VMEM((2, rows, LANES), F32),
            pltpu.VMEM((8 * pair, rows, width), F32),
            pltpu.SemaphoreType.DMA((2,)),
            pltpu.SemaphoreType.DMA((2, 3)),
        ],
        compiler_params=limit(32),
        cost_estimate=cost(10),
        name="finish",
    )(scale, spread_table, first, second, pack, filtered, tracer)


def solution(mesh):
    segments, lats = mesh.shape["lon"], mesh.shape["lat"]
    tables = tuple(make_tables(NLON // segments, segments))
    line = P(None, "lat", "lon")
    return jax.shard_map(
        functools.partial(on_device, segments, lats, tables),
        mesh=mesh,
        in_specs=(line, line, line, P("lat"), P("lat")),
        out_specs=(line, line, line),
        check_vma=False,
    )
```
